256 devices in a mesh: layer: 8 (over z_hi, x), seq: 32 (over z_lo, y, core).
Axes of the slice: x: 4, y: 4, z: 8 (z_hi: 2, z_lo: 4; z = z_hi * 4 + z_lo), core: 2. Of those that a mesh axis runs over, the one named last changes fastest.
Arguments:
- train_acts: bfloat16 [2, 256, 14336], P(None, 'seq', 'layer'), may hold values from -6 to 6
- query_acts: bfloat16 [2, 256, 14336], P(None, 'seq', 'layer'), may hold values from -6 to 6
- train_grads: bfloat16 [2, 256, 4096], P(None, 'layer', 'seq'), may hold values from -6 to 6
- query_grads: bfloat16 [2, 256, 4096], P(None, 'layer', 'seq'), may hold values from -6 to 6
- basis_in: bfloat16 [2, 14336, 14336], P(None, 'layer', 'seq'), may hold values from -0.046875 to 0.046875
- basis_out: bfloat16 [2, 4096, 4096], P(None, 'seq', 'layer'), may hold values from -0.09375 to 0.09375
- eigen: float32 [2, 4096, 14336], P(None, 'layer', 'seq'), may hold values from 0.05 to 5
- query_segment: int32 [256], replicated, may hold values from 0 to 15, never falling along the last dimension, each value on 1 to 128 neighbouring positions
Outputs:
- token_scores: float32 [16, 256], P(None, 'seq')
The draws below stay inside these ranges and needn't reach their ends.
Inputs may be any that keep to these rules, and one draw needn't show every extreme that they name: query_segment never falls; each query has 1 to 128 tokens, one exactly 128.
All inputs are finite; a program needn't handle non-finite values.
Results may differ from the reference program's by a relative error of at most 0.0049.
Values may be sent and summed in bfloat16 or wider, within the bound.
A program may use at most 64 MiB of HBM per device.

```python
import math
import jax
import jax.numpy as jnp
import numpy as np
from jax import lax

D = 4096
FF = 14336
TRAIN = 256
QTOK = 256
QUERIES = 16
LAYERS = 2
QMOST = 128


def shard_levels(stream_key, dims, pieces, low, high):
    loudness = 1.0
    for axis_at, shards_of in pieces:
        heights = jax.random.uniform(jax.random.fold_in(jax.random.fold_in(stream_key, 6), axis_at), (shards_of,), jnp.float32, low / len(pieces), high / len(pieces))
        loudness = loudness * jnp.repeat(jnp.exp(heights), dims[axis_at] // shards_of).reshape((-1,) + (1,) * (len(dims) - 1 - axis_at))
    return loudness


def split_up(amount, total, bound, lean):
    weights = [(1 << 20) // math.isqrt(rank ** lean) + 1 for rank in range(2, amount + 1)]
    rest, given = total - bound - (amount - 1), [1] * (amount - 1)
    while rest > 0:
        movable = [i for i in range(amount - 1) if given[i] < bound]
        pool, left = sum([weights[i] for i in movable]), rest
        for i in movable:
            addition = min(bound - given[i], max(1, left * weights[i] // pool), rest)
            given[i] = given[i] + addition
            rest = rest - addition
    return np.array([bound] + given)


def ragged(own_key, count, total, bound, skew):
    if count == 2:
        one = jax.random.randint(own_key, (), max(1, total - bound), min(bound, total - 1) + 1)
        return jnp.stack([one, total - one])
    sizes = jnp.asarray(split_up(count, total, bound, skew), jnp.int32)
    twos = (count - 1) // 2
    donor, taker = sizes[1:1 + 2 * twos:2], sizes[2:2 + 2 * twos:2]
    room = jnp.minimum(donor - 1, bound - taker)
    shifted = jax.random.randint(jax.random.fold_in(own_key, 1), (twos,), 0, 1 << 20) % (room + 1)
    sizes = sizes.at[1:1 + 2 * twos:2].set(donor - shifted).at[2:2 + 2 * twos:2].set(taker + shifted)
    return sizes[jax.random.permutation(jax.random.fold_in(own_key, 2), count)]


def bell_draw(key, shape, width, bound, split=(), kind=jnp.bfloat16):
    loudness = shard_levels(key, shape, split, -0.22, 0.18) if split else 1.0
    entries = jax.random.normal(key, shape, jnp.float32) * width * loudness
    return jnp.minimum(jnp.maximum(entries, -bound), bound).astype(kind)


def setup_inputs(seed: int = 0) -> dict:
    arg_keys = jax.random.split(jax.random.key(seed), 9)
    train_acts = bell_draw(arg_keys[0], (LAYERS, TRAIN, FF), 1.0, 6.0, ((1, 32), (2, 8)))
    query_acts = bell_draw(arg_keys[1], (LAYERS, QTOK, FF), 1.0, 6.0, ((1, 32), (2, 8)))
    train_grads = bell_draw(arg_keys[2], (LAYERS, TRAIN, D), 1.0, 6.0, ((1, 8), (2, 32)))
    query_grads = bell_draw(arg_keys[3], (LAYERS, QTOK, D), 1.0, 6.0, ((1, 8), (2, 32)))
    basis_in = bell_draw(arg_keys[4], (LAYERS, FF, FF), FF ** -0.5, 0.046875, ((1, 8), (2, 32)))
    basis_out = bell_draw(arg_keys[5], (LAYERS, D, D), D ** -0.5, 0.09375, ((1, 32), (2, 8)))
    eigen = jnp.clip(jnp.exp(math.log(5.0) - 4.6051702 * jax.random.uniform(arg_keys[6], (LAYERS, D, FF), jnp.float32) ** shard_levels(arg_keys[6], (LAYERS, D, FF), ((1, 8), (2, 32)), -0.2, 0.2)), 0.05, 5.0)
    query_segment = jnp.searchsorted(jnp.cumsum(ragged(arg_keys[7], QUERIES, QTOK, QMOST, 2)), jnp.arange(QTOK), side="right").astype(jnp.int32)
    return dict(train_acts=train_acts, query_acts=query_acts, train_grads=train_grads, query_grads=query_grads, basis_in=basis_in, basis_out=basis_out, eigen=eigen, query_segment=query_segment)


DAMPING = 0.1

def reference(train_acts, query_acts, train_grads, query_grads, basis_in, basis_out, eigen, query_segment):
    factor = 1.0 / math.sqrt(D * FF * QMOST)
    member = (query_segment[:, None] == jnp.arange(QUERIES, dtype=jnp.int32)[None, :]).astype(jnp.bfloat16)
    summed = jnp.zeros((QUERIES, TRAIN), jnp.float32)
    for level in range(LAYERS):
        train_in = jnp.dot(train_acts[level], basis_in[level], preferred_element_type=jnp.float32).astype(jnp.bfloat16)
        query_in = jnp.dot(query_acts[level], basis_in[level], preferred_element_type=jnp.float32).astype(jnp.bfloat16)
        train_out = jnp.dot(train_grads[level], basis_out[level], preferred_element_type=jnp.float32).astype(jnp.bfloat16)
        query_out = jnp.dot(query_grads[level], basis_out[level], preferred_element_type=jnp.float32).astype(jnp.bfloat16)
        eigen_level = eigen[level]

        def one_query(column):
            masked = query_out * column[:, None]
            cross = jnp.dot(masked.T, query_in, preferred_element_type=jnp.float32)
            precond = (cross * factor / (eigen_level + DAMPING)).astype(jnp.bfloat16)
            projected = jnp.dot(train_out, precond, preferred_element_type=jnp.float32)
            return lax.optimization_barrier(jnp.sum(projected * train_in.astype(jnp.float32), axis=1))
        summed = summed + lax.map(one_query, member.T)
    return summed
```

```python
import functools
import math

import jax
import jax.numpy as jnp
from jax import lax
from jax.experimental import pallas as pl
from jax.experimental.pallas import tpu as pltpu
from jax.sharding import PartitionSpec as P

D = 4096
FF = 14336
QUERIES = 16
LAYERS = 2
QMOST = 128
DAMPING = 0.1

MESH = pl.DeviceIdType.MESH
BF16 = jnp.bfloat16
F32 = jnp.float32

HI, X, Z, Y, CORE = 2, 4, 4, 4, 2
TOK = 256
ROWS_IN = FF // (HI * X)
COLS_IN = FF // (Z * Y * CORE)
ROWS_OUT = D // (Z * Y * CORE)
COLS_OUT = D // (HI * X)
COPIES = 128
PIECE = COLS_IN // X
GROUP = 16
VMEM_LIMIT = 62 * 1024 * 1024
NT = (((1,), (1,)), ((), ()))


class Links:
    def __init__(self, send_sem, recv_sem, peer):
        self.send_sem, self.recv_sem, self.peer = send_sem, recv_sem, peer
        self.sent = []
        self.pooled = 0
        self.finished = 0

    def start(self, src, dst, peer, recv=None, again=None):
        if recv is None:
            recv = self.recv_sem.at[self.pooled]
            self.pooled += 1
        copy = pltpu.make_async_remote_copy(
            src_ref=src,
            dst_ref=dst,
            send_sem=self.send_sem.at[len(self.sent)],
            recv_sem=recv,
            device_id=peer,
            device_id_type=MESH,
        )
        copy.start()
        self.sent.append(again or (lambda: src))
        return copy

    def landed(self, block, recv, peer):
        pltpu.make_async_remote_copy(
            src_ref=block,
            dst_ref=block,
            send_sem=self.send_sem.at[0],
            recv_sem=recv,
            device_id=peer,
            device_id_type=MESH,
        ).wait_recv()

    def finish(self):
        for at in range(self.finished, len(self.sent)):
            block = self.sent[at]()
            pltpu.make_async_remote_copy(
                src_ref=block,
                dst_ref=block,
                send_sem=self.send_sem.at[at],
                recv_sem=self.recv_sem.at[0],
                device_id=self.peer,
                device_id_type=MESH,
            ).wait_send()
        self.finished = len(self.sent)


def received(copies):
    for copy in copies:
        copy.wait_recv()


def kernel(
    ta_hbm, qa_hbm, tg_hbm, qg_hbm, bo_hbm, seg_hbm, bi_hbm, eig_hbm,
    out_ref,
    ta, qa, seg, bi, eig, tokens, acts, grads_s, grads, bo,
    part_out, own_out, ry, rz_s, rz, out_t,
    part_in, rx_s, rx, zs, zr, give, rin,
    scores, es1, er1, es2, er2, es3, er3,
    local_sem, send_sem, recv_sem, z_sem, y_sem, on_sem, piece_sem, x_sem, hi_sem, hand_sem, give_sem,
):
    li = lax.axis_index("layer")
    si = lax.axis_index("seq")
    hi, x = li // X, li % X
    z, y, core = si // (Y * CORE), (si // CORE) % Y, si % CORE
    other = 1 - core
    factor = 1.0 / math.sqrt(D * FF * QMOST)

    def device(hh, xx, zz, yy, cc):
        return {"layer": hh * X + xx, "seq": (zz * Y + yy) * CORE + cc}

    z_of = [lax.rem(z + d, Z) for d in range(Z)]
    y_of = [lax.rem(y + d, Y) for d in range(Y)]
    x_of = [lax.rem(x + d, X) for d in range(X)]
    ring_of = [lax.rem(hi * Z + z + d, HI * Z) for d in range(HI * Z)]
    mate = device(hi, x, z, y, other)
    z_peer = [device(hi, x, z_of[d], y, core) for d in range(Z)]
    y_peer = [device(hi, x, z, y_of[d], core) for d in range(Y)]
    x_peer = [device(hi, x_of[d], z, y, core) for d in range(X)]
    x_other = [device(hi, x_of[d], z, y, other) for d in range(X)]
    hi_peer = device(1 - hi, x, z, y, core)
    hi_other = device(1 - hi, x, z, y, other)
    ring_peer = [device(at // Z, x, at % Z, y, core) for at in ring_of]
    links = Links(send_sem, recv_sem, mate)

    barrier = pltpu.get_barrier_semaphore()
    peers = [mate, hi_other] + ring_peer[1:] + y_peer[1:] + x_peer[1:] + x_other[1:]
    for peer in peers:
        pl.semaphore_signal(barrier, inc=1, device_id=peer, device_id_type=MESH)

    bo_span = pl.ds(pl.multiple_of(core * ROWS_OUT, ROWS_OUT), ROWS_OUT)
    moves = [(ta_hbm, ta), (qa_hbm, qa), (tg_hbm, grads_s.at[0]), (qg_hbm, grads_s.at[1])]
    moves += [(bo_hbm, bo.at[:, bo_span, :]), (seg_hbm, seg)]
    moves += [(bi_hbm.at[level], bi.at[level, core]) for level in range(LAYERS)]
    moves += [(eig_hbm.at[level], eig.at[level]) for level in range(LAYERS)]
    loads = []
    for at, (src, dst) in enumerate(moves):
        loads.append(pltpu.make_async_copy(src, dst, local_sem.at[at]))
        loads[-1].start()

    for load in loads[:2]:
        load.wait()
    rows = ta.shape[0] // LAYERS
    for level in range(LAYERS):
        span = slice(level * rows, (level + 1) * rows)
        block = jnp.concatenate([ta[...].astype(F32)[span], qa[...].astype(F32)[span]], axis=0)
        acts[level, z, y] = block.astype(BF16)

    def sort_segments():
        wide = jnp.broadcast_to(seg[...].astype(F32), (8, TOK)).astype(BF16)
        old = lax.broadcasted_iota(jnp.int32, (TOK, TOK), 0)
        new = lax.broadcasted_iota(jnp.int32, (TOK, TOK), 1)
        half = TOK // CORE
        source = (new % half) // rows * (rows * CORE) + new // half * rows + new % rows
        pick = (old == source).astype(F32).astype(BF16)
        return jnp.dot(wide, pick, preferred_element_type=F32)[:1]

    pl.semaphore_wait(barrier, len(peers))

    nearest = z - 1 + 2 * (1 - (z + Z - 1) // Z)
    farthest = 3 * (1 - z // 2)
    order = [z, nearest, 6 - z - nearest - farthest, farthest]

    def along_z(level):
        block = acts.at[level, z, y]
        for at in order[1:]:
            links.start(block, block, device(hi, x, at, y, core), z_sem.at[level, z])

    def along_y(level, k):
        block = acts.at[level, order[k], y]
        links.start(block, block, y_peer[1], y_sem.at[level, 0, order[k]])
        links.start(block, block, y_peer[3], y_sem.at[level, 1, order[k]])

    def spread(level, k):
        links.landed(acts.at[level, order[k], y], z_sem.at[level, order[k]], mate)
        along_y(level, k)

    def pass_on(level, k):
        left = acts.at[level, order[k], y_of[3]]
        right = acts.at[level, order[k], y_of[1]]
        links.landed(left, y_sem.at[level, 0, order[k]], mate)
        if k % 2 == 0:
            links.start(left, left, y_peer[1], on_sem.at[level, order[k]])
        links.landed(right, y_sem.at[level, 1, order[k]], mate)
        if k % 2 == 1:
            links.start(right, right, y_peer[3], on_sem.at[level, order[k]])

    def gathered(level):
        for k in range(Z):
            links.landed(acts.at[level, order[k], y_of[2]], on_sem.at[level, order[k]], mate)

    y_rows = TOK // Y
    z_rows = y_rows // Z

    def rotate_out(level):
        own = grads[level].reshape(TOK, CORE * ROWS_OUT)
        product = jnp.dot(own, bo[level], preferred_element_type=F32)
        product = product.reshape(TOK // (CORE * rows), CORE, rows, COLS_OUT)
        product = jnp.swapaxes(product, 0, 1).reshape(TOK, COLS_OUT)
        part_out[level] = product
        own_out[level] = product.astype(BF16).reshape(Y, y_rows, COLS_OUT)
        return [
            links.start(own_out.at[level, y_of[d]], ry.at[level, d - 1], y_peer[d])
            for d in (2, 1, 3)
        ]

    def add_y(level, starts):
        received(starts)
        total = part_out[level, pl.ds(pl.multiple_of(y * y_rows, y_rows), y_rows), :]
        for d in range(Y - 1):
            total = total + ry[level, d].astype(F32)
        rz_s[level] = total.reshape(Z, z_rows, COLS_OUT)
        return [
            links.start(rz_s.at[level, z_of[d]], rz.at[level, d - 1], z_peer[d])
            for d in (2, 1, 3)
        ]

    def add_z(level, starts):
        received(starts)
        total = rz_s[level, z]
        for d in range(Z - 1):
            total = total + rz[level, d]
        out_t[core, level, y, z] = total.astype(BF16)
        block = out_t.at[core, level, y, z]
        return [links.start(block, block, z_peer[d]) for d in (2, 1, 3)]

    def gather_y(level, starts):
        received(starts)
        block = out_t.at[core, level, y]
        return [links.start(block, block, y_peer[d]) for d in (2, 1, 3)]

    def hand_over(level, starts):
        received(starts)
        block = out_t.at[core, level]
        links.start(block, block, mate, hand_sem.at[level], lambda: out_t.at[core, level])

    def handed(level):
        links.landed(out_t.at[other, level], hand_sem.at[level], mate)

    def prepare(level):
        loads[8 + level].wait()
        eig[level] = factor / (eig[level] + DAMPING)

    def rotate(level):
        @pl.loop(0, TOK // 32)
        def _(p):
            pair = acts[level, p // (Y // 2), pl.ds(p % (Y // 2) * 2, 2)].astype(F32)
            for at in range(2):
                piece = pair[:, at * rows:(at + 1) * rows].reshape(2 * rows, ROWS_IN)
                here = pl.ds(pl.multiple_of(at * (TOK // 2) + p * 2 * rows, 2 * rows), 2 * rows)
                tokens[here, :] = piece.astype(BF16)

        @pl.loop(0, CORE)
        def _(c):
            product = lax.dot_general(bi[level, c], tokens[...], NT, preferred_element_type=F32)
            part_in[level, c] = product.reshape(X, PIECE, TOK)
            rx_s[level, c] = product.astype(BF16).reshape(X, PIECE, TOK)
            for k in range(CORE):
                @pl.when(c == k)
                def _(k=k):
                    for d in (2, 1, 3):
                        links.start(
                            rx_s.at[level, k, x_of[d]], rx.at[level, k, d - 1], x_peer[d],
                            x_sem.at[level, k, d - 1], lambda: zs.at[level, k],
                        )

    def add_x(level, c):
        for d in range(X - 1):
            links.landed(rx.at[level, c, d], x_sem.at[level, c, d], mate)
        total = part_in[level, c, x]
        for d in range(X - 1):
            total = total + rx[level, c, d].astype(F32)
        part_in[level, c, x] = total
        zs[level, c] = total.astype(BF16)
        links.start(
            zs.at[level, c], zr.at[level, c], hi_peer, hi_sem.at[level, c],
            lambda: zs.at[level, c],
        )

    def add_hi(level, c):
        links.landed(zr.at[level, c], hi_sem.at[level, c], mate)
        total = part_in[level, c, x] + zr[level, c].astype(F32)
        give[level, c] = total.astype(BF16)

        @pl.when(core == c)
        def _():
            rin[level, core, x] = give[level, c]

        @pl.when(core != c)
        def _():
            pltpu.make_async_remote_copy(
                src_ref=give.at[level, c],
                dst_ref=rin.at[level, core, x],
                send_sem=give_sem.at[level],
                recv_sem=piece_sem.at[level, 0, core],
                device_id=mate,
                device_id_type=MESH,
            ).start()

        for d in (1, 2, 3):
            links.start(
                give.at[level, c], rin.at[level, core, x], device(hi, x_of[d], z, y, c),
                piece_sem.at[level, d, core], lambda: give.at[level, c],
            )

    along_y(0, 0)
    along_z(0)
    for load in loads[2:6]:
        load.wait()
    theirs = grads.at[:, hi, x, :, bo_span]
    grads_in = [
        links.start(grads_s.at[core], theirs, hi_peer),
        links.start(grads_s.at[other], theirs, hi_other),
        links.start(grads_s.at[other], theirs, mate),
    ]
    along_y(1, 0)
    bo_swap = links.start(bo.at[:, bo_span, :], bo.at[:, bo_span, :], mate)
    bi_swap = [links.start(bi_hbm.at[level], bi.at[level, core], mate) for level in range(LAYERS)]
    for c in range(CORE):
        @pl.when(core == c)
        def _(c=c):
            grads[:, hi, x, :, pl.ds(c * ROWS_OUT, ROWS_OUT)] = grads_s[c]

    segment = sort_segments()

    spread(0, 1)
    along_z(1)
    pass_on(0, 0)
    received(grads_in)
    block = grads.at[:, :, x]
    grads_x = [links.start(block, block, x_peer[d]) for d in (2, 1, 3)]
    spread(0, 2)
    pass_on(0, 1)
    prepare(0)
    received([bo_swap])
    spread(0, 3)
    received(grads_x)
    out = [rotate_out(0), None]
    pass_on(0, 2)
    pass_on(0, 3)
    pass_on(1, 0)
    spread(1, 1)
    spread(1, 2)
    spread(1, 3)
    out[1] = rotate_out(1)
    out[0] = add_y(0, out[0])
    gathered(0)
    loads[6].wait()
    received(bi_swap[:1])
    rotate(0)

    pass_on(1, 1)
    pass_on(1, 2)
    out[0] = add_z(0, out[0])
    pass_on(1, 3)
    out[1] = add_y(1, out[1])
    out[0] = gather_y(0, out[0])
    add_x(0, 0)
    add_x(0, 1)
    out[1] = add_z(1, out[1])
    prepare(1)
    gathered(1)
    loads[7].wait()
    received(bi_swap[1:])
    rotate(1)
    hand_over(0, out[0])
    out[1] = gather_y(1, out[1])
    add_hi(0, 0)
    add_hi(0, 1)
    add_x(1, 0)
    handed(0)


    scores[...] = jnp.zeros_like(scores)

    @pl.loop(0, LAYERS * X)
    def _(step):
        level, d = step // X, step % X
        at = lax.rem(x + X - d, X)

        @pl.when(step == 1)
        def _():
            add_x(1, 1)
            hand_over(1, out[1])

        @pl.when(step == 3)
        def _():
            add_hi(1, 0)

        @pl.when(step == 4)
        def _():
            add_hi(1, 1)
            handed(1)

        links.landed(rin.at[level, other, at], piece_sem.at[level, d, other], mate)

        @pl.when(d != 0)
        def _():
            links.landed(rin.at[level, core, at], piece_sem.at[level, d, core], mate)

        both = [rin[level, c, at] for c in range(CORE)]
        train_in = jnp.concatenate([b[:, :TOK // 2] for b in both], axis=1).astype(F32)
        query_in = jnp.concatenate([b[:, TOK // 2:] for b in both], axis=1)
        scale = eig[level, pl.ds(pl.multiple_of(at * PIECE, PIECE), PIECE), :]
        query_out = out_t[1, level].reshape(TOK, COLS_OUT)
        train_out = out_t[0, level].reshape(TOK, COLS_OUT)

        @pl.loop(0, QUERIES // GROUP)
        def _(g):
            masked = []
            for k in range(GROUP):
                member = (segment == (g * GROUP + k).astype(F32)).astype(F32).astype(BF16)
                masked.append(query_in * member)
            masked = jnp.concatenate(masked, axis=0)
            cross = jnp.dot(masked, query_out, preferred_element_type=F32)
            cross = cross.reshape(GROUP, PIECE, COLS_OUT) * scale[None]
            precond = cross.astype(BF16).reshape(GROUP * PIECE, COLS_OUT)
            right = lax.dot_general(precond, train_out, NT, preferred_element_type=F32)
            right = right.reshape(GROUP, PIECE, TOK) * train_in[None]
            right = jnp.sum(right.reshape(GROUP, PIECE // 8, 8, TOK), axis=1)
            here = pl.ds(g * GROUP, GROUP)
            scores[here] = scores[here] + right

    summed = jnp.sum(scores[...], axis=1)
    half = TOK // 2
    es1[0] = summed[:, :half]
    es1[1] = summed[:, half:]
    ends = []
    for d in (2, 1, 3):
        ends.append(links.start(es1.at[other], er1.at[X - 1 + d], x_other[d]))
        ends.append(links.start(es1.at[core], er1.at[d], x_peer[d]))
    ends.append(links.start(es1.at[other], er1.at[0], mate))
    links.finish()
    for level in range(LAYERS):
        pltpu.make_async_remote_copy(
            src_ref=give.at[level, 0],
            dst_ref=give.at[level, 0],
            send_sem=give_sem.at[level],
            recv_sem=recv_sem.at[0],
            device_id=mate,
            device_id_type=MESH,
        ).wait_send()
    received(ends)
    total = es1[core]
    for d in range(X * CORE - 1):
        total = total + er1[d]
    es2[...] = total
    ends = []
    for d in (4, 3, 5, 2, 6, 1, 7):
        ends.append(links.start(es2, er2.at[d - 1], ring_peer[d]))
    received(ends)
    for d in range(HI * Z - 1):
        total = total + er2[d]
    es3[...] = total
    ends = [links.start(es3, er3.at[d - 1], y_peer[d]) for d in (2, 1, 3)]
    received(ends)
    for d in range(Y - 1):
        total = total + er3[d]
    out_ref[...] = total
    links.finish()


def fused(ta, qa, tg, qg, basis_in, basis_out, eigen, segment):
    y_rows = TOK // Y
    z_rows = y_rows // Z
    half = TOK // 2
    scratch = [
        pltpu.VMEM((16, ROWS_IN), BF16),
        pltpu.VMEM((16, ROWS_IN), BF16),
        pltpu.VMEM((1, TOK), jnp.int32),
        pltpu.VMEM((LAYERS, CORE, COLS_IN, ROWS_IN), BF16),
        pltpu.VMEM((LAYERS, COLS_IN, COLS_OUT), F32),
        pltpu.VMEM((TOK, ROWS_IN), BF16),
        pltpu.VMEM((LAYERS, Z, Y, 16, ROWS_IN), BF16),
        pltpu.VMEM((2, LAYERS, 32, ROWS_OUT), BF16),
        pltpu.VMEM((LAYERS, HI, X, 32, CORE * ROWS_OUT), BF16),
        pltpu.VMEM((LAYERS, CORE * ROWS_OUT, COLS_OUT), BF16),
        pltpu.VMEM((LAYERS, TOK, COLS_OUT), F32),
        pltpu.VMEM((LAYERS, Y, y_rows, COLS_OUT), BF16),
        pltpu.VMEM((LAYERS, Y - 1, y_rows, COLS_OUT), BF16),
        pltpu.VMEM((LAYERS, Z, z_rows, COLS_OUT), F32),
        pltpu.VMEM((LAYERS, Z - 1, z_rows, COLS_OUT), F32),
        pltpu.VMEM((2, LAYERS, Y, Z, z_rows, COLS_OUT), BF16),
        pltpu.VMEM((LAYERS, 2, X, PIECE, TOK), F32),
        pltpu.VMEM((LAYERS, 2, X, PIECE, TOK), BF16),
        pltpu.VMEM((LAYERS, 2, X - 1, PIECE, TOK), BF16),
        pltpu.VMEM((LAYERS, 2, PIECE, TOK), BF16),
        pltpu.VMEM((LAYERS, 2, PIECE, TOK), BF16),
        pltpu.VMEM((LAYERS, CORE, PIECE, TOK), BF16),
        pltpu.VMEM((LAYERS, 2, X, PIECE, TOK), BF16),
        pltpu.VMEM((QUERIES, 8, TOK), F32),
        pltpu.VMEM((2, QUERIES, half), F32),
        pltpu.VMEM((HI * Z - 1, QUERIES, half), F32),
        pltpu.VMEM((QUERIES, half), F32),
        pltpu.VMEM((Y * CORE - 1, QUERIES, half), F32),
        pltpu.VMEM((QUERIES, half), F32),
        pltpu.VMEM((X - 1, QUERIES, half), F32),
        pltpu.SemaphoreType.DMA((6 + 2 * LAYERS,)),
        pltpu.SemaphoreType.DMA((COPIES,)),
        pltpu.SemaphoreType.DMA((COPIES,)),
        pltpu.SemaphoreType.DMA((LAYERS, Z)),
        pltpu.SemaphoreType.DMA((LAYERS, 2, Z)),
        pltpu.SemaphoreType.DMA((LAYERS, Z)),
        pltpu.SemaphoreType.DMA((LAYERS, X, 2)),
        pltpu.SemaphoreType.DMA((LAYERS, CORE, X - 1)),
        pltpu.SemaphoreType.DMA((LAYERS, CORE)),
        pltpu.SemaphoreType.DMA((LAYERS,)),
        pltpu.SemaphoreType.DMA((LAYERS,)),
    ]
    return pl.pallas_call(
        kernel,
        out_shape=jax.ShapeDtypeStruct((QUERIES, half), F32),
        in_specs=[pl.BlockSpec(memory_space=pl.ANY)] * 8,
        out_specs=pl.BlockSpec(memory_space=pltpu.VMEM),
        scratch_shapes=scratch,
        compiler_params=pltpu.CompilerParams(
            collective_id=0, has_side_effects=True, vmem_limit_bytes=VMEM_LIMIT
        ),
        cost_estimate=pl.CostEstimate(flops=9_400_000_000, bytes_accessed=6_000_000, transcendentals=0),
    )(ta, qa, tg, qg, basis_out, segment, basis_in, eigen)


def on_device(
    train_acts, query_acts, train_grads, query_grads, basis_in, basis_out, eigen, query_segment
):
    half = fused(
        train_acts.reshape(-1, ROWS_IN),
        query_acts.reshape(-1, ROWS_IN),
        train_grads,
        query_grads,
        jnp.swapaxes(basis_in, 1, 2),
        basis_out,
        jnp.swapaxes(eigen, 1, 2),
        query_segment.reshape(1, TOK),
    )
    own = TOK // (Z * Y * CORE)
    start = lax.axis_index("seq") // CORE * own
    return lax.dynamic_slice(half, (0, start), (QUERIES, own))


def solution(mesh):
    placed = (
        P(None, "seq", "layer"),
        P(None, "seq", "layer"),
        P(None, "layer", "seq"),
        P(None, "layer", "seq"),
        P(None, "layer", "seq"),
        P(None, "seq", "layer"),
        P(None, "layer", "seq"),
        P(),
    )
    return jax.shard_map(
        on_device, mesh=mesh, in_specs=placed, out_specs=P(None, "seq"), check_vma=False
    )
```

```python
import functools
import math

import jax
import jax.numpy as jnp
from jax import lax
from jax.experimental import pallas as pl
from jax.experimental.pallas import tpu as pltpu
from jax.sharding import PartitionSpec as P

D = 4096
FF = 14336
QUERIES = 16
LAYERS = 2
QMOST = 128
DAMPING = 0.1

MESH = pl.DeviceIdType.MESH
BF16 = jnp.bfloat16
F32 = jnp.float32

HI, X, Z, Y, CORE = 2, 4, 4, 4, 2
TOK = 256
ROWS_IN = FF // (HI * X)
COLS_IN = FF // (Z * Y * CORE)
ROWS_OUT = D // (Z * Y * CORE)
COLS_OUT = D // (HI * X)
COPIES = 128
PIECE = COLS_IN // X
GROUP = 16
VMEM_LIMIT = 62 * 1024 * 1024
NT = (((1,), (1,)), ((), ()))


class Links:
    def __init__(self, send_sem, recv_sem, peer):
        self.send_sem, self.recv_sem, self.peer = send_sem, recv_sem, peer
        self.sent = []
        self.pooled = 0
        self.finished = 0

    def start(self, src, dst, peer, recv=None, again=None):
        if recv is None:
            recv = self.recv_sem.at[self.pooled]
            self.pooled += 1
        copy = pltpu.make_async_remote_copy(
            src_ref=src,
            dst_ref=dst,
            send_sem=self.send_sem.at[len(self.sent)],
            recv_sem=recv,
            device_id=peer,
            device_id_type=MESH,
        )
        copy.start()
        self.sent.append(again or (lambda: src))
        return copy

    def landed(self, block, recv, peer):
        pltpu.make_async_remote_copy(
            src_ref=block,
            dst_ref=block,
            send_sem=self.send_sem.at[0],
            recv_sem=recv,
            device_id=peer,
            device_id_type=MESH,
        ).wait_recv()

    def finish(self):
        for at in range(self.finished, len(self.sent)):
            block = self.sent[at]()
            pltpu.make_async_remote_copy(
                src_ref=block,
                dst_ref=block,
                send_sem=self.send_sem.at[at],
                recv_sem=self.recv_sem.at[0],
                device_id=self.peer,
                device_id_type=MESH,
            ).wait_send()
        self.finished = len(self.sent)


def received(copies):
    for copy in copies:
        copy.wait_recv()


def kernel(
    ta_hbm, qa_hbm, tg_hbm, qg_hbm, bo_hbm, seg_hbm, bi_hbm, eig_hbm,
    out_ref,
    ta, qa, seg, bi, eig, tokens, acts, grads_s, grads, bo,
    part_out, own_out, ry, rz_s, rz, out_t,
    part_in, rx_s, rx, zs, zr, give, rin,
    scores, es1, er1, es2, er2, es3, er3,
    local_sem, send_sem, recv_sem, z_sem, y_sem, on_sem, piece_sem, x_sem, hi_sem, hand_sem, give_sem, out_sem,
):
    li = lax.axis_index("layer")
    si = lax.axis_index("seq")
    hi, x = li // X, li % X
    z, y, core = si // (Y * CORE), (si // CORE) % Y, si % CORE
    other = 1 - core
    factor = 1.0 / math.sqrt(D * FF * QMOST)

    def device(hh, xx, zz, yy, cc):
        return {"layer": hh * X + xx, "seq": (zz * Y + yy) * CORE + cc}

    z_of = [lax.rem(z + d, Z) for d in range(Z)]
    y_of = [lax.rem(y + d, Y) for d in range(Y)]
    x_of = [lax.rem(x + d, X) for d in range(X)]
    ring_of = [lax.rem(hi * Z + z + d, HI * Z) for d in range(HI * Z)]
    mate = device(hi, x, z, y, other)
    z_peer = [device(hi, x, z_of[d], y, core) for d in range(Z)]
    y_peer = [device(hi, x, z, y_of[d], core) for d in range(Y)]
    x_peer = [device(hi, x_of[d], z, y, core) for d in range(X)]
    x_other = [device(hi, x_of[d], z, y, other) for d in range(X)]
    hi_peer = device(1 - hi, x, z, y, core)
    hi_other = device(1 - hi, x, z, y, other)
    ring_peer = [device(at // Z, x, at % Z, y, core) for at in ring_of]
    links = Links(send_sem, recv_sem, mate)

    barrier = pltpu.get_barrier_semaphore()
    peers = [mate, hi_other] + ring_peer[1:] + y_peer[1:] + x_peer[1:] + x_other[1:]
    for peer in peers:
        pl.semaphore_signal(barrier, inc=1, device_id=peer, device_id_type=MESH)

    bo_span = pl.ds(pl.multiple_of(core * ROWS_OUT, ROWS_OUT), ROWS_OUT)
    moves = [(ta_hbm, ta), (qa_hbm, qa), (tg_hbm, grads_s.at[0]), (qg_hbm, grads_s.at[1])]
    moves += [(bo_hbm, bo.at[:, bo_span, :]), (seg_hbm, seg)]
    moves += [(bi_hbm.at[level], bi.at[level, core]) for level in range(LAYERS)]
    moves += [(eig_hbm.at[level], eig.at[level]) for level in range(LAYERS)]
    loads = []
    for at, (src, dst) in enumerate(moves):
        loads.append(pltpu.make_async_copy(src, dst, local_sem.at[at]))
        loads[-1].start()

    for load in loads[:2]:
        load.wait()
    rows = ta.shape[0] // LAYERS
    for level in range(LAYERS):
        span = slice(level * rows, (level + 1) * rows)
        block = jnp.concatenate([ta[...].astype(F32)[span], qa[...].astype(F32)[span]], axis=0)
        acts[level, z, y] = block.astype(BF16)

    def sort_segments():
        wide = jnp.broadcast_to(seg[...].astype(F32), (8, TOK)).astype(BF16)
        old = lax.broadcasted_iota(jnp.int32, (TOK, TOK), 0)
        new = lax.broadcasted_iota(jnp.int32, (TOK, TOK), 1)
        half = TOK // CORE
        source = (new % half) // rows * (rows * CORE) + new // half * rows + new % rows
        pick = (old == source).astype(F32).astype(BF16)
        return jnp.dot(wide, pick, preferred_element_type=F32)[:1]

    pl.semaphore_wait(barrier, len(peers))

    nearest = z - 1 + 2 * (1 - (z + Z - 1) // Z)
    farthest = 3 * (1 - z // 2)
    order = [z, nearest, 6 - z - nearest - farthest, farthest]

    def along_z(level, k):
        block = acts.at[level, z, y]
        links.start(block, block, device(hi, x, order[k], y, core), z_sem.at[level, z])

    def along_y(level, k):
        block = acts.at[level, order[k], y]
        links.start(block, block, y_peer[1], y_sem.at[level, 0, order[k]])
        links.start(block, block, y_peer[3], y_sem.at[level, 1, order[k]])

    def spread(level, k):
        links.landed(acts.at[level, order[k], y], z_sem.at[level, order[k]], mate)
        along_y(level, k)

    def pass_on(level, k):
        left = acts.at[level, order[k], y_of[3]]
        right = acts.at[level, order[k], y_of[1]]
        links.landed(left, y_sem.at[level, 0, order[k]], mate)
        if k % 2 == 0:
            links.start(left, left, y_peer[1], on_sem.at[level, order[k]])
        links.landed(right, y_sem.at[level, 1, order[k]], mate)
        if k % 2 == 1:
            links.start(right, right, y_peer[3], on_sem.at[level, order[k]])

    def gathered(level):
        for k in range(Z):
            links.landed(acts.at[level, order[k], y_of[2]], on_sem.at[level, order[k]], mate)

    y_rows = TOK // Y
    z_rows = y_rows // Z

    def rotate_out(level):
        own = grads[level].reshape(TOK, CORE * ROWS_OUT)
        product = jnp.dot(own, bo[level], preferred_element_type=F32)
        product = product.reshape(TOK // (CORE * rows), CORE, rows, COLS_OUT)
        product = jnp.swapaxes(product, 0, 1).reshape(TOK, COLS_OUT)
        part_out[level] = product
        own_out[level] = product.astype(BF16).reshape(Y, y_rows, COLS_OUT)
        return [
            links.start(own_out.at[level, y_of[d]], ry.at[level, d - 1], y_peer[d])
            for d in (2, 1, 3)
        ]

    def add_y(level, starts):
        received(starts)
        total = part_out[level, pl.ds(pl.multiple_of(y * y_rows, y_rows), y_rows), :]
        for d in range(Y - 1):
            total = total + ry[level, d].astype(F32)
        rz_s[level] = total.reshape(Z, z_rows, COLS_OUT)
        return [
            links.start(rz_s.at[level, z_of[d]], rz.at[level, d - 1], z_peer[d])
            for d in (2, 1, 3)
        ]

    def add_z(level, starts):
        received(starts)
        total = rz_s[level, z]
        for d in range(Z - 1):
            total = total + rz[level, d]
        out_t[core, level, y, z] = total.astype(BF16)
        block = out_t.at[core, level, y, z]
        return [links.start(block, block, z_peer[d]) for d in (2, 1, 3)]

    def gather_y(level, starts):
        received(starts)
        for d in (2, 1, 3):
            block = out_t.at[core, level, y]
            links.start(
                block, block, y_peer[d], out_sem.at[level, d], lambda: out_t.at[core, level, 0]
            )

    def hand_over(level):
        for d in (2, 1, 3):
            links.landed(out_t.at[core, level, y_of[d]], out_sem.at[level, d], mate)
        block = out_t.at[core, level]
        links.start(block, block, mate, hand_sem.at[level], lambda: out_t.at[core, level])

    def handed(level):
        links.landed(out_t.at[other, level], hand_sem.at[level], mate)

    def prepare(level):
        loads[8 + level].wait()
        eig[level] = factor / (eig[level] + DAMPING)

    def rotate(level):
        @pl.loop(0, TOK // 32)
        def _(p):
            pair = acts[level, p // (Y // 2), pl.ds(p % (Y // 2) * 2, 2)].astype(F32)
            for at in range(2):
                piece = pair[:, at * rows:(at + 1) * rows].reshape(2 * rows, ROWS_IN)
                here = pl.ds(pl.multiple_of(at * (TOK // 2) + p * 2 * rows, 2 * rows), 2 * rows)
                tokens[here, :] = piece.astype(BF16)

        @pl.loop(0, CORE)
        def _(c):
            product = lax.dot_general(bi[level, c], tokens[...], NT, preferred_element_type=F32)
            part_in[level, c] = product.reshape(X, PIECE, TOK)
            rx_s[level, c] = product.astype(BF16).reshape(X, PIECE, TOK)
            for k in range(CORE):
                @pl.when(c == k)
                def _(k=k):
                    for d in (2, 1, 3):
                        links.start(
                            rx_s.at[level, k, x_of[d]], rx.at[level, k, d - 1], x_peer[d],
                            x_sem.at[level, k, d - 1], lambda: zs.at[level, k],
                        )

    def add_x(level, c):
        for d in range(X - 1):
            links.landed(rx.at[level, c, d], x_sem.at[level, c, d], mate)
        total = part_in[level, c, x]
        for d in range(X - 1):
            total = total + rx[level, c, d].astype(F32)
        part_in[level, c, x] = total
        zs[level, c] = total.astype(BF16)
        links.start(
            zs.at[level, c], zr.at[level, c], hi_peer, hi_sem.at[level, c],
            lambda: zs.at[level, c],
        )

    def add_hi(level, c):
        links.landed(zr.at[level, c], hi_sem.at[level, c], mate)
        total = part_in[level, c, x] + zr[level, c].astype(F32)
        give[level, c] = total.astype(BF16)

        @pl.when(core == c)
        def _():
            rin[level, core, x] = give[level, c]

        @pl.when(core != c)
        def _():
            pltpu.make_async_remote_copy(
                src_ref=give.at[level, c],
                dst_ref=rin.at[level, core, x],
                send_sem=give_sem.at[level],
                recv_sem=piece_sem.at[level, 0, core],
                device_id=mate,
                device_id_type=MESH,
            ).start()

        for d in (1, 2, 3):
            links.start(
                give.at[level, c], rin.at[level, core, x], device(hi, x_of[d], z, y, c),
                piece_sem.at[level, d, core], lambda: give.at[level, c],
            )

    along_z(0, 1)
    along_y(0, 0)
    along_z(0, 2)
    for load in loads[2:6]:
        load.wait()
    theirs = grads.at[:, hi, x, :, bo_span]
    grads_in = [
        links.start(grads_s.at[core], theirs, hi_peer),
        links.start(grads_s.at[other], theirs, hi_other),
        links.start(grads_s.at[other], theirs, mate),
    ]
    along_y(1, 0)
    bo_swap = links.start(bo.at[:, bo_span, :], bo.at[:, bo_span, :], mate)
    for c in range(CORE):
        @pl.when(core == c)
        def _(c=c):
            grads[:, hi, x, :, pl.ds(c * ROWS_OUT, ROWS_OUT)] = grads_s[c]

    segment = sort_segments()

    spread(0, 1)
    along_z(0, 3)
    pass_on(0, 0)
    along_z(1, 1)
    spread(0, 2)
    along_z(1, 2)
    received(grads_in)
    block = grads.at[:, :, x]
    grads_x = [links.start(block, block, x_peer[d]) for d in (2, 1, 3)]
    pass_on(0, 1)
    bi_0 = links.start(bi_hbm.at[0], bi.at[0, core], mate)
    prepare(0)
    received([bo_swap])
    spread(0, 3)
    along_z(1, 3)
    received(grads_x)
    out = [rotate_out(0), None]
    pass_on(0, 2)
    pass_on(0, 3)
    pass_on(1, 0)
    spread(1, 1)
    spread(1, 2)
    bi_1 = links.start(bi_hbm.at[1], bi.at[1, core], mate)
    spread(1, 3)
    out[0] = add_y(0, out[0])
    gathered(0)
    loads[6].wait()
    received([bi_0])
    rotate(0)

    pass_on(1, 1)
    pass_on(1, 2)
    out[0] = add_z(0, out[0])
    pass_on(1, 3)
    out[1] = rotate_out(1)
    gather_y(0, out[0])
    add_x(0, 0)
    add_x(0, 1)
    prepare(1)
    gathered(1)
    loads[7].wait()
    received([bi_1])
    rotate(1)
    out[1] = add_y(1, out[1])
    hand_over(0)
    add_hi(0, 0)
    add_hi(0, 1)
    add_x(1, 0)
    out[1] = add_z(1, out[1])
    handed(0)


    scores[...] = jnp.zeros_like(scores)

    @pl.loop(0, LAYERS * X)
    def _(step):
        level, d = step // X, step % X
        at = lax.rem(x + X - d, X)

        @pl.when(step == 1)
        def _():
            add_x(1, 1)
            gather_y(1, out[1])

        @pl.when(step == 4)
        def _():
            add_hi(1, 0)
            hand_over(1)
            add_hi(1, 1)
            handed(1)

        links.landed(rin.at[level, other, at], piece_sem.at[level, d, other], mate)

        @pl.when(d != 0)
        def _():
            links.landed(rin.at[level, core, at], piece_sem.at[level, d, core], mate)

        both = [rin[level, c, at] for c in range(CORE)]
        train_in = jnp.concatenate([b[:, :TOK // 2] for b in both], axis=1).astype(F32)
        query_in = jnp.concatenate([b[:, TOK // 2:] for b in both], axis=1)
        scale = eig[level, pl.ds(pl.multiple_of(at * PIECE, PIECE), PIECE), :]
        query_out = out_t[1, level].reshape(TOK, COLS_OUT)
        train_out = out_t[0, level].reshape(TOK, COLS_OUT)

        @pl.loop(0, QUERIES // GROUP)
        def _(g):
            masked = []
            for k in range(GROUP):
                member = (segment == (g * GROUP + k).astype(F32)).astype(F32).astype(BF16)
                masked.append(query_in * member)
            masked = jnp.concatenate(masked, axis=0)
            cross = jnp.dot(masked, query_out, preferred_element_type=F32)
            cross = cross.reshape(GROUP, PIECE, COLS_OUT) * scale[None]
            precond = cross.astype(BF16).reshape(GROUP * PIECE, COLS_OUT)
            right = lax.dot_general(precond, train_out, NT, preferred_element_type=F32)
            right = right.reshape(GROUP, PIECE, TOK) * train_in[None]
            right = jnp.sum(right.reshape(GROUP, PIECE // 8, 8, TOK), axis=1)
            here = pl.ds(g * GROUP, GROUP)
            scores[here] = scores[here] + right

    summed = jnp.sum(scores[...], axis=1)
    half = TOK // 2
    es1[0] = summed[:, :half]
    es1[1] = summed[:, half:]
    ends = []
    for d in (2, 1, 3):
        ends.append(links.start(es1.at[other], er1.at[X - 1 + d], x_other[d]))
        ends.append(links.start(es1.at[core], er1.at[d], x_peer[d]))
    ends.append(links.start(es1.at[other], er1.at[0], mate))
    links.finish()
    for level in range(LAYERS):
        pltpu.make_async_remote_copy(
            src_ref=give.at[level, 0],
            dst_ref=give.at[level, 0],
            send_sem=give_sem.at[level],
            recv_sem=recv_sem.at[0],
            device_id=mate,
            device_id_type=MESH,
        ).wait_send()
    received(ends)
    total = es1[core]
    for d in range(X * CORE - 1):
        total = total + er1[d]
    es2[...] = total
    ends = []
    for d in (4, 3, 5, 2, 6, 1, 7):
        ends.append(links.start(es2, er2.at[d - 1], ring_peer[d]))
    received(ends)
    for d in range(HI * Z - 1):
        total = total + er2[d]
    es3[...] = total
    ends = [links.start(es3, er3.at[d - 1], y_peer[d]) for d in (2, 1, 3)]
    received(ends)
    for d in range(Y - 1):
        total = total + er3[d]
    own = half // (Z * Y)
    total = pltpu.roll(total, lax.rem(half - (z * Y + y) * own, half), axis=1)
    out_ref[...] = total.T[:own]
    links.finish()


def fused(ta, qa, tg, qg, basis_in, basis_out, eigen, segment):
    y_rows = TOK // Y
    z_rows = y_rows // Z
    half = TOK // 2
    scratch = [
        pltpu.VMEM((16, ROWS_IN), BF16),
        pltpu.VMEM((16, ROWS_IN), BF16),
        pltpu.VMEM((1, TOK), jnp.int32),
        pltpu.VMEM((LAYERS, CORE, COLS_IN, ROWS_IN), BF16),
        pltpu.VMEM((LAYERS, COLS_IN, COLS_OUT), F32),
        pltpu.VMEM((TOK, ROWS_IN), BF16),
        pltpu.VMEM((LAYERS, Z, Y, 16, ROWS_IN), BF16),
        pltpu.VMEM((2, LAYERS, 32, ROWS_OUT), BF16),
        pltpu.VMEM((LAYERS, HI, X, 32, CORE * ROWS_OUT), BF16),
        pltpu.VMEM((LAYERS, CORE * ROWS_OUT, COLS_OUT), BF16),
        pltpu.VMEM((LAYERS, TOK, COLS_OUT), F32),
        pltpu.VMEM((LAYERS, Y, y_rows, COLS_OUT), BF16),
        pltpu.VMEM((LAYERS, Y - 1, y_rows, COLS_OUT), BF16),
        pltpu.VMEM((LAYERS, Z, z_rows, COLS_OUT), F32),
        pltpu.VMEM((LAYERS, Z - 1, z_rows, COLS_OUT), F32),
        pltpu.VMEM((2, LAYERS, Y, Z, z_rows, COLS_OUT), BF16),
        pltpu.VMEM((LAYERS, 2, X, PIECE, TOK), F32),
        pltpu.VMEM((LAYERS, 2, X, PIECE, TOK), BF16),
        pltpu.VMEM((LAYERS, 2, X - 1, PIECE, TOK), BF16),
        pltpu.VMEM((LAYERS, 2, PIECE, TOK), BF16),
        pltpu.VMEM((LAYERS, 2, PIECE, TOK), BF16),
        pltpu.VMEM((LAYERS, CORE, PIECE, TOK), BF16),
        pltpu.VMEM((LAYERS, 2, X, PIECE, TOK), BF16),
        pltpu.VMEM((QUERIES, 8, TOK), F32),
        pltpu.VMEM((2, QUERIES, half), F32),
        pltpu.VMEM((HI * Z - 1, QUERIES, half), F32),
        pltpu.VMEM((QUERIES, half), F32),
        pltpu.VMEM((Y * CORE - 1, QUERIES, half), F32),
        pltpu.VMEM((QUERIES, half), F32),
        pltpu.VMEM((X - 1, QUERIES, half), F32),
        pltpu.SemaphoreType.DMA((6 + 2 * LAYERS,)),
        pltpu.SemaphoreType.DMA((COPIES,)),
        pltpu.SemaphoreType.DMA((COPIES,)),
        pltpu.SemaphoreType.DMA((LAYERS, Z)),
        pltpu.SemaphoreType.DMA((LAYERS, 2, Z)),
        pltpu.SemaphoreType.DMA((LAYERS, Z)),
        pltpu.SemaphoreType.DMA((LAYERS, X, 2)),
        pltpu.SemaphoreType.DMA((LAYERS, CORE, X - 1)),
        pltpu.SemaphoreType.DMA((LAYERS, CORE)),
        pltpu.SemaphoreType.DMA((LAYERS,)),
        pltpu.SemaphoreType.DMA((LAYERS,)),
        pltpu.SemaphoreType.DMA((LAYERS, Y)),
    ]
    return pl.pallas_call(
        kernel,
        out_shape=jax.ShapeDtypeStruct((half // (Z * Y), QUERIES), F32),
        in_specs=[pl.BlockSpec(memory_space=pl.ANY)] * 8,
        out_specs=pl.BlockSpec(memory_space=pltpu.VMEM),
        scratch_shapes=scratch,
        compiler_params=pltpu.CompilerParams(
            collective_id=0, has_side_effects=True, vmem_limit_bytes=VMEM_LIMIT
        ),
        cost_estimate=pl.CostEstimate(flops=9_400_000_000, bytes_accessed=6_000_000, transcendentals=0),
    )(ta, qa, tg, qg, basis_out, segment, basis_in, eigen)


def on_device(
    train_acts, query_acts, train_grads, query_grads, basis_in, basis_out, eigen, query_segment
):
    own = fused(
        train_acts.reshape(-1, ROWS_IN),
        query_acts.reshape(-1, ROWS_IN),
        train_grads,
        query_grads,
        jnp.swapaxes(basis_in, 1, 2),
        basis_out,
        jnp.swapaxes(eigen, 1, 2),
        query_segment.reshape(1, TOK),
    )
    return jnp.swapaxes(own, 0, 1)


def solution(mesh):
    placed = (
        P(None, "seq", "layer"),
        P(None, "seq", "layer"),
        P(None, "layer", "seq"),
        P(None, "layer", "seq"),
        P(None, "layer", "seq"),
        P(None, "seq", "layer"),
        P(None, "layer", "seq"),
        P(),
    )
    return jax.shard_map(
        on_device, mesh=mesh, in_specs=placed, out_specs=P(None, "seq"), check_vma=False
    )
```

```python
import functools
import math

import jax
import jax.numpy as jnp
from jax import lax
from jax.experimental import pallas as pl
from jax.experimental.pallas import tpu as pltpu
from jax.sharding import PartitionSpec as P

D = 4096
FF = 14336
QUERIES = 16
LAYERS = 2
QMOST = 128
DAMPING = 0.1

MESH = pl.DeviceIdType.MESH
BF16 = jnp.bfloat16
F32 = jnp.float32

HI, X, Z, Y, CORE = 2, 4, 4, 4, 2
TOK = 256
ROWS_IN = FF // (HI * X)
COLS_IN = FF // (Z * Y * CORE)
ROWS_OUT = D // (Z * Y * CORE)
COLS_OUT = D // (HI * X)
COPIES = 128
PIECE = COLS_IN // X
GROUP = 16
VMEM_LIMIT = 62 * 1024 * 1024
NT = (((1,), (1,)), ((), ()))


class Links:
    def __init__(self, send_sem, recv_sem, peer):
        self.send_sem, self.recv_sem, self.peer = send_sem, recv_sem, peer
        self.sent = []
        self.pooled = 0
        self.finished = 0

    def start(self, src, dst, peer, recv=None, again=None):
        if recv is None:
            recv = self.recv_sem.at[self.pooled]
            self.pooled += 1
        copy = pltpu.make_async_remote_copy(
            src_ref=src,
            dst_ref=dst,
            send_sem=self.send_sem.at[len(self.sent)],
            recv_sem=recv,
            device_id=peer,
            device_id_type=MESH,
        )
        copy.start()
        self.sent.append(again or (lambda: src))
        return copy

    def landed(self, block, recv, peer):
        pltpu.make_async_remote_copy(
            src_ref=block,
            dst_ref=block,
            send_sem=self.send_sem.at[0],
            recv_sem=recv,
            device_id=peer,
            device_id_type=MESH,
        ).wait_recv()

    def finish(self):
        for at in range(self.finished, len(self.sent)):
            block = self.sent[at]()
            pltpu.make_async_remote_copy(
                src_ref=block,
                dst_ref=block,
                send_sem=self.send_sem.at[at],
                recv_sem=self.recv_sem.at[0],
                device_id=self.peer,
                device_id_type=MESH,
            ).wait_send()
        self.finished = len(self.sent)


def received(copies):
    for copy in copies:
        copy.wait_recv()


def kernel(
    ta_hbm, qa_hbm, tg_hbm, qg_hbm, bo_hbm, seg_hbm, bi_hbm, eig_hbm,
    out_ref,
    ta, qa, seg, bi, eig, tokens, acts, grads_s, grads, bo,
    part_out, own_out, ry, rz_s, rz, out_t,
    part_in, rx_s, rx, zs, zm, zr, give, rin,
    scores, es1, er1, es2, er2, es3, er3,
    local_sem, send_sem, recv_sem, z_sem, y_sem, on_sem, piece_sem, x_sem, hi_sem, hand_sem, give_sem, out_sem, way_sem,
):
    li = lax.axis_index("layer")
    si = lax.axis_index("seq")
    hi, x = li // X, li % X
    z, y, core = si // (Y * CORE), (si // CORE) % Y, si % CORE
    other = 1 - core
    factor = 1.0 / math.sqrt(D * FF * QMOST)

    def device(hh, xx, zz, yy, cc):
        return {"layer": hh * X + xx, "seq": (zz * Y + yy) * CORE + cc}

    z_of = [lax.rem(z + d, Z) for d in range(Z)]
    y_of = [lax.rem(y + d, Y) for d in range(Y)]
    x_of = [lax.rem(x + d, X) for d in range(X)]
    ring_of = [lax.rem(hi * Z + z + d, HI * Z) for d in range(HI * Z)]
    mate = device(hi, x, z, y, other)
    z_peer = [device(hi, x, z_of[d], y, core) for d in range(Z)]
    y_peer = [device(hi, x, z, y_of[d], core) for d in range(Y)]
    x_peer = [device(hi, x_of[d], z, y, core) for d in range(X)]
    x_other = [device(hi, x_of[d], z, y, other) for d in range(X)]
    hi_peer = device(1 - hi, x, z, y, core)
    hi_other = device(1 - hi, x, z, y, other)
    ring_peer = [device(at // Z, x, at % Z, y, core) for at in ring_of]
    links = Links(send_sem, recv_sem, mate)

    barrier = pltpu.get_barrier_semaphore()
    peers = [mate, hi_other] + ring_peer[1:] + y_peer[1:] + x_peer[1:] + x_other[1:]
    for peer in peers:
        pl.semaphore_signal(barrier, inc=1, device_id=peer, device_id_type=MESH)

    bo_span = pl.ds(pl.multiple_of(core * ROWS_OUT, ROWS_OUT), ROWS_OUT)
    moves = [(ta_hbm, ta), (qa_hbm, qa), (tg_hbm, grads_s.at[0]), (qg_hbm, grads_s.at[1])]
    moves += [(bo_hbm, bo.at[:, bo_span, :]), (seg_hbm, seg)]
    moves += [(bi_hbm.at[level], bi.at[level, core]) for level in range(LAYERS)]
    moves += [(eig_hbm.at[level], eig.at[level]) for level in range(LAYERS)]
    loads = []
    for at, (src, dst) in enumerate(moves):
        loads.append(pltpu.make_async_copy(src, dst, local_sem.at[at]))
        loads[-1].start()

    for load in loads[:2]:
        load.wait()
    rows = ta.shape[0] // LAYERS
    for level in range(LAYERS):
        span = slice(level * rows, (level + 1) * rows)
        block = jnp.concatenate([ta[...].astype(F32)[span], qa[...].astype(F32)[span]], axis=0)
        acts[level, z, y] = block.astype(BF16)

    def sort_segments():
        wide = jnp.broadcast_to(seg[...].astype(F32), (8, TOK)).astype(BF16)
        old = lax.broadcasted_iota(jnp.int32, (TOK, TOK), 0)
        new = lax.broadcasted_iota(jnp.int32, (TOK, TOK), 1)
        half = TOK // CORE
        source = (new % half) // rows * (rows * CORE) + new // half * rows + new % rows
        pick = (old == source).astype(F32).astype(BF16)
        return jnp.dot(wide, pick, preferred_element_type=F32)[:1]

    pl.semaphore_wait(barrier, len(peers))

    nearest = z - 1 + 2 * (1 - (z + Z - 1) // Z)
    farthest = 3 * (1 - z // 2)
    order = [z, nearest, 6 - z - nearest - farthest, farthest]

    def along_z(level, k):
        block = acts.at[level, z, y]
        links.start(block, block, device(hi, x, order[k], y, core), z_sem.at[level, z])

    def along_y(level, k):
        block = acts.at[level, order[k], y]
        links.start(block, block, y_peer[1], y_sem.at[level, 0, order[k]])
        links.start(block, block, y_peer[3], y_sem.at[level, 1, order[k]])

    def spread(level, k):
        links.landed(acts.at[level, order[k], y], z_sem.at[level, order[k]], mate)
        along_y(level, k)

    def pass_on(level, k):
        left = acts.at[level, order[k], y_of[3]]
        right = acts.at[level, order[k], y_of[1]]
        links.landed(left, y_sem.at[level, 0, order[k]], mate)
        if k % 2 == 0:
            links.start(left, left, y_peer[1], on_sem.at[level, order[k]])
        links.landed(right, y_sem.at[level, 1, order[k]], mate)
        if k % 2 == 1:
            links.start(right, right, y_peer[3], on_sem.at[level, order[k]])

    def gathered(level):
        for k in range(Z):
            links.landed(acts.at[level, order[k], y_of[2]], on_sem.at[level, order[k]], mate)

    y_rows = TOK // Y
    z_rows = y_rows // Z

    def rotate_out(level):
        own = grads[level].reshape(TOK, CORE * ROWS_OUT)
        product = jnp.dot(own, bo[level], preferred_element_type=F32)
        product = product.reshape(TOK // (CORE * rows), CORE, rows, COLS_OUT)
        product = jnp.swapaxes(product, 0, 1).reshape(TOK, COLS_OUT)
        part_out[level] = product
        own_out[level] = product.astype(BF16).reshape(Y, y_rows, COLS_OUT)
        return [
            links.start(own_out.at[level, y_of[d]], ry.at[level, d - 1], y_peer[d])
            for d in (2, 1, 3)
        ]

    def add_y(level, starts):
        received(starts)
        total = part_out[level, pl.ds(pl.multiple_of(y * y_rows, y_rows), y_rows), :]
        for d in range(Y - 1):
            total = total + ry[level, d].astype(F32)
        rz_s[level] = total.reshape(Z, z_rows, COLS_OUT)
        return [
            links.start(rz_s.at[level, z_of[d]], rz.at[level, d - 1], z_peer[d])
            for d in (2, 1, 3)
        ]

    def add_z(level, starts):
        received(starts)
        total = rz_s[level, z]
        for d in range(Z - 1):
            total = total + rz[level, d]
        out_t[core, level, y, z] = total.astype(BF16)
        block = out_t.at[core, level, y, z]
        return [links.start(block, block, z_peer[d]) for d in (2, 1, 3)]

    def gather_y(level, starts):
        received(starts)
        for d in (2, 1, 3):
            block = out_t.at[core, level, y]
            links.start(
                block, block, y_peer[d], out_sem.at[level, d], lambda: out_t.at[core, level, 0]
            )

    def hand_over(level):
        for d in (2, 1, 3):
            links.landed(out_t.at[core, level, y_of[d]], out_sem.at[level, d], mate)
        block = out_t.at[core, level]
        links.start(block, block, mate, hand_sem.at[level], lambda: out_t.at[core, level])

    def handed(level):
        links.landed(out_t.at[other, level], hand_sem.at[level], mate)

    def prepare(level):
        loads[8 + level].wait()
        eig[level] = factor / (eig[level] + DAMPING)

    def rotate(level):
        @pl.loop(0, TOK // 32)
        def _(p):
            pair = acts[level, p // (Y // 2), pl.ds(p % (Y // 2) * 2, 2)].astype(F32)
            for at in range(2):
                piece = pair[:, at * rows:(at + 1) * rows].reshape(2 * rows, ROWS_IN)
                here = pl.ds(pl.multiple_of(at * (TOK // 2) + p * 2 * rows, 2 * rows), 2 * rows)
                tokens[here, :] = piece.astype(BF16)

        @pl.loop(0, CORE)
        def _(c):
            product = lax.dot_general(bi[level, c], tokens[...], NT, preferred_element_type=F32)
            part_in[level, c] = product.reshape(X, PIECE, TOK)
            rx_s[level, c] = product.astype(BF16).reshape(X, PIECE, TOK)
            for k in range(CORE):
                @pl.when(c == k)
                def _(k=k):
                    for d in (2, 1, 3):
                        links.start(
                            rx_s.at[level, k, x_of[d]], rx.at[level, k, d - 1], x_peer[d],
                            x_sem.at[level, k, d - 1], lambda: zs.at[level, k],
                        )

    def add_x(level, c):
        for d in range(X - 1):
            links.landed(rx.at[level, c, d], x_sem.at[level, c, d], mate)
        total = part_in[level, c, x]
        for d in range(X - 1):
            total = total + rx[level, c, d].astype(F32)
        part_in[level, c, x] = total
        zs[level, c] = total.astype(BF16)
        if level == 0:
            links.start(
                zs.at[level, c], zr.at[level, c], hi_peer, hi_sem.at[level, c],
                lambda: zs.at[level, c],
            )
        else:
            links.start(
                zs.at[level, c], zm.at[c], ring_peer[way[c]], way_sem.at[c],
                lambda: zs.at[level, c],
            )

    way = (2, 6)

    def relay(level, c):
        links.landed(zm.at[c], way_sem.at[c], mate)
        links.start(
            zm.at[c], zr.at[level, c], ring_peer[way[c]], hi_sem.at[level, c],
            lambda: zm.at[c],
        )

    def add_hi(level, c):
        links.landed(zr.at[level, c], hi_sem.at[level, c], mate)
        total = part_in[level, c, x] + zr[level, c].astype(F32)
        give[level, c] = total.astype(BF16)

        @pl.when(core == c)
        def _():
            rin[level, core, x] = give[level, c]

        @pl.when(core != c)
        def _():
            pltpu.make_async_remote_copy(
                src_ref=give.at[level, c],
                dst_ref=rin.at[level, core, x],
                send_sem=give_sem.at[level],
                recv_sem=piece_sem.at[level, 0, core],
                device_id=mate,
                device_id_type=MESH,
            ).start()

        for d in (1, 2, 3):
            links.start(
                give.at[level, c], rin.at[level, core, x], device(hi, x_of[d], z, y, c),
                piece_sem.at[level, d, core], lambda: give.at[level, c],
            )

    along_z(0, 1)
    along_y(0, 0)
    along_z(0, 2)
    for load in loads[2:6]:
        load.wait()
    theirs = grads.at[:, hi, x, :, bo_span]
    grads_in = [
        links.start(grads_s.at[core], theirs, hi_peer),
        links.start(grads_s.at[other], theirs, hi_other),
        links.start(grads_s.at[other], theirs, mate),
    ]
    along_y(1, 0)
    bo_swap = links.start(bo.at[:, bo_span, :], bo.at[:, bo_span, :], mate)
    for c in range(CORE):
        @pl.when(core == c)
        def _(c=c):
            grads[:, hi, x, :, pl.ds(c * ROWS_OUT, ROWS_OUT)] = grads_s[c]

    segment = sort_segments()

    spread(0, 1)
    along_z(0, 3)
    pass_on(0, 0)
    along_z(1, 1)
    spread(0, 2)
    along_z(1, 2)
    received(grads_in)
    block = grads.at[:, :, x]
    grads_x = [links.start(block, block, x_peer[d]) for d in (2, 1, 3)]
    pass_on(0, 1)
    bi_0 = links.start(bi_hbm.at[0], bi.at[0, core], mate)
    prepare(0)
    received([bo_swap])
    spread(0, 3)
    along_z(1, 3)
    received(grads_x)
    out = [rotate_out(0), None]
    pass_on(0, 2)
    pass_on(0, 3)
    pass_on(1, 0)
    spread(1, 1)
    spread(1, 2)
    bi_1 = links.start(bi_hbm.at[1], bi.at[1, core], mate)
    spread(1, 3)
    out[0] = add_y(0, out[0])
    gathered(0)
    loads[6].wait()
    received([bi_0])
    rotate(0)

    pass_on(1, 1)
    pass_on(1, 2)
    out[0] = add_z(0, out[0])
    pass_on(1, 3)
    out[1] = rotate_out(1)
    gather_y(0, out[0])
    add_x(0, 0)
    add_x(0, 1)
    prepare(1)
    gathered(1)
    loads[7].wait()
    received([bi_1])
    rotate(1)
    out[1] = add_y(1, out[1])
    hand_over(0)
    add_hi(0, 0)
    add_hi(0, 1)
    add_x(1, 0)
    out[1] = add_z(1, out[1])
    handed(0)


    scores[...] = jnp.zeros_like(scores)

    @pl.loop(0, LAYERS * X)
    def _(step):
        level, d = step // X, step % X
        at = lax.rem(x + X - d, X)

        @pl.when(step == 1)
        def _():
            add_x(1, 1)
            gather_y(1, out[1])

        @pl.when(step == 2)
        def _():
            relay(1, 0)

        @pl.when(step == 3)
        def _():
            relay(1, 1)

        @pl.when(step == 4)
        def _():
            add_hi(1, 0)
            hand_over(1)
            add_hi(1, 1)
            handed(1)

        links.landed(rin.at[level, other, at], piece_sem.at[level, d, other], mate)

        @pl.when(d != 0)
        def _():
            links.landed(rin.at[level, core, at], piece_sem.at[level, d, core], mate)

        both = [rin[level, c, at] for c in range(CORE)]
        train_in = jnp.concatenate([b[:, :TOK // 2] for b in both], axis=1).astype(F32)
        query_in = jnp.concatenate([b[:, TOK // 2:] for b in both], axis=1)
        scale = eig[level, pl.ds(pl.multiple_of(at * PIECE, PIECE), PIECE), :]
        query_out = out_t[1, level].reshape(TOK, COLS_OUT)
        train_out = out_t[0, level].reshape(TOK, COLS_OUT)

        @pl.loop(0, QUERIES // GROUP)
        def _(g):
            masked = []
            for k in range(GROUP):
                member = (segment == (g * GROUP + k).astype(F32)).astype(F32).astype(BF16)
                masked.append(query_in * member)
            masked = jnp.concatenate(masked, axis=0)
            cross = jnp.dot(masked, query_out, preferred_element_type=F32)
            cross = cross.reshape(GROUP, PIECE, COLS_OUT) * scale[None]
            precond = cross.astype(BF16).reshape(GROUP * PIECE, COLS_OUT)
            right = lax.dot_general(precond, train_out, NT, preferred_element_type=F32)
            right = right.reshape(GROUP, PIECE, TOK) * train_in[None]
            right = jnp.sum(right.reshape(GROUP, PIECE // 8, 8, TOK), axis=1)
            here = pl.ds(g * GROUP, GROUP)
            scores[here] = scores[here] + right

    summed = jnp.sum(scores[...], axis=1)
    half = TOK // 2
    es1[0] = summed[:, :half]
    es1[1] = summed[:, half:]
    ends = []
    for d in (2, 1, 3):
        ends.append(links.start(es1.at[other], er1.at[X - 1 + d], x_other[d]))
        ends.append(links.start(es1.at[core], er1.at[d], x_peer[d]))
    ends.append(links.start(es1.at[other], er1.at[0], mate))
    links.finish()
    for level in range(LAYERS):
        pltpu.make_async_remote_copy(
            src_ref=give.at[level, 0],
            dst_ref=give.at[level, 0],
            send_sem=give_sem.at[level],
            recv_sem=recv_sem.at[0],
            device_id=mate,
            device_id_type=MESH,
        ).wait_send()
    received(ends)
    total = es1[core]
    for d in range(X * CORE - 1):
        total = total + er1[d]
    es2[...] = total
    ends = []
    for d in (4, 3, 5, 2, 6, 1, 7):
        ends.append(links.start(es2, er2.at[d - 1], ring_peer[d]))
    received(ends)
    for d in range(HI * Z - 1):
        total = total + er2[d]
    es3[...] = total
    ends = [links.start(es3, er3.at[d - 1], y_peer[d]) for d in (2, 1, 3)]
    received(ends)
    for d in range(Y - 1):
        total = total + er3[d]
    own = half // (Z * Y)
    total = pltpu.roll(total, lax.rem(half - (z * Y + y) * own, half), axis=1)
    out_ref[...] = total.T[:own]
    links.finish()


def fused(ta, qa, tg, qg, basis_in, basis_out, eigen, segment):
    y_rows = TOK // Y
    z_rows = y_rows // Z
    half = TOK // 2
    scratch = [
        pltpu.VMEM((16, ROWS_IN), BF16),
        pltpu.VMEM((16, ROWS_IN), BF16),
        pltpu.VMEM((1, TOK), jnp.int32),
        pltpu.VMEM((LAYERS, CORE, COLS_IN, ROWS_IN), BF16),
        pltpu.VMEM((LAYERS, COLS_IN, COLS_OUT), F32),
        pltpu.VMEM((TOK, ROWS_IN), BF16),
        pltpu.VMEM((LAYERS, Z, Y, 16, ROWS_IN), BF16),
        pltpu.VMEM((2, LAYERS, 32, ROWS_OUT), BF16),
        pltpu.VMEM((LAYERS, HI, X, 32, CORE * ROWS_OUT), BF16),
        pltpu.VMEM((LAYERS, CORE * ROWS_OUT, COLS_OUT), BF16),
        pltpu.VMEM((LAYERS, TOK, COLS_OUT), F32),
        pltpu.VMEM((LAYERS, Y, y_rows, COLS_OUT), BF16),
        pltpu.VMEM((LAYERS, Y - 1, y_rows, COLS_OUT), BF16),
        pltpu.VMEM((LAYERS, Z, z_rows, COLS_OUT), F32),
        pltpu.VMEM((LAYERS, Z - 1, z_rows, COLS_OUT), F32),
        pltpu.VMEM((2, LAYERS, Y, Z, z_rows, COLS_OUT), BF16),
        pltpu.VMEM((LAYERS, 2, X, PIECE, TOK), F32),
        pltpu.VMEM((LAYERS, 2, X, PIECE, TOK), BF16),
        pltpu.VMEM((LAYERS, 2, X - 1, PIECE, TOK), BF16),
        pltpu.VMEM((LAYERS, 2, PIECE, TOK), BF16),
        pltpu.VMEM((CORE, PIECE, TOK), BF16),
        pltpu.VMEM((LAYERS, 2, PIECE, TOK), BF16),
        pltpu.VMEM((LAYERS, CORE, PIECE, TOK), BF16),
        pltpu.VMEM((LAYERS, 2, X, PIECE, TOK), BF16),
        pltpu.VMEM((QUERIES, 8, TOK), F32),
        pltpu.VMEM((2, QUERIES, half), F32),
        pltpu.VMEM((HI * Z - 1, QUERIES, half), F32),
        pltpu.VMEM((QUERIES, half), F32),
        pltpu.VMEM((Y * CORE - 1, QUERIES, half), F32),
        pltpu.VMEM((QUERIES, half), F32),
        pltpu.VMEM((X - 1, QUERIES, half), F32),
        pltpu.SemaphoreType.DMA((6 + 2 * LAYERS,)),
        pltpu.SemaphoreType.DMA((COPIES,)),
        pltpu.SemaphoreType.DMA((COPIES,)),
        pltpu.SemaphoreType.DMA((LAYERS, Z)),
        pltpu.SemaphoreType.DMA((LAYERS, 2, Z)),
        pltpu.SemaphoreType.DMA((LAYERS, Z)),
        pltpu.SemaphoreType.DMA((LAYERS, X, 2)),
        pltpu.SemaphoreType.DMA((LAYERS, CORE, X - 1)),
        pltpu.SemaphoreType.DMA((LAYERS, CORE)),
        pltpu.SemaphoreType.DMA((LAYERS,)),
        pltpu.SemaphoreType.DMA((LAYERS,)),
        pltpu.SemaphoreType.DMA((LAYERS, Y)),
        pltpu.SemaphoreType.DMA((CORE,)),
    ]
    return pl.pallas_call(
        kernel,
        out_shape=jax.ShapeDtypeStruct((half // (Z * Y), QUERIES), F32),
        in_specs=[pl.BlockSpec(memory_space=pl.ANY)] * 8,
        out_specs=pl.BlockSpec(memory_space=pltpu.VMEM),
        scratch_shapes=scratch,
        compiler_params=pltpu.CompilerParams(
            collective_id=0, has_side_effects=True, vmem_limit_bytes=VMEM_LIMIT
        ),
        cost_estimate=pl.CostEstimate(flops=9_400_000_000, bytes_accessed=6_000_000, transcendentals=0),
    )(ta, qa, tg, qg, basis_out, segment, basis_in, eigen)


def on_device(
    train_acts, query_acts, train_grads, query_grads, basis_in, basis_out, eigen, query_segment
):
    own = fused(
        train_acts.reshape(-1, ROWS_IN),
        query_acts.reshape(-1, ROWS_IN),
        train_grads,
        query_grads,
        jnp.swapaxes(basis_in, 1, 2),
        basis_out,
        jnp.swapaxes(eigen, 1, 2),
        query_segment.reshape(1, TOK),
    )
    return jnp.swapaxes(own, 0, 1)


def solution(mesh):
    placed = (
        P(None, "seq", "layer"),
        P(None, "seq", "layer"),
        P(None, "layer", "seq"),
        P(None, "layer", "seq"),
        P(None, "layer", "seq"),
        P(None, "seq", "layer"),
        P(None, "layer", "seq"),
        P(),
    )
    return jax.shard_map(
        on_device, mesh=mesh, in_specs=placed, out_specs=P(None, "seq"), check_vma=False
    )
```

```python
import functools
import math

import jax
import jax.numpy as jnp
from jax import lax
from jax.experimental import pallas as pl
from jax.experimental.pallas import tpu as pltpu
from jax.sharding import PartitionSpec as P

D = 4096
FF = 14336
QUERIES = 16
LAYERS = 2
QMOST = 128
DAMPING = 0.1

MESH = pl.DeviceIdType.MESH
BF16 = jnp.bfloat16
F32 = jnp.float32

HI, X, Z, Y, CORE = 2, 4, 4, 4, 2
TOK = 256
ROWS_IN = FF // (HI * X)
COLS_IN = FF // (Z * Y * CORE)
ROWS_OUT = D // (Z * Y * CORE)
COLS_OUT = D // (HI * X)
COPIES = 128
PIECE = COLS_IN // X
GROUP = 16
VMEM_LIMIT = 62 * 1024 * 1024
NT = (((1,), (1,)), ((), ()))


class Links:
    def __init__(self, send_sem, recv_sem, peer):
        self.send_sem, self.recv_sem, self.peer = send_sem, recv_sem, peer
        self.sent = []
        self.pooled = 0
        self.finished = 0

    def start(self, src, dst, peer, recv=None, again=None):
        if recv is None:
            recv = self.recv_sem.at[self.pooled]
            self.pooled += 1
        copy = pltpu.make_async_remote_copy(
            src_ref=src,
            dst_ref=dst,
            send_sem=self.send_sem.at[len(self.sent)],
            recv_sem=recv,
            device_id=peer,
            device_id_type=MESH,
        )
        copy.start()
        self.sent.append(again or (lambda: src))
        return copy

    def landed(self, block, recv, peer):
        pltpu.make_async_remote_copy(
            src_ref=block,
            dst_ref=block,
            send_sem=self.send_sem.at[0],
            recv_sem=recv,
            device_id=peer,
            device_id_type=MESH,
        ).wait_recv()

    def finish(self):
        for at in range(self.finished, len(self.sent)):
            block = self.sent[at]()
            pltpu.make_async_remote_copy(
                src_ref=block,
                dst_ref=block,
                send_sem=self.send_sem.at[at],
                recv_sem=self.recv_sem.at[0],
                device_id=self.peer,
                device_id_type=MESH,
            ).wait_send()
        self.finished = len(self.sent)


def received(copies):
    for copy in copies:
        copy.wait_recv()


def kernel(
    ta_hbm, qa_hbm, tg_hbm, qg_hbm, bo_hbm, seg_hbm, bi_hbm, eig_hbm,
    out_ref,
    ta, qa, seg, bi, eig, tokens, acts, grads_s, grads, bo,
    part_out, own_out, ry, rz_s, rz, out_t,
    part_in, rx_s, rx, zs, zr, give, rin,
    scores, es1, er1, es2, er2, es3, er3,
    local_sem, send_sem, recv_sem, z_sem, y_sem, on_sem, piece_sem, x_sem, hi_sem, hand_sem, give_sem, out_sem,
):
    li = lax.axis_index("layer")
    si = lax.axis_index("seq")
    hi, x = li // X, li % X
    z, y, core = si // (Y * CORE), (si // CORE) % Y, si % CORE
    other = 1 - core
    factor = 1.0 / math.sqrt(D * FF * QMOST)

    def device(hh, xx, zz, yy, cc):
        return {"layer": hh * X + xx, "seq": (zz * Y + yy) * CORE + cc}

    z_of = [lax.rem(z + d, Z) for d in range(Z)]
    y_of = [lax.rem(y + d, Y) for d in range(Y)]
    x_of = [lax.rem(x + d, X) for d in range(X)]
    ring_of = [lax.rem(hi * Z + z + d, HI * Z) for d in range(HI * Z)]
    mate = device(hi, x, z, y, other)
    z_peer = [device(hi, x, z_of[d], y, core) for d in range(Z)]
    y_peer = [device(hi, x, z, y_of[d], core) for d in range(Y)]
    x_peer = [device(hi, x_of[d], z, y, core) for d in range(X)]
    x_other = [device(hi, x_of[d], z, y, other) for d in range(X)]
    hi_peer = device(1 - hi, x, z, y, core)
    hi_other = device(1 - hi, x, z, y, other)
    ring_peer = [device(at // Z, x, at % Z, y, core) for at in ring_of]
    links = Links(send_sem, recv_sem, mate)

    barrier = pltpu.get_barrier_semaphore()
    peers = [mate, hi_other] + ring_peer[1:] + y_peer[1:] + x_peer[1:] + x_other[1:]
    for peer in peers:
        pl.semaphore_signal(barrier, inc=1, device_id=peer, device_id_type=MESH)

    bo_span = pl.ds(pl.multiple_of(core * ROWS_OUT, ROWS_OUT), ROWS_OUT)
    moves = [(ta_hbm, ta), (qa_hbm, qa), (tg_hbm, grads_s.at[0]), (qg_hbm, grads_s.at[1])]
    moves += [(bo_hbm, bo.at[:, bo_span, :]), (seg_hbm, seg)]
    moves += [(bi_hbm.at[level], bi.at[level, core]) for level in range(LAYERS)]
    moves += [(eig_hbm.at[level], eig.at[level]) for level in range(LAYERS)]
    loads = []
    for at, (src, dst) in enumerate(moves):
        loads.append(pltpu.make_async_copy(src, dst, local_sem.at[at]))
        loads[-1].start()

    for load in loads[:2]:
        load.wait()
    rows = ta.shape[0] // LAYERS
    for level in range(LAYERS):
        span = slice(level * rows, (level + 1) * rows)
        block = jnp.concatenate([ta[...].astype(F32)[span], qa[...].astype(F32)[span]], axis=0)
        acts[level, z, y] = block.astype(BF16)

    def sort_segments():
        wide = jnp.broadcast_to(seg[...].astype(F32), (8, TOK)).astype(BF16)
        old = lax.broadcasted_iota(jnp.int32, (TOK, TOK), 0)
        new = lax.broadcasted_iota(jnp.int32, (TOK, TOK), 1)
        half = TOK // CORE
        source = (new % half) // rows * (rows * CORE) + new // half * rows + new % rows
        pick = (old == source).astype(F32).astype(BF16)
        return jnp.dot(wide, pick, preferred_element_type=F32)[:1]

    pl.semaphore_wait(barrier, len(peers))

    nearest = z - 1 + 2 * (1 - (z + Z - 1) // Z)
    farthest = 3 * (1 - z // 2)
    order = [z, nearest, 6 - z - nearest - farthest, farthest]

    def along_z(level, k):
        block = acts.at[level, z, y]
        links.start(block, block, device(hi, x, order[k], y, core), z_sem.at[level, z])

    def along_y(level, k):
        block = acts.at[level, order[k], y]
        links.start(block, block, y_peer[1], y_sem.at[level, 0, order[k]])
        links.start(block, block, y_peer[3], y_sem.at[level, 1, order[k]])

    def spread(level, k):
        links.landed(acts.at[level, order[k], y], z_sem.at[level, order[k]], mate)
        along_y(level, k)

    def pass_on(level, k):
        left = acts.at[level, order[k], y_of[3]]
        right = acts.at[level, order[k], y_of[1]]
        links.landed(left, y_sem.at[level, 0, order[k]], mate)
        if k % 2 == 0:
            links.start(left, left, y_peer[1], on_sem.at[level, order[k]])
        links.landed(right, y_sem.at[level, 1, order[k]], mate)
        if k % 2 == 1:
            links.start(right, right, y_peer[3], on_sem.at[level, order[k]])

    def gathered(level):
        for k in range(Z):
            links.landed(acts.at[level, order[k], y_of[2]], on_sem.at[level, order[k]], mate)

    y_rows = TOK // Y
    z_rows = y_rows // Z

    def rotate_out(level):
        own = grads[level].reshape(TOK, CORE * ROWS_OUT)
        product = jnp.dot(own, bo[level], preferred_element_type=F32)
        product = product.reshape(TOK // (CORE * rows), CORE, rows, COLS_OUT)
        product = jnp.swapaxes(product, 0, 1).reshape(TOK, COLS_OUT)
        part_out[level] = product
        own_out[level] = product.astype(BF16).reshape(Y, y_rows, COLS_OUT)
        return [
            links.start(own_out.at[level, y_of[d]], ry.at[level, d - 1], y_peer[d])
            for d in (2, 1, 3)
        ]

    def add_y(level, starts):
        received(starts)
        total = part_out[level, pl.ds(pl.multiple_of(y * y_rows, y_rows), y_rows), :]
        for d in range(Y - 1):
            total = total + ry[level, d].astype(F32)
        rz_s[level] = total.reshape(Z, z_rows, COLS_OUT)
        return [
            links.start(rz_s.at[level, z_of[d]], rz.at[level, d - 1], z_peer[d])
            for d in (2, 1, 3)
        ]

    def add_z(level, starts):
        received(starts)
        total = rz_s[level, z]
        for d in range(Z - 1):
            total = total + rz[level, d]
        out_t[core, level, y, z] = total.astype(BF16)
        block = out_t.at[core, level, y, z]
        return [links.start(block, block, z_peer[d]) for d in (2, 1, 3)]

    def gather_y(level, starts):
        received(starts)
        for d in (2, 1, 3):
            block = out_t.at[core, level, y]
            links.start(
                block, block, y_peer[d], out_sem.at[level, d], lambda: out_t.at[core, level, 0]
            )

    def hand_over(level):
        for d in (2, 1, 3):
            links.landed(out_t.at[core, level, y_of[d]], out_sem.at[level, d], mate)
        block = out_t.at[core, level]
        links.start(block, block, mate, hand_sem.at[level], lambda: out_t.at[core, level])

    def handed(level):
        links.landed(out_t.at[other, level], hand_sem.at[level], mate)

    def prepare(level):
        loads[8 + level].wait()
        eig[level] = factor / (eig[level] + DAMPING)

    def rotate(level):
        @pl.loop(0, TOK // 32)
        def _(p):
            pair = acts[level, p // (Y // 2), pl.ds(p % (Y // 2) * 2, 2)].astype(F32)
            for at in range(2):
                piece = pair[:, at * rows:(at + 1) * rows].reshape(2 * rows, ROWS_IN)
                here = pl.ds(pl.multiple_of(at * (TOK // 2) + p * 2 * rows, 2 * rows), 2 * rows)
                tokens[here, :] = piece.astype(BF16)

        @pl.loop(0, CORE)
        def _(c):
            product = lax.dot_general(bi[level, c], tokens[...], NT, preferred_element_type=F32)
            part_in[level, c] = product.reshape(X, PIECE, TOK)
            rx_s[level, c] = product.astype(BF16).reshape(X, PIECE, TOK)
            for k in range(CORE):
                @pl.when(c == k)
                def _(k=k):
                    for d in (2, 1, 3):
                        links.start(
                            rx_s.at[level, k, x_of[d]], rx.at[level, k, d - 1], x_peer[d],
                            x_sem.at[level, k, d - 1], lambda: zs.at[level, k],
                        )

    def add_x(level, c):
        for d in range(X - 1):
            links.landed(rx.at[level, c, d], x_sem.at[level, c, d], mate)
        total = part_in[level, c, x]
        for d in range(X - 1):
            total = total + rx[level, c, d].astype(F32)
        part_in[level, c, x] = total
        zs[level, c] = total.astype(BF16)
        links.start(
            zs.at[level, c], zr.at[level, c], hi_peer, hi_sem.at[level, c],
            lambda: zs.at[level, c],
        )

    def add_hi(level, c):
        links.landed(zr.at[level, c], hi_sem.at[level, c], mate)
        total = part_in[level, c, x] + zr[level, c].astype(F32)
        give[level, c] = total.astype(BF16)

        @pl.when(core == c)
        def _():
            rin[level, core, x] = give[level, c]

        @pl.when(core != c)
        def _():
            pltpu.make_async_remote_copy(
                src_ref=give.at[level, c],
                dst_ref=rin.at[level, core, x],
                send_sem=give_sem.at[level],
                recv_sem=piece_sem.at[level, 0, core],
                device_id=mate,
                device_id_type=MESH,
            ).start()

        for d in (1, 2, 3):
            links.start(
                give.at[level, c], rin.at[level, core, x], device(hi, x_of[d], z, y, c),
                piece_sem.at[level, d, core], lambda: give.at[level, c],
            )

    along_z(0, 1)
    along_y(0, 0)
    along_z(0, 2)
    for load in loads[2:6]:
        load.wait()
    theirs = grads.at[:, hi, x, :, bo_span]
    grads_in = [
        links.start(grads_s.at[core], theirs, hi_peer),
        links.start(grads_s.at[other], theirs, hi_other),
        links.start(grads_s.at[other], theirs, mate),
    ]
    along_y(1, 0)
    bo_swap = links.start(bo.at[:, bo_span, :], bo.at[:, bo_span, :], mate)
    for c in range(CORE):
        @pl.when(core == c)
        def _(c=c):
            grads[:, hi, x, :, pl.ds(c * ROWS_OUT, ROWS_OUT)] = grads_s[c]

    segment = sort_segments()

    along_z(0, 3)
    spread(0, 1)
    spread(0, 2)
    along_z(1, 1)
    along_z(1, 2)
    pass_on(0, 0)
    received(grads_in)
    block = grads.at[:, :, x]
    grads_x = [links.start(block, block, x_peer[d]) for d in (2, 1, 3)]
    spread(0, 3)
    along_z(1, 3)
    bi_0 = links.start(bi_hbm.at[0], bi.at[0, core], mate)
    prepare(0)
    pass_on(0, 1)
    received([bo_swap])
    received(grads_x)
    out = [rotate_out(0), None]
    spread(1, 1)
    spread(1, 2)
    pass_on(0, 2)
    pass_on(1, 0)
    pass_on(0, 3)
    spread(1, 3)
    bi_1 = links.start(bi_hbm.at[1], bi.at[1, core], mate)
    out[0] = add_y(0, out[0])
    pass_on(1, 1)
    gathered(0)
    loads[6].wait()
    received([bi_0])
    rotate(0)

    pass_on(1, 2)
    pass_on(1, 3)
    out[0] = add_z(0, out[0])
    out[1] = rotate_out(1)
    add_x(0, 0)
    prepare(1)
    gathered(1)
    loads[7].wait()
    received([bi_1])
    rotate(1)
    add_x(0, 1)
    gather_y(0, out[0])
    out[1] = add_y(1, out[1])
    add_x(1, 0)
    hand_over(0)
    add_hi(0, 0)
    add_hi(0, 1)
    add_x(1, 1)
    out[1] = add_z(1, out[1])
    handed(0)

    scores[...] = jnp.zeros_like(scores)

    @pl.loop(0, LAYERS * X)
    def _(step):
        level, d = step // X, step % X
        at = lax.rem(x + X - d, X)

        @pl.when(step == 1)
        def _():
            gather_y(1, out[1])

        @pl.when(step == 4)
        def _():
            add_hi(1, 0)
            hand_over(1)
            add_hi(1, 1)
            handed(1)

        links.landed(rin.at[level, other, at], piece_sem.at[level, d, other], mate)

        @pl.when(d != 0)
        def _():
            links.landed(rin.at[level, core, at], piece_sem.at[level, d, core], mate)

        both = [rin[level, c, at] for c in range(CORE)]
        train_in = jnp.concatenate([b[:, :TOK // 2] for b in both], axis=1).astype(F32)
        query_in = jnp.concatenate([b[:, TOK // 2:] for b in both], axis=1)
        scale = eig[level, pl.ds(pl.multiple_of(at * PIECE, PIECE), PIECE), :]
        query_out = out_t[1, level].reshape(TOK, COLS_OUT)
        train_out = out_t[0, level].reshape(TOK, COLS_OUT)

        @pl.loop(0, QUERIES // GROUP)
        def _(g):
            masked = []
            for k in range(GROUP):
                member = (segment == (g * GROUP + k).astype(F32)).astype(F32).astype(BF16)
                masked.append(query_in * member)
            masked = jnp.concatenate(masked, axis=0)
            cross = jnp.dot(masked, query_out, preferred_element_type=F32)
            cross = cross.reshape(GROUP, PIECE, COLS_OUT) * scale[None]
            precond = cross.astype(BF16).reshape(GROUP * PIECE, COLS_OUT)
            right = lax.dot_general(precond, train_out, NT, preferred_element_type=F32)
            right = right.reshape(GROUP, PIECE, TOK) * train_in[None]
            right = jnp.sum(right.reshape(GROUP, PIECE // 8, 8, TOK), axis=1)
            here = pl.ds(g * GROUP, GROUP)
            scores[here] = scores[here] + right

    summed = jnp.sum(scores[...], axis=1)
    half = TOK // 2
    es1[0] = summed[:, :half]
    es1[1] = summed[:, half:]
    ends = []
    for d in (2, 1, 3):
        ends.append(links.start(es1.at[other], er1.at[X - 1 + d], x_other[d]))
        ends.append(links.start(es1.at[core], er1.at[d], x_peer[d]))
    ends.append(links.start(es1.at[other], er1.at[0], mate))
    links.finish()
    for level in range(LAYERS):
        pltpu.make_async_remote_copy(
            src_ref=give.at[level, 0],
            dst_ref=give.at[level, 0],
            send_sem=give_sem.at[level],
            recv_sem=recv_sem.at[0],
            device_id=mate,
            device_id_type=MESH,
        ).wait_send()
    received(ends)
    total = es1[core]
    for d in range(X * CORE - 1):
        total = total + er1[d]
    es2[...] = total
    ends = []
    for d in (4, 3, 5, 2, 6, 1, 7):
        ends.append(links.start(es2, er2.at[d - 1], ring_peer[d]))
    received(ends)
    for d in range(HI * Z - 1):
        total = total + er2[d]
    es3[...] = total
    ends = [links.start(es3, er3.at[d - 1], y_peer[d]) for d in (2, 1, 3)]
    received(ends)
    for d in range(Y - 1):
        total = total + er3[d]
    own = half // (Z * Y)
    total = pltpu.roll(total, lax.rem(half - (z * Y + y) * own, half), axis=1)
    out_ref[...] = total.T[:own]
    links.finish()


def fused(ta, qa, tg, qg, basis_in, basis_out, eigen, segment):
    y_rows = TOK // Y
    z_rows = y_rows // Z
    half = TOK // 2
    scratch = [
        pltpu.VMEM((16, ROWS_IN), BF16),
        pltpu.VMEM((16, ROWS_IN), BF16),
        pltpu.VMEM((1, TOK), jnp.int32),
        pltpu.VMEM((LAYERS, CORE, COLS_IN, ROWS_IN), BF16),
        pltpu.VMEM((LAYERS, COLS_IN, COLS_OUT), F32),
        pltpu.VMEM((TOK, ROWS_IN), BF16),
        pltpu.VMEM((LAYERS, Z, Y, 16, ROWS_IN), BF16),
        pltpu.VMEM((2, LAYERS, 32, ROWS_OUT), BF16),
        pltpu.VMEM((LAYERS, HI, X, 32, CORE * ROWS_OUT), BF16),
        pltpu.VMEM((LAYERS, CORE * ROWS_OUT, COLS_OUT), BF16),
        pltpu.VMEM((LAYERS, TOK, COLS_OUT), F32),
        pltpu.VMEM((LAYERS, Y, y_rows, COLS_OUT), BF16),
        pltpu.VMEM((LAYERS, Y - 1, y_rows, COLS_OUT), BF16),
        pltpu.VMEM((LAYERS, Z, z_rows, COLS_OUT), F32),
        pltpu.VMEM((LAYERS, Z - 1, z_rows, COLS_OUT), F32),
        pltpu.VMEM((2, LAYERS, Y, Z, z_rows, COLS_OUT), BF16),
        pltpu.VMEM((LAYERS, 2, X, PIECE, TOK), F32),
        pltpu.VMEM((LAYERS, 2, X, PIECE, TOK), BF16),
        pltpu.VMEM((LAYERS, 2, X - 1, PIECE, TOK), BF16),
        pltpu.VMEM((LAYERS, 2, PIECE, TOK), BF16),
        pltpu.VMEM((LAYERS, 2, PIECE, TOK), BF16),
        pltpu.VMEM((LAYERS, CORE, PIECE, TOK), BF16),
        pltpu.VMEM((LAYERS, 2, X, PIECE, TOK), BF16),
        pltpu.VMEM((QUERIES, 8, TOK), F32),
        pltpu.VMEM((2, QUERIES, half), F32),
        pltpu.VMEM((HI * Z - 1, QUERIES, half), F32),
        pltpu.VMEM((QUERIES, half), F32),
        pltpu.VMEM((Y * CORE - 1, QUERIES, half), F32),
        pltpu.VMEM((QUERIES, half), F32),
        pltpu.VMEM((X - 1, QUERIES, half), F32),
        pltpu.SemaphoreType.DMA((6 + 2 * LAYERS,)),
        pltpu.SemaphoreType.DMA((COPIES,)),
        pltpu.SemaphoreType.DMA((COPIES,)),
        pltpu.SemaphoreType.DMA((LAYERS, Z)),
        pltpu.SemaphoreType.DMA((LAYERS, 2, Z)),
        pltpu.SemaphoreType.DMA((LAYERS, Z)),
        pltpu.SemaphoreType.DMA((LAYERS, X, 2)),
        pltpu.SemaphoreType.DMA((LAYERS, CORE, X - 1)),
        pltpu.SemaphoreType.DMA((LAYERS, CORE)),
        pltpu.SemaphoreType.DMA((LAYERS,)),
        pltpu.SemaphoreType.DMA((LAYERS,)),
        pltpu.SemaphoreType.DMA((LAYERS, Y)),
    ]
    return pl.pallas_call(
        kernel,
        out_shape=jax.ShapeDtypeStruct((half // (Z * Y), QUERIES), F32),
        in_specs=[pl.BlockSpec(memory_space=pl.ANY)] * 8,
        out_specs=pl.BlockSpec(memory_space=pltpu.VMEM),
        scratch_shapes=scratch,
        compiler_params=pltpu.CompilerParams(
            collective_id=0, has_side_effects=True, vmem_limit_bytes=VMEM_LIMIT
        ),
        cost_estimate=pl.CostEstimate(flops=9_400_000_000, bytes_accessed=6_000_000, transcendentals=0),
    )(ta, qa, tg, qg, basis_out, segment, basis_in, eigen)


def on_device(
    train_acts, query_acts, train_grads, query_grads, basis_in, basis_out, eigen, query_segment
):
    own = fused(
        train_acts.reshape(-1, ROWS_IN),
        query_acts.reshape(-1, ROWS_IN),
        train_grads,
        query_grads,
        jnp.swapaxes(basis_in, 1, 2),
        basis_out,
        jnp.swapaxes(eigen, 1, 2),
        query_segment.reshape(1, TOK),
    )
    return jnp.swapaxes(own, 0, 1)


def solution(mesh):
    placed = (
        P(None, "seq", "layer"),
        P(None, "seq", "layer"),
        P(None, "layer", "seq"),
        P(None, "layer", "seq"),
        P(None, "layer", "seq"),
        P(None, "seq", "layer"),
        P(None, "layer", "seq"),
        P(),
    )
    return jax.shard_map(
        on_device, mesh=mesh, in_specs=placed, out_specs=P(None, "seq"), check_vma=False
    )
```

```python
import functools
import math

import jax
import jax.numpy as jnp
from jax import lax
from jax.experimental import pallas as pl
from jax.experimental.pallas import tpu as pltpu
from jax.sharding import PartitionSpec as P

D = 4096
FF = 14336
QUERIES = 16
LAYERS = 2
QMOST = 128
DAMPING = 0.1

MESH = pl.DeviceIdType.MESH
BF16 = jnp.bfloat16
F32 = jnp.float32

HI, X, Z, Y, CORE = 2, 4, 4, 4, 2
TOK = 256
ROWS_IN = FF // (HI * X)
COLS_IN = FF // (Z * Y * CORE)
ROWS_OUT = D // (Z * Y * CORE)
COLS_OUT = D // (HI * X)
COPIES = 128
PIECE = COLS_IN // X
GROUP = 16
VMEM_LIMIT = 62 * 1024 * 1024
NT = (((1,), (1,)), ((), ()))


class Links:
    def __init__(self, send_sem, recv_sem, peer):
        self.send_sem, self.recv_sem, self.peer = send_sem, recv_sem, peer
        self.sent = []
        self.pooled = 0
        self.finished = 0

    def start(self, src, dst, peer, recv=None, again=None):
        if recv is None:
            recv = self.recv_sem.at[self.pooled]
            self.pooled += 1
        copy = pltpu.make_async_remote_copy(
            src_ref=src,
            dst_ref=dst,
            send_sem=self.send_sem.at[len(self.sent)],
            recv_sem=recv,
            device_id=peer,
            device_id_type=MESH,
        )
        copy.start()
        self.sent.append(again or (lambda: src))
        return copy

    def landed(self, block, recv, peer):
        pltpu.make_async_remote_copy(
            src_ref=block,
            dst_ref=block,
            send_sem=self.send_sem.at[0],
            recv_sem=recv,
            device_id=peer,
            device_id_type=MESH,
        ).wait_recv()

    def finish(self):
        for at in range(self.finished, len(self.sent)):
            block = self.sent[at]()
            pltpu.make_async_remote_copy(
                src_ref=block,
                dst_ref=block,
                send_sem=self.send_sem.at[at],
                recv_sem=self.recv_sem.at[0],
                device_id=self.peer,
                device_id_type=MESH,
            ).wait_send()
        self.finished = len(self.sent)


def received(copies):
    for copy in copies:
        copy.wait_recv()


def kernel(
    ta_hbm, qa_hbm, tg_hbm, qg_hbm, bo_hbm, seg_hbm, bi_hbm, eig_hbm,
    out_ref,
    ta, qa, seg, bi, eig, tokens, acts, grads_s, grads, bo,
    part_out, own_out, ry, rz_s, rz, out_t,
    part_in, rx_s, rx, zs, zr, give, rin,
    scores, es1, er1, es2, er2, es3, er3,
    local_sem, send_sem, recv_sem, z_sem, y_sem, on_sem, piece_sem, x_sem, hi_sem, hand_sem, give_sem, out_sem,
):
    li = lax.axis_index("layer")
    si = lax.axis_index("seq")
    hi, x = li // X, li % X
    z, y, core = si // (Y * CORE), (si // CORE) % Y, si % CORE
    other = 1 - core
    factor = 1.0 / math.sqrt(D * FF * QMOST)

    def device(hh, xx, zz, yy, cc):
        return {"layer": hh * X + xx, "seq": (zz * Y + yy) * CORE + cc}

    z_of = [lax.rem(z + d, Z) for d in range(Z)]
    y_of = [lax.rem(y + d, Y) for d in range(Y)]
    x_of = [lax.rem(x + d, X) for d in range(X)]
    ring_of = [lax.rem(hi * Z + z + d, HI * Z) for d in range(HI * Z)]
    mate = device(hi, x, z, y, other)
    z_peer = [device(hi, x, z_of[d], y, core) for d in range(Z)]
    y_peer = [device(hi, x, z, y_of[d], core) for d in range(Y)]
    x_peer = [device(hi, x_of[d], z, y, core) for d in range(X)]
    x_other = [device(hi, x_of[d], z, y, other) for d in range(X)]
    hi_peer = device(1 - hi, x, z, y, core)
    hi_other = device(1 - hi, x, z, y, other)
    ring_peer = [device(at // Z, x, at % Z, y, core) for at in ring_of]
    links = Links(send_sem, recv_sem, mate)

    barrier = pltpu.get_barrier_semaphore()
    peers = [mate, hi_other] + ring_peer[1:] + y_peer[1:] + x_peer[1:] + x_other[1:]
    for peer in peers:
        pl.semaphore_signal(barrier, inc=1, device_id=peer, device_id_type=MESH)

    bo_span = pl.ds(pl.multiple_of(core * ROWS_OUT, ROWS_OUT), ROWS_OUT)
    moves = [(ta_hbm, ta), (qa_hbm, qa), (tg_hbm, grads_s.at[0]), (qg_hbm, grads_s.at[1])]
    moves += [(bo_hbm, bo.at[:, bo_span, :]), (seg_hbm, seg)]
    moves += [(bi_hbm.at[level], bi.at[level, core]) for level in range(LAYERS)]
    moves += [(eig_hbm.at[level], eig.at[level]) for level in range(LAYERS)]
    loads = []
    for at, (src, dst) in enumerate(moves):
        loads.append(pltpu.make_async_copy(src, dst, local_sem.at[at]))
        loads[-1].start()

    for load in loads[:2]:
        load.wait()
    rows = ta.shape[0] // LAYERS
    for level in range(LAYERS):
        span = slice(level * rows, (level + 1) * rows)
        block = jnp.concatenate([ta[...].astype(F32)[span], qa[...].astype(F32)[span]], axis=0)
        acts[level, z, y] = block.astype(BF16)

    def sort_segments():
        wide = jnp.broadcast_to(seg[...].astype(F32), (8, TOK)).astype(BF16)
        old = lax.broadcasted_iota(jnp.int32, (TOK, TOK), 0)
        new = lax.broadcasted_iota(jnp.int32, (TOK, TOK), 1)
        half = TOK // CORE
        source = (new % half) // rows * (rows * CORE) + new // half * rows + new % rows
        pick = (old == source).astype(F32).astype(BF16)
        return jnp.dot(wide, pick, preferred_element_type=F32)[:1]

    pl.semaphore_wait(barrier, len(peers))

    nearest = z - 1 + 2 * (1 - (z + Z - 1) // Z)
    farthest = 3 * (1 - z // 2)
    order = [z, nearest, 6 - z - nearest - farthest, farthest]

    def along_z(level, k):
        block = acts.at[level, z, y]
        links.start(block, block, device(hi, x, order[k], y, core), z_sem.at[level, z])

    def along_y(level, k):
        block = acts.at[level, order[k], y]
        links.start(block, block, y_peer[1], y_sem.at[level, 0, order[k]])
        links.start(block, block, y_peer[3], y_sem.at[level, 1, order[k]])

    def spread(level, k):
        links.landed(acts.at[level, order[k], y], z_sem.at[level, order[k]], mate)
        along_y(level, k)

    def pass_on(level, k):
        left = acts.at[level, order[k], y_of[3]]
        right = acts.at[level, order[k], y_of[1]]
        links.landed(left, y_sem.at[level, 0, order[k]], mate)
        if k % 2 == 0:
            links.start(left, left, y_peer[1], on_sem.at[level, order[k]])
        links.landed(right, y_sem.at[level, 1, order[k]], mate)
        if k % 2 == 1:
            links.start(right, right, y_peer[3], on_sem.at[level, order[k]])

    def gathered(level):
        for k in range(Z):
            links.landed(acts.at[level, order[k], y_of[2]], on_sem.at[level, order[k]], mate)

    y_rows = TOK // Y
    z_rows = y_rows // Z

    def rotate_out(level):
        own = grads[level].reshape(TOK, CORE * ROWS_OUT)
        product = jnp.dot(own, bo[level], preferred_element_type=F32)
        product = product.reshape(TOK // (CORE * rows), CORE, rows, COLS_OUT)
        product = jnp.swapaxes(product, 0, 1).reshape(TOK, COLS_OUT)
        part_out[level] = product
        own_out[level] = product.astype(BF16).reshape(Y, y_rows, COLS_OUT)
        return [
            links.start(own_out.at[level, y_of[d]], ry.at[level, d - 1], y_peer[d])
            for d in (2, 1, 3)
        ]

    def add_y(level, starts):
        received(starts)
        total = part_out[level, pl.ds(pl.multiple_of(y * y_rows, y_rows), y_rows), :]
        for d in range(Y - 1):
            total = total + ry[level, d].astype(F32)
        rz_s[level] = total.reshape(Z, z_rows, COLS_OUT)
        return [
            links.start(rz_s.at[level, z_of[d]], rz.at[level, d - 1], z_peer[d])
            for d in (2, 1, 3)
        ]

    def add_z(level, starts):
        received(starts)
        total = rz_s[level, z]
        for d in range(Z - 1):
            total = total + rz[level, d]
        out_t[core, level, y, z] = total.astype(BF16)
        block = out_t.at[core, level, y, z]
        return [links.start(block, block, z_peer[d]) for d in (2, 1, 3)]

    def gather_y(level, starts):
        received(starts)
        for d in (2, 1, 3):
            block = out_t.at[core, level, y]
            links.start(
                block, block, y_peer[d], out_sem.at[level, d], lambda: out_t.at[core, level, 0]
            )

    def hand_over(level):
        for d in (2, 1, 3):
            links.landed(out_t.at[core, level, y_of[d]], out_sem.at[level, d], mate)
        block = out_t.at[core, level]
        links.start(block, block, mate, hand_sem.at[level], lambda: out_t.at[core, level])

    def handed(level):
        links.landed(out_t.at[other, level], hand_sem.at[level], mate)

    def prepare(level):
        loads[8 + level].wait()
        eig[level] = factor / (eig[level] + DAMPING)

    def rotate(level):
        @pl.loop(0, TOK // 32)
        def _(p):
            pair = acts[level, p // (Y // 2), pl.ds(p % (Y // 2) * 2, 2)].astype(F32)
            for at in range(2):
                piece = pair[:, at * rows:(at + 1) * rows].reshape(2 * rows, ROWS_IN)
                here = pl.ds(pl.multiple_of(at * (TOK // 2) + p * 2 * rows, 2 * rows), 2 * rows)
                tokens[here, :] = piece.astype(BF16)

        @pl.loop(0, CORE)
        def _(c):
            product = lax.dot_general(bi[level, c], tokens[...], NT, preferred_element_type=F32)
            part_in[level, c] = product.reshape(X, PIECE, TOK)
            rx_s[level, c] = product.astype(BF16).reshape(X, PIECE, TOK)
            for k in range(CORE):
                @pl.when(c == k)
                def _(k=k):
                    for d in (2, 1, 3):
                        links.start(
                            rx_s.at[level, k, x_of[d]], rx.at[level, k, d - 1], x_peer[d],
                            x_sem.at[level, k, d - 1], lambda: zs.at[level, k],
                        )

    def add_x(level, c):
        for d in range(X - 1):
            links.landed(rx.at[level, c, d], x_sem.at[level, c, d], mate)
        total = part_in[level, c, x]
        for d in range(X - 1):
            total = total + rx[level, c, d].astype(F32)
        part_in[level, c, x] = total
        zs[level, c] = total.astype(BF16)
        links.start(
            zs.at[level, c], zr.at[level, c], hi_peer, hi_sem.at[level, c],
            lambda: zs.at[level, c],
        )

    def add_hi(level, c):
        links.landed(zr.at[level, c], hi_sem.at[level, c], mate)
        total = part_in[level, c, x] + zr[level, c].astype(F32)
        give[level, c] = total.astype(BF16)

        @pl.when(core == c)
        def _():
            rin[level, core, x] = give[level, c]

        @pl.when(core != c)
        def _():
            pltpu.make_async_remote_copy(
                src_ref=give.at[level, c],
                dst_ref=rin.at[level, core, x],
                send_sem=give_sem.at[level],
                recv_sem=piece_sem.at[level, 0, core],
                device_id=mate,
                device_id_type=MESH,
            ).start()

        for d in (1, 2, 3):
            links.start(
                give.at[level, c], rin.at[level, core, x], device(hi, x_of[d], z, y, c),
                piece_sem.at[level, d, core], lambda: give.at[level, c],
            )

    along_z(0, 1)
    along_y(0, 0)
    along_z(0, 2)
    for load in loads[2:6]:
        load.wait()
    theirs = grads.at[:, hi, x, :, bo_span]
    grads_in = [
        links.start(grads_s.at[core], theirs, hi_peer),
        links.start(grads_s.at[other], theirs, hi_other),
        links.start(grads_s.at[other], theirs, mate),
    ]
    along_y(1, 0)
    bo_swap = links.start(bo.at[:, bo_span, :], bo.at[:, bo_span, :], mate)
    for c in range(CORE):
        @pl.when(core == c)
        def _(c=c):
            grads[:, hi, x, :, pl.ds(c * ROWS_OUT, ROWS_OUT)] = grads_s[c]

    segment = sort_segments()

    along_z(0, 3)
    spread(0, 1)
    spread(0, 2)
    along_z(1, 1)
    along_z(1, 2)
    pass_on(0, 0)
    received(grads_in)
    block = grads.at[:, :, x]
    grads_x = [links.start(block, block, x_peer[d]) for d in (2, 1, 3)]
    spread(0, 3)
    along_z(1, 3)
    bi_0 = links.start(bi_hbm.at[0], bi.at[0, core], mate)
    prepare(0)
    pass_on(0, 1)
    received([bo_swap])
    received(grads_x)
    out = [rotate_out(0), None]
    spread(1, 1)
    spread(1, 2)
    pass_on(0, 2)
    pass_on(1, 0)
    out[1] = rotate_out(1)
    pass_on(0, 3)
    spread(1, 3)
    bi_1 = links.start(bi_hbm.at[1], bi.at[1, core], mate)
    out[0] = add_y(0, out[0])
    pass_on(1, 1)
    gathered(0)
    loads[6].wait()
    received([bi_0])
    rotate(0)

    pass_on(1, 2)
    out[1] = add_y(1, out[1])
    pass_on(1, 3)
    out[0] = add_z(0, out[0])
    add_x(0, 0)
    prepare(1)
    gather_y(0, out[0])
    out[1] = add_z(1, out[1])
    gathered(1)
    loads[7].wait()
    received([bi_1])
    rotate(1)
    add_x(0, 1)
    gather_y(1, out[1])
    hand_over(0)
    add_hi(0, 0)
    add_x(1, 0)
    add_hi(0, 1)
    add_x(1, 1)
    handed(0)

    scores[...] = jnp.zeros_like(scores)

    @pl.loop(0, LAYERS * X)
    def _(step):
        level, d = step // X, step % X
        at = lax.rem(x + X - d, X)

        @pl.when(step == 2)
        def _():
            hand_over(1)

        @pl.when(step == 4)
        def _():
            add_hi(1, 0)
            add_hi(1, 1)
            handed(1)

        links.landed(rin.at[level, other, at], piece_sem.at[level, d, other], mate)

        @pl.when(d != 0)
        def _():
            links.landed(rin.at[level, core, at], piece_sem.at[level, d, core], mate)

        both = [rin[level, c, at] for c in range(CORE)]
        train_in = jnp.concatenate([b[:, :TOK // 2] for b in both], axis=1).astype(F32)
        query_in = jnp.concatenate([b[:, TOK // 2:] for b in both], axis=1)
        scale = eig[level, pl.ds(pl.multiple_of(at * PIECE, PIECE), PIECE), :]
        query_out = out_t[1, level].reshape(TOK, COLS_OUT)
        train_out = out_t[0, level].reshape(TOK, COLS_OUT)

        @pl.loop(0, QUERIES // GROUP)
        def _(g):
            masked = []
            for k in range(GROUP):
                member = (segment == (g * GROUP + k).astype(F32)).astype(F32).astype(BF16)
                masked.append(query_in * member)
            masked = jnp.concatenate(masked, axis=0)
            cross = jnp.dot(masked, query_out, preferred_element_type=F32)
            cross = cross.reshape(GROUP, PIECE, COLS_OUT) * scale[None]
            precond = cross.astype(BF16).reshape(GROUP * PIECE, COLS_OUT)
            right = lax.dot_general(precond, train_out, NT, preferred_element_type=F32)
            right = right.reshape(GROUP, PIECE, TOK) * train_in[None]
            right = jnp.sum(right.reshape(GROUP, PIECE // 8, 8, TOK), axis=1)
            here = pl.ds(g * GROUP, GROUP)
            scores[here] = scores[here] + right

    summed = jnp.sum(scores[...], axis=1)
    half = TOK // 2
    es1[0] = summed[:, :half]
    es1[1] = summed[:, half:]
    ends = []
    for d in (2, 1, 3):
        ends.append(links.start(es1.at[other], er1.at[X - 1 + d], x_other[d]))
        ends.append(links.start(es1.at[core], er1.at[d], x_peer[d]))
    ends.append(links.start(es1.at[other], er1.at[0], mate))
    links.finish()
    for level in range(LAYERS):
        pltpu.make_async_remote_copy(
            src_ref=give.at[level, 0],
            dst_ref=give.at[level, 0],
            send_sem=give_sem.at[level],
            recv_sem=recv_sem.at[0],
            device_id=mate,
            device_id_type=MESH,
        ).wait_send()
    received(ends)
    total = es1[core]
    for d in range(X * CORE - 1):
        total = total + er1[d]
    es2[...] = total
    ends = []
    for d in (4, 3, 5, 2, 6, 1, 7):
        ends.append(links.start(es2, er2.at[d - 1], ring_peer[d]))
    received(ends)
    for d in range(HI * Z - 1):
        total = total + er2[d]
    es3[...] = total
    ends = [links.start(es3, er3.at[d - 1], y_peer[d]) for d in (2, 1, 3)]
    received(ends)
    for d in range(Y - 1):
        total = total + er3[d]
    own = half // (Z * Y)
    total = pltpu.roll(total, lax.rem(half - (z * Y + y) * own, half), axis=1)
    out_ref[...] = total.T[:own]
    links.finish()


def fused(ta, qa, tg, qg, basis_in, basis_out, eigen, segment):
    y_rows = TOK // Y
    z_rows = y_rows // Z
    half = TOK // 2
    scratch = [
        pltpu.VMEM((16, ROWS_IN), BF16),
        pltpu.VMEM((16, ROWS_IN), BF16),
        pltpu.VMEM((1, TOK), jnp.int32),
        pltpu.VMEM((LAYERS, CORE, COLS_IN, ROWS_IN), BF16),
        pltpu.VMEM((LAYERS, COLS_IN, COLS_OUT), F32),
        pltpu.VMEM((TOK, ROWS_IN), BF16),
        pltpu.VMEM((LAYERS, Z, Y, 16, ROWS_IN), BF16),
        pltpu.VMEM((2, LAYERS, 32, ROWS_OUT), BF16),
        pltpu.VMEM((LAYERS, HI, X, 32, CORE * ROWS_OUT), BF16),
        pltpu.VMEM((LAYERS, CORE * ROWS_OUT, COLS_OUT), BF16),
        pltpu.VMEM((LAYERS, TOK, COLS_OUT), F32),
        pltpu.VMEM((LAYERS, Y, y_rows, COLS_OUT), BF16),
        pltpu.VMEM((LAYERS, Y - 1, y_rows, COLS_OUT), BF16),
        pltpu.VMEM((LAYERS, Z, z_rows, COLS_OUT), F32),
        pltpu.VMEM((LAYERS, Z - 1, z_rows, COLS_OUT), F32),
        pltpu.VMEM((2, LAYERS, Y, Z, z_rows, COLS_OUT), BF16),
        pltpu.VMEM((LAYERS, 2, X, PIECE, TOK), F32),
        pltpu.VMEM((LAYERS, 2, X, PIECE, TOK), BF16),
        pltpu.VMEM((LAYERS, 2, X - 1, PIECE, TOK), BF16),
        pltpu.VMEM((LAYERS, 2, PIECE, TOK), BF16),
        pltpu.VMEM((LAYERS, 2, PIECE, TOK), BF16),
        pltpu.VMEM((LAYERS, CORE, PIECE, TOK), BF16),
        pltpu.VMEM((LAYERS, 2, X, PIECE, TOK), BF16),
        pltpu.VMEM((QUERIES, 8, TOK), F32),
        pltpu.VMEM((2, QUERIES, half), F32),
        pltpu.VMEM((HI * Z - 1, QUERIES, half), F32),
        pltpu.VMEM((QUERIES, half), F32),
        pltpu.VMEM((Y * CORE - 1, QUERIES, half), F32),
        pltpu.VMEM((QUERIES, half), F32),
        pltpu.VMEM((X - 1, QUERIES, half), F32),
        pltpu.SemaphoreType.DMA((6 + 2 * LAYERS,)),
        pltpu.SemaphoreType.DMA((COPIES,)),
        pltpu.SemaphoreType.DMA((COPIES,)),
        pltpu.SemaphoreType.DMA((LAYERS, Z)),
        pltpu.SemaphoreType.DMA((LAYERS, 2, Z)),
        pltpu.SemaphoreType.DMA((LAYERS, Z)),
        pltpu.SemaphoreType.DMA((LAYERS, X, 2)),
        pltpu.SemaphoreType.DMA((LAYERS, CORE, X - 1)),
        pltpu.SemaphoreType.DMA((LAYERS, CORE)),
        pltpu.SemaphoreType.DMA((LAYERS,)),
        pltpu.SemaphoreType.DMA((LAYERS,)),
        pltpu.SemaphoreType.DMA((LAYERS, Y)),
    ]
    return pl.pallas_call(
        kernel,
        out_shape=jax.ShapeDtypeStruct((half // (Z * Y), QUERIES), F32),
        in_specs=[pl.BlockSpec(memory_space=pl.ANY)] * 8,
        out_specs=pl.BlockSpec(memory_space=pltpu.VMEM),
        scratch_shapes=scratch,
        compiler_params=pltpu.CompilerParams(
            collective_id=0, has_side_effects=True, vmem_limit_bytes=VMEM_LIMIT
        ),
        cost_estimate=pl.CostEstimate(flops=9_400_000_000, bytes_accessed=6_000_000, transcendentals=0),
    )(ta, qa, tg, qg, basis_out, segment, basis_in, eigen)


def on_device(
    train_acts, query_acts, train_grads, query_grads, basis_in, basis_out, eigen, query_segment
):
    own = fused(
        train_acts.reshape(-1, ROWS_IN),
        query_acts.reshape(-1, ROWS_IN),
        train_grads,
        query_grads,
        jnp.swapaxes(basis_in, 1, 2),
        basis_out,
        jnp.swapaxes(eigen, 1, 2),
        query_segment.reshape(1, TOK),
    )
    return jnp.swapaxes(own, 0, 1)


def solution(mesh):
    placed = (
        P(None, "seq", "layer"),
        P(None, "seq", "layer"),
        P(None, "layer", "seq"),
        P(None, "layer", "seq"),
        P(None, "layer", "seq"),
        P(None, "seq", "layer"),
        P(None, "layer", "seq"),
        P(),
    )
    return jax.shard_map(
        on_device, mesh=mesh, in_specs=placed, out_specs=P(None, "seq"), check_vma=False
    )
```

```python
import functools
import math

import jax
import jax.numpy as jnp
from jax import lax
from jax.experimental import pallas as pl
from jax.experimental.pallas import tpu as pltpu
from jax.sharding import PartitionSpec as P

D = 4096
FF = 14336
QUERIES = 16
LAYERS = 2
QMOST = 128
DAMPING = 0.1

MESH = pl.DeviceIdType.MESH
BF16 = jnp.bfloat16
F32 = jnp.float32

HI, X, Z, Y, CORE = 2, 4, 4, 4, 2
TOK = 256
ROWS_IN = FF // (HI * X)
COLS_IN = FF // (Z * Y * CORE)
ROWS_OUT = D // (Z * Y * CORE)
COLS_OUT = D // (HI * X)
COPIES = 144
PIECE = COLS_IN // X
GROUP = 16
VMEM_LIMIT = 62 * 1024 * 1024
NT = (((1,), (1,)), ((), ()))


class Links:
    def __init__(self, send_sem, recv_sem, peer):
        self.send_sem, self.recv_sem, self.peer = send_sem, recv_sem, peer
        self.sent = []
        self.pooled = 0
        self.finished = 0

    def start(self, src, dst, peer, recv=None, again=None):
        if recv is None:
            recv = self.recv_sem.at[self.pooled]
            self.pooled += 1
        copy = pltpu.make_async_remote_copy(
            src_ref=src,
            dst_ref=dst,
            send_sem=self.send_sem.at[len(self.sent)],
            recv_sem=recv,
            device_id=peer,
            device_id_type=MESH,
        )
        copy.start()
        self.sent.append(again or (lambda: src))
        return copy

    def landed(self, block, recv, peer):
        pltpu.make_async_remote_copy(
            src_ref=block,
            dst_ref=block,
            send_sem=self.send_sem.at[0],
            recv_sem=recv,
            device_id=peer,
            device_id_type=MESH,
        ).wait_recv()

    def finish(self):
        for at in range(self.finished, len(self.sent)):
            block = self.sent[at]()
            pltpu.make_async_remote_copy(
                src_ref=block,
                dst_ref=block,
                send_sem=self.send_sem.at[at],
                recv_sem=self.recv_sem.at[0],
                device_id=self.peer,
                device_id_type=MESH,
            ).wait_send()
        self.finished = len(self.sent)


def received(copies):
    for copy in copies:
        copy.wait_recv()


def kernel(
    ta_hbm, qa_hbm, tg_hbm, qg_hbm, bo_hbm, seg_hbm, bi_hbm, eig_hbm,
    out_ref,
    ta, qa, seg, bi, eig, tokens, acts, grads_s, grads, bo,
    part_out, own_out, ry, rz_s, rz, out_t,
    part_in, rx_s, rx, zs, zr, give, rin,
    scores, es1, er1, es2, er2,
    local_sem, send_sem, recv_sem, z_sem, y_sem, on_sem, piece_sem, x_sem, hi_sem, hand_sem, give_sem, out_sem,
):
    li = lax.axis_index("layer")
    si = lax.axis_index("seq")
    hi, x = li // X, li % X
    z, y, core = si // (Y * CORE), (si // CORE) % Y, si % CORE
    other = 1 - core
    factor = 1.0 / math.sqrt(D * FF * QMOST)

    def device(hh, xx, zz, yy, cc):
        return {"layer": hh * X + xx, "seq": (zz * Y + yy) * CORE + cc}

    z_of = [lax.rem(z + d, Z) for d in range(Z)]
    y_of = [lax.rem(y + d, Y) for d in range(Y)]
    x_of = [lax.rem(x + d, X) for d in range(X)]
    ring_of = [lax.rem(hi * Z + z + d, HI * Z) for d in range(HI * Z)]
    mate = device(hi, x, z, y, other)
    z_peer = [device(hi, x, z_of[d], y, core) for d in range(Z)]
    y_peer = [device(hi, x, z, y_of[d], core) for d in range(Y)]
    x_peer = [device(hi, x_of[d], z, y, core) for d in range(X)]
    x_other = [device(hi, x_of[d], z, y, other) for d in range(X)]
    hi_peer = device(1 - hi, x, z, y, core)
    hi_other = device(1 - hi, x, z, y, other)
    ring_peer = [device(at // Z, x, at % Z, y, core) for at in ring_of]
    ring_other = [device(at // Z, x, at % Z, y, other) for at in ring_of]
    flat = [(dx, dy) for dx in (2, 1, 3, 0) for dy in (2, 1, 3, 0) if dx or dy]
    flat_peer = [device(hi, x_of[dx], z, y_of[dy], core) for dx, dy in flat]
    links = Links(send_sem, recv_sem, mate)

    barrier = pltpu.get_barrier_semaphore()
    peers = ring_other + ring_peer[1:] + flat_peer + x_other[1:]
    for peer in peers:
        pl.semaphore_signal(barrier, inc=1, device_id=peer, device_id_type=MESH)

    bo_span = pl.ds(pl.multiple_of(core * ROWS_OUT, ROWS_OUT), ROWS_OUT)
    moves = [(ta_hbm, ta), (qa_hbm, qa), (tg_hbm, grads_s.at[0]), (qg_hbm, grads_s.at[1])]
    moves += [(bo_hbm, bo.at[:, bo_span, :]), (seg_hbm, seg)]
    moves += [(bi_hbm.at[level], bi.at[level, core]) for level in range(LAYERS)]
    moves += [(eig_hbm.at[level], eig.at[level]) for level in range(LAYERS)]
    loads = []
    for at, (src, dst) in enumerate(moves):
        loads.append(pltpu.make_async_copy(src, dst, local_sem.at[at]))
        loads[-1].start()

    for load in loads[:2]:
        load.wait()
    rows = ta.shape[0] // LAYERS
    for level in range(LAYERS):
        span = slice(level * rows, (level + 1) * rows)
        block = jnp.concatenate([ta[...].astype(F32)[span], qa[...].astype(F32)[span]], axis=0)
        acts[level, z, y] = block.astype(BF16)

    def sort_segments():
        wide = jnp.broadcast_to(seg[...].astype(F32), (8, TOK)).astype(BF16)
        old = lax.broadcasted_iota(jnp.int32, (TOK, TOK), 0)
        new = lax.broadcasted_iota(jnp.int32, (TOK, TOK), 1)
        half = TOK // CORE
        source = (new % half) // rows * (rows * CORE) + new // half * rows + new % rows
        pick = (old == source).astype(F32).astype(BF16)
        return jnp.dot(wide, pick, preferred_element_type=F32)[:1]

    pl.semaphore_wait(barrier, len(peers))

    nearest = z - 1 + 2 * (1 - (z + Z - 1) // Z)
    farthest = 3 * (1 - z // 2)
    order = [z, nearest, 6 - z - nearest - farthest, farthest]

    def along_z(level, k):
        block = acts.at[level, z, y]
        links.start(block, block, device(hi, x, order[k], y, core), z_sem.at[level, z])

    def along_y(level, k):
        block = acts.at[level, order[k], y]
        links.start(block, block, y_peer[1], y_sem.at[level, 0, order[k]])
        links.start(block, block, y_peer[3], y_sem.at[level, 1, order[k]])
        if level == 1 and k >= 2:
            links.start(block, block, y_peer[2], on_sem.at[level, order[k]])

    def spread(level, k):
        links.landed(acts.at[level, order[k], y], z_sem.at[level, order[k]], mate)
        along_y(level, k)

    def pass_on(level, k):
        left = acts.at[level, order[k], y_of[3]]
        right = acts.at[level, order[k], y_of[1]]
        links.landed(left, y_sem.at[level, 0, order[k]], mate)
        late = level == 1 and k >= 2
        if k % 2 == 0 and not late:
            links.start(left, left, y_peer[1], on_sem.at[level, order[k]])
        links.landed(right, y_sem.at[level, 1, order[k]], mate)
        if k % 2 == 1 and not late:
            links.start(right, right, y_peer[3], on_sem.at[level, order[k]])

    def gathered(level):
        for k in range(Z):
            links.landed(acts.at[level, order[k], y_of[2]], on_sem.at[level, order[k]], mate)

    y_rows = TOK // Y
    z_rows = y_rows // Z

    def rotate_out(level):
        own = grads[level].reshape(TOK, CORE * ROWS_OUT)
        product = jnp.dot(own, bo[level], preferred_element_type=F32)
        product = product.reshape(TOK // (CORE * rows), CORE, rows, COLS_OUT)
        product = jnp.swapaxes(product, 0, 1).reshape(TOK, COLS_OUT)
        part_out[level] = product
        own_out[level] = product.astype(BF16).reshape(Y, y_rows, COLS_OUT)
        return [
            links.start(own_out.at[level, y_of[d]], ry.at[level, d - 1], y_peer[d])
            for d in (2, 1, 3)
        ]

    def add_y(level, starts):
        received(starts)
        total = part_out[level, pl.ds(pl.multiple_of(y * y_rows, y_rows), y_rows), :]
        for d in range(Y - 1):
            total = total + ry[level, d].astype(F32)
        rz_s[level] = total.reshape(Z, z_rows, COLS_OUT)
        return [
            links.start(rz_s.at[level, z_of[d]], rz.at[level, d - 1], z_peer[d])
            for d in (2, 1, 3)
        ]

    def add_z(level, starts):
        received(starts)
        total = rz_s[level, z]
        for d in range(Z - 1):
            total = total + rz[level, d]
        out_t[core, level, y, z] = total.astype(BF16)
        block = out_t.at[core, level, y, z]
        return [links.start(block, block, z_peer[d]) for d in (2, 1, 3)]

    def gather_y(level, starts):
        received(starts)
        for d in (2, 1, 3):
            block = out_t.at[core, level, y]
            links.start(
                block, block, y_peer[d], out_sem.at[level, d], lambda: out_t.at[core, level, 0]
            )

    def hand_over(level):
        for d in (2, 1, 3):
            links.landed(out_t.at[core, level, y_of[d]], out_sem.at[level, d], mate)
        block = out_t.at[core, level]
        links.start(block, block, mate, hand_sem.at[level], lambda: out_t.at[core, level])

    def handed(level):
        links.landed(out_t.at[other, level], hand_sem.at[level], mate)

    def prepare(level):
        loads[8 + level].wait()
        eig[level] = factor / (eig[level] + DAMPING)

    def rotate(level):
        @pl.loop(0, TOK // 32)
        def _(p):
            pair = acts[level, p // (Y // 2), pl.ds(p % (Y // 2) * 2, 2)].astype(F32)
            for at in range(2):
                piece = pair[:, at * rows:(at + 1) * rows].reshape(2 * rows, ROWS_IN)
                here = pl.ds(pl.multiple_of(at * (TOK // 2) + p * 2 * rows, 2 * rows), 2 * rows)
                tokens[here, :] = piece.astype(BF16)

        @pl.loop(0, CORE)
        def _(c):
            product = lax.dot_general(bi[level, c], tokens[...], NT, preferred_element_type=F32)
            part_in[level, c] = product.reshape(X, PIECE, TOK)
            rx_s[level, c] = product.astype(BF16).reshape(X, PIECE, TOK)
            for k in range(CORE):
                @pl.when(c == k)
                def _(k=k):
                    for d in (2, 1, 3):
                        links.start(
                            rx_s.at[level, k, x_of[d]], rx.at[level, k, d - 1], x_peer[d],
                            x_sem.at[level, k, d - 1], lambda: zs.at[level, k],
                        )

    def add_x(level, c):
        for d in range(X - 1):
            links.landed(rx.at[level, c, d], x_sem.at[level, c, d], mate)
        total = part_in[level, c, x]
        for d in range(X - 1):
            total = total + rx[level, c, d].astype(F32)
        part_in[level, c, x] = total
        zs[level, c] = total.astype(BF16)
        links.start(
            zs.at[level, c], zr.at[level, c], hi_peer, hi_sem.at[level, c],
            lambda: zs.at[level, c],
        )

    def add_hi(level, c):
        links.landed(zr.at[level, c], hi_sem.at[level, c], mate)
        total = part_in[level, c, x] + zr[level, c].astype(F32)
        give[level, c] = total.astype(BF16)

        @pl.when(core == c)
        def _():
            rin[level, core, x] = give[level, c]

        @pl.when(core != c)
        def _():
            pltpu.make_async_remote_copy(
                src_ref=give.at[level, c],
                dst_ref=rin.at[level, core, x],
                send_sem=give_sem.at[level],
                recv_sem=piece_sem.at[level, 0, core],
                device_id=mate,
                device_id_type=MESH,
            ).start()

        for d in (1, 2, 3):
            links.start(
                give.at[level, c], rin.at[level, core, x], device(hi, x_of[d], z, y, c),
                piece_sem.at[level, d, core], lambda: give.at[level, c],
            )

    along_z(0, 1)
    along_y(0, 0)
    along_z(0, 2)
    for load in loads[2:6]:
        load.wait()
    theirs = grads.at[:, hi, x, :, bo_span]
    grads_in = [
        links.start(grads_s.at[core], theirs, hi_peer),
        links.start(grads_s.at[other], theirs, hi_other),
        links.start(grads_s.at[other], theirs, mate),
    ]
    along_y(1, 0)
    bo_swap = links.start(bo.at[:, bo_span, :], bo.at[:, bo_span, :], mate)
    for c in range(CORE):
        @pl.when(core == c)
        def _(c=c):
            grads[:, hi, x, :, pl.ds(c * ROWS_OUT, ROWS_OUT)] = grads_s[c]

    segment = sort_segments()

    along_z(0, 3)
    spread(0, 1)
    spread(0, 2)
    along_z(1, 1)
    along_z(1, 2)
    pass_on(0, 0)
    received(grads_in)
    block = grads.at[:, :, x]
    grads_x = [links.start(block, block, x_peer[d]) for d in (2, 1, 3)]
    spread(0, 3)
    along_z(1, 3)
    bi_0 = links.start(bi_hbm.at[0], bi.at[0, core], mate)
    prepare(0)
    pass_on(0, 1)
    received([bo_swap])
    received(grads_x)
    out = [rotate_out(0), None]
    spread(1, 1)
    spread(1, 2)
    pass_on(0, 2)
    pass_on(1, 0)
    pass_on(0, 3)
    spread(1, 3)
    bi_1 = links.start(bi_hbm.at[1], bi.at[1, core], mate)
    out[0] = add_y(0, out[0])
    pass_on(1, 1)
    gathered(0)
    loads[6].wait()
    received([bi_0])
    rotate(0)

    out[0] = add_z(0, out[0])
    out[1] = rotate_out(1)
    add_x(0, 0)
    prepare(1)
    pass_on(1, 2)
    pass_on(1, 3)
    gathered(1)
    loads[7].wait()
    received([bi_1])
    rotate(1)
    add_x(0, 1)
    gather_y(0, out[0])
    out[1] = add_y(1, out[1])
    add_x(1, 0)
    hand_over(0)
    add_hi(0, 0)
    add_hi(0, 1)
    add_x(1, 1)
    out[1] = add_z(1, out[1])
    handed(0)

    scores[...] = jnp.zeros_like(scores)

    @pl.loop(0, LAYERS * X)
    def _(step):
        level, d = step // X, step % X
        at = lax.rem(x + X - d, X)

        @pl.when(step == 1)
        def _():
            gather_y(1, out[1])

        @pl.when(step == 4)
        def _():
            add_hi(1, 0)
            hand_over(1)
            add_hi(1, 1)
            handed(1)

        links.landed(rin.at[level, other, at], piece_sem.at[level, d, other], mate)

        @pl.when(d != 0)
        def _():
            links.landed(rin.at[level, core, at], piece_sem.at[level, d, core], mate)

        both = [rin[level, c, at] for c in range(CORE)]
        train_in = jnp.concatenate([b[:, :TOK // 2] for b in both], axis=1).astype(F32)
        query_in = jnp.concatenate([b[:, TOK // 2:] for b in both], axis=1)
        scale = eig[level, pl.ds(pl.multiple_of(at * PIECE, PIECE), PIECE), :]
        query_out = out_t[1, level].reshape(TOK, COLS_OUT)
        train_out = out_t[0, level].reshape(TOK, COLS_OUT)

        @pl.loop(0, QUERIES // GROUP)
        def _(g):
            masked = []
            for k in range(GROUP):
                member = (segment == (g * GROUP + k).astype(F32)).astype(F32).astype(BF16)
                masked.append(query_in * member)
            masked = jnp.concatenate(masked, axis=0)
            cross = jnp.dot(masked, query_out, preferred_element_type=F32)
            cross = cross.reshape(GROUP, PIECE, COLS_OUT) * scale[None]
            precond = cross.astype(BF16).reshape(GROUP * PIECE, COLS_OUT)
            right = lax.dot_general(precond, train_out, NT, preferred_element_type=F32)
            right = right.reshape(GROUP, PIECE, TOK) * train_in[None]
            right = jnp.sum(right.reshape(GROUP, PIECE // 8, 8, TOK), axis=1)
            here = pl.ds(g * GROUP, GROUP)
            scores[here] = scores[here] + right

    summed = jnp.sum(scores[...], axis=1)
    half = TOK // 2
    es1[0] = summed[:, :half]
    es1[1] = summed[:, half:]
    ends = []
    for d in (4, 3, 5, 2, 6, 1, 7, 0):
        ends.append(links.start(es1.at[other], er1.at[HI * Z + d], ring_other[d]))
        if d:
            ends.append(links.start(es1.at[core], er1.at[d], ring_peer[d]))
    links.finish()
    for level in range(LAYERS):
        pltpu.make_async_remote_copy(
            src_ref=give.at[level, 0],
            dst_ref=give.at[level, 0],
            send_sem=give_sem.at[level],
            recv_sem=recv_sem.at[0],
            device_id=mate,
            device_id_type=MESH,
        ).wait_send()
    received(ends)
    er1[0] = es1[core]
    total = jnp.sum(er1[...], axis=0)
    es2[...] = total
    ends = []
    for at, (dx, dy) in enumerate(flat):
        ends.append(links.start(es2, er2.at[at], flat_peer[at]))
    received(ends)
    total = total + jnp.sum(er2[...], axis=0)
    own = half // (Z * Y)
    total = pltpu.roll(total, lax.rem(half - (z * Y + y) * own, half), axis=1)
    out_ref[...] = total.T[:own]
    links.finish()


def fused(ta, qa, tg, qg, basis_in, basis_out, eigen, segment):
    y_rows = TOK // Y
    z_rows = y_rows // Z
    half = TOK // 2
    scratch = [
        pltpu.VMEM((16, ROWS_IN), BF16),
        pltpu.VMEM((16, ROWS_IN), BF16),
        pltpu.VMEM((1, TOK), jnp.int32),
        pltpu.VMEM((LAYERS, CORE, COLS_IN, ROWS_IN), BF16),
        pltpu.VMEM((LAYERS, COLS_IN, COLS_OUT), F32),
        pltpu.VMEM((TOK, ROWS_IN), BF16),
        pltpu.VMEM((LAYERS, Z, Y, 16, ROWS_IN), BF16),
        pltpu.VMEM((2, LAYERS, 32, ROWS_OUT), BF16),
        pltpu.VMEM((LAYERS, HI, X, 32, CORE * ROWS_OUT), BF16),
        pltpu.VMEM((LAYERS, CORE * ROWS_OUT, COLS_OUT), BF16),
        pltpu.VMEM((LAYERS, TOK, COLS_OUT), F32),
        pltpu.VMEM((LAYERS, Y, y_rows, COLS_OUT), BF16),
        pltpu.VMEM((LAYERS, Y - 1, y_rows, COLS_OUT), BF16),
        pltpu.VMEM((LAYERS, Z, z_rows, COLS_OUT), F32),
        pltpu.VMEM((LAYERS, Z - 1, z_rows, COLS_OUT), F32),
        pltpu.VMEM((2, LAYERS, Y, Z, z_rows, COLS_OUT), BF16),
        pltpu.VMEM((LAYERS, 2, X, PIECE, TOK), F32),
        pltpu.VMEM((LAYERS, 2, X, PIECE, TOK), BF16),
        pltpu.VMEM((LAYERS, 2, X - 1, PIECE, TOK), BF16),
        pltpu.VMEM((LAYERS, 2, PIECE, TOK), BF16),
        pltpu.VMEM((LAYERS, 2, PIECE, TOK), BF16),
        pltpu.VMEM((LAYERS, CORE, PIECE, TOK), BF16),
        pltpu.VMEM((LAYERS, 2, X, PIECE, TOK), BF16),
        pltpu.VMEM((QUERIES, 8, TOK), F32),
        pltpu.VMEM((2, QUERIES, half), F32),
        pltpu.VMEM((HI * Z * CORE, QUERIES, half), F32),
        pltpu.VMEM((QUERIES, half), F32),
        pltpu.VMEM((X * Y - 1, QUERIES, half), F32),
        pltpu.SemaphoreType.DMA((6 + 2 * LAYERS,)),
        pltpu.SemaphoreType.DMA((COPIES,)),
        pltpu.SemaphoreType.DMA((COPIES,)),
        pltpu.SemaphoreType.DMA((LAYERS, Z)),
        pltpu.SemaphoreType.DMA((LAYERS, 2, Z)),
        pltpu.SemaphoreType.DMA((LAYERS, Z)),
        pltpu.SemaphoreType.DMA((LAYERS, X, 2)),
        pltpu.SemaphoreType.DMA((LAYERS, CORE, X - 1)),
        pltpu.SemaphoreType.DMA((LAYERS, CORE)),
        pltpu.SemaphoreType.DMA((LAYERS,)),
        pltpu.SemaphoreType.DMA((LAYERS,)),
        pltpu.SemaphoreType.DMA((LAYERS, Y)),
    ]
    return pl.pallas_call(
        kernel,
        out_shape=jax.ShapeDtypeStruct((half // (Z * Y), QUERIES), F32),
        in_specs=[pl.BlockSpec(memory_space=pl.ANY)] * 8,
        out_specs=pl.BlockSpec(memory_space=pltpu.VMEM),
        scratch_shapes=scratch,
        compiler_params=pltpu.CompilerParams(
            collective_id=0, has_side_effects=True, vmem_limit_bytes=VMEM_LIMIT
        ),
        cost_estimate=pl.CostEstimate(flops=9_400_000_000, bytes_accessed=6_000_000, transcendentals=0),
    )(ta, qa, tg, qg, basis_out, segment, basis_in, eigen)


def on_device(
    train_acts, query_acts, train_grads, query_grads, basis_in, basis_out, eigen, query_segment
):
    own = fused(
        train_acts.reshape(-1, ROWS_IN),
        query_acts.reshape(-1, ROWS_IN),
        train_grads,
        query_grads,
        jnp.swapaxes(basis_in, 1, 2),
        basis_out,
        jnp.swapaxes(eigen, 1, 2),
        query_segment.reshape(1, TOK),
    )
    return jnp.swapaxes(own, 0, 1)


def solution(mesh):
    placed = (
        P(None, "seq", "layer"),
        P(None, "seq", "layer"),
        P(None, "layer", "seq"),
        P(None, "layer", "seq"),
        P(None, "layer", "seq"),
        P(None, "seq", "layer"),
        P(None, "layer", "seq"),
        P(),
    )
    return jax.shard_map(
        on_device, mesh=mesh, in_specs=placed, out_specs=P(None, "seq"), check_vma=False
    )
```

```python
import functools
import math

import jax
import jax.numpy as jnp
from jax import lax
from jax.experimental import pallas as pl
from jax.experimental.pallas import tpu as pltpu
from jax.sharding import PartitionSpec as P

D = 4096
FF = 14336
QUERIES = 16
LAYERS = 2
QMOST = 128
DAMPING = 0.1

MESH = pl.DeviceIdType.MESH
BF16 = jnp.bfloat16
F32 = jnp.float32

HI, X, Z, Y, CORE = 2, 4, 4, 4, 2
TOK = 256
ROWS_IN = FF // (HI * X)
COLS_IN = FF // (Z * Y * CORE)
ROWS_OUT = D // (Z * Y * CORE)
COLS_OUT = D // (HI * X)
COPIES = 160
PIECE = COLS_IN // X
GROUP = 16
VMEM_LIMIT = 62 * 1024 * 1024
NT = (((1,), (1,)), ((), ()))


class Links:
    def __init__(self, send_sem, recv_sem, peer):
        self.send_sem, self.recv_sem, self.peer = send_sem, recv_sem, peer
        self.sent = []
        self.pooled = 0
        self.finished = 0

    def start(self, src, dst, peer, recv=None, again=None):
        if recv is None:
            recv = self.recv_sem.at[self.pooled]
            self.pooled += 1
        copy = pltpu.make_async_remote_copy(
            src_ref=src,
            dst_ref=dst,
            send_sem=self.send_sem.at[len(self.sent)],
            recv_sem=recv,
            device_id=peer,
            device_id_type=MESH,
        )
        copy.start()
        self.sent.append(again or (lambda: src))
        return copy

    def landed(self, block, recv, peer):
        pltpu.make_async_remote_copy(
            src_ref=block,
            dst_ref=block,
            send_sem=self.send_sem.at[0],
            recv_sem=recv,
            device_id=peer,
            device_id_type=MESH,
        ).wait_recv()

    def finish(self):
        for at in range(self.finished, len(self.sent)):
            block = self.sent[at]()
            pltpu.make_async_remote_copy(
                src_ref=block,
                dst_ref=block,
                send_sem=self.send_sem.at[at],
                recv_sem=self.recv_sem.at[0],
                device_id=self.peer,
                device_id_type=MESH,
            ).wait_send()
        self.finished = len(self.sent)


def received(copies):
    for copy in copies:
        copy.wait_recv()


def kernel(
    ta_hbm, qa_hbm, tg_hbm, qg_hbm, bo_hbm, seg_hbm, bi_hbm, eig_hbm,
    out_ref,
    ta, qa, seg, bi, eig, tokens, acts, grads_s, grads, bo,
    part_out, own_out, ry, rz_s, rz, out_t,
    part_in, rx_s, rx, zs, zr, give, rin,
    scores, es1, er1, es2, er2, es3, er3,
    local_sem, send_sem, recv_sem, z_sem, y_sem, on_sem, piece_sem, x_sem, hi_sem, hand_sem, give_sem, out_sem,
):
    li = lax.axis_index("layer")
    si = lax.axis_index("seq")
    hi, x = li // X, li % X
    z, y, core = si // (Y * CORE), (si // CORE) % Y, si % CORE
    other = 1 - core
    factor = 1.0 / math.sqrt(D * FF * QMOST)

    def device(hh, xx, zz, yy, cc):
        return {"layer": hh * X + xx, "seq": (zz * Y + yy) * CORE + cc}

    z_of = [lax.rem(z + d, Z) for d in range(Z)]
    y_of = [lax.rem(y + d, Y) for d in range(Y)]
    x_of = [lax.rem(x + d, X) for d in range(X)]
    ring_of = [lax.rem(hi * Z + z + d, HI * Z) for d in range(HI * Z)]
    mate = device(hi, x, z, y, other)
    z_peer = [device(hi, x, z_of[d], y, core) for d in range(Z)]
    y_peer = [device(hi, x, z, y_of[d], core) for d in range(Y)]
    x_peer = [device(hi, x_of[d], z, y, core) for d in range(X)]
    x_other = [device(hi, x_of[d], z, y, other) for d in range(X)]
    hi_peer = device(1 - hi, x, z, y, core)
    hi_other = device(1 - hi, x, z, y, other)
    ring_peer = [device(at // Z, x, at % Z, y, core) for at in ring_of]
    links = Links(send_sem, recv_sem, mate)

    barrier = pltpu.get_barrier_semaphore()
    peers = [mate, hi_other] + ring_peer[1:] + y_peer[1:] + x_peer[1:] + x_other[1:]
    for peer in peers:
        pl.semaphore_signal(barrier, inc=1, device_id=peer, device_id_type=MESH)

    bo_span = pl.ds(pl.multiple_of(core * ROWS_OUT, ROWS_OUT), ROWS_OUT)
    moves = [(ta_hbm, ta), (qa_hbm, qa), (tg_hbm, grads_s.at[0]), (qg_hbm, grads_s.at[1])]
    moves += [(bo_hbm, bo.at[:, bo_span, :]), (seg_hbm, seg)]
    moves += [(bi_hbm.at[level], bi.at[level, core]) for level in range(LAYERS)]
    moves += [(eig_hbm.at[level], eig.at[level]) for level in range(LAYERS)]
    loads = []
    for at, (src, dst) in enumerate(moves):
        loads.append(pltpu.make_async_copy(src, dst, local_sem.at[at]))
        loads[-1].start()

    for load in loads[:2]:
        load.wait()
    rows = ta.shape[0] // LAYERS
    for level in range(LAYERS):
        span = slice(level * rows, (level + 1) * rows)
        block = jnp.concatenate([ta[...].astype(F32)[span], qa[...].astype(F32)[span]], axis=0)
        acts[level, z, y] = block.astype(BF16)

    def sort_segments():
        wide = jnp.broadcast_to(seg[...].astype(F32), (8, TOK)).astype(BF16)
        old = lax.broadcasted_iota(jnp.int32, (TOK, TOK), 0)
        new = lax.broadcasted_iota(jnp.int32, (TOK, TOK), 1)
        half = TOK // CORE
        pair, far, odd = new % half // (half // 2), new % (half // 2) // 16, new % 16 // rows
        source = (far * Y + pair * 2 + odd) * 16 + new // half * rows + new % rows
        pick = (old == source).astype(F32).astype(BF16)
        return jnp.dot(wide, pick, preferred_element_type=F32)[:1]

    pl.semaphore_wait(barrier, len(peers))

    nearest = z - 1 + 2 * (1 - (z + Z - 1) // Z)
    farthest = 3 * (1 - z // 2)
    order = [z, nearest, 6 - z - nearest - farthest, farthest]

    def along_z(level, k):
        block = acts.at[level, z, y]
        links.start(block, block, device(hi, x, order[k], y, core), z_sem.at[level, z])

    def along_y(level, k):
        block = acts.at[level, order[k], y]
        links.start(block, block, y_peer[1], y_sem.at[level, 0, order[k]])
        links.start(block, block, y_peer[3], y_sem.at[level, 1, order[k]])

    def spread(level, k):
        links.landed(acts.at[level, order[k], y], z_sem.at[level, order[k]], mate)
        along_y(level, k)

    def pass_on(level, k):
        left = acts.at[level, order[k], y_of[3]]
        right = acts.at[level, order[k], y_of[1]]
        links.landed(left, y_sem.at[level, 0, order[k]], mate)
        if k % 2 == 0:
            links.start(left, left, y_peer[1], on_sem.at[level, order[k]])
        links.landed(right, y_sem.at[level, 1, order[k]], mate)
        if k % 2 == 1:
            links.start(right, right, y_peer[3], on_sem.at[level, order[k]])

    def gathered(level):
        for k in range(Z):
            links.landed(acts.at[level, order[k], y_of[2]], on_sem.at[level, order[k]], mate)

    y_rows = TOK // Y
    z_rows = y_rows // Z

    def rotate_out(level):
        own = grads[level].reshape(TOK, CORE * ROWS_OUT)
        product = jnp.dot(own, bo[level], preferred_element_type=F32)
        product = product.reshape(Z, Y // 2, 2, CORE, rows, COLS_OUT)
        product = jnp.transpose(product, (3, 1, 0, 2, 4, 5)).reshape(TOK, COLS_OUT)
        part_out[level] = product
        own_out[level] = product.astype(BF16).reshape(Y, y_rows, COLS_OUT)
        return [
            links.start(own_out.at[level, y_of[d]], ry.at[level, d - 1], y_peer[d])
            for d in (2, 1, 3)
        ]

    def add_y(level, starts):
        received(starts)
        total = part_out[level, pl.ds(pl.multiple_of(y * y_rows, y_rows), y_rows), :]
        for d in range(Y - 1):
            total = total + ry[level, d].astype(F32)
        rz_s[level] = total.reshape(Z, z_rows, COLS_OUT)
        return [
            links.start(rz_s.at[level, z_of[d]], rz.at[level, d - 1], z_peer[d])
            for d in (2, 1, 3)
        ]

    def add_z(level, starts):
        received(starts)
        total = rz_s[level, z]
        for d in range(Z - 1):
            total = total + rz[level, d]
        out_t[core, level, y, z] = total.astype(BF16)
        block = out_t.at[core, level, y, z]
        return [links.start(block, block, z_peer[d]) for d in (2, 1, 3)]

    def gather_y(level, starts):
        received(starts)
        for d in (2, 1, 3):
            block = out_t.at[core, level, y]
            links.start(
                block, block, y_peer[d], out_sem.at[level, d], lambda: out_t.at[core, level, 0]
            )

    def hand_over(level):
        for d in (2, 1, 3):
            links.landed(out_t.at[core, level, y_of[d]], out_sem.at[level, d], mate)
        block = out_t.at[core, level]
        links.start(block, block, mate, hand_sem.at[level], lambda: out_t.at[core, level])

    def handed(level):
        links.landed(out_t.at[other, level], hand_sem.at[level], mate)

    def prepare(level):
        loads[8 + level].wait()
        eig[level] = factor / (eig[level] + DAMPING)

    wide = TOK // 2
    pairs = (y // 2, 1 - y // 2)

    def lanes(slot):
        if slot == 0:
            return pl.ds(0, TOK)
        return pl.ds(pl.multiple_of(pairs[slot - 1] * wide, wide), wide)

    def sort(level, pair):
        @pl.loop(0, Z)
        def _(zz):
            block = acts[level, zz, pl.ds(pair * 2, 2)].astype(F32)
            for at in range(2):
                piece = block[:, at * rows:(at + 1) * rows].reshape(2 * rows, ROWS_IN)
                here = pl.ds(pl.multiple_of(pair * wide + at * (wide // 2) + zz * 16, 16), 16)
                tokens[here, :] = piece.astype(BF16)

    def rotate(slot):
        level = min(slot, 1)
        if slot == 0:
            sort(level, 0)
            sort(level, 1)
        else:
            sort(level, pairs[slot - 1])

        @pl.loop(0, CORE)
        def _(c):
            own = tokens[lanes(slot), :]
            product = lax.dot_general(bi[level, c], own, NT, preferred_element_type=F32)
            product = product.reshape(X, PIECE, product.shape[1])
            part_in[level, c, :, :, lanes(slot)] = product
            rx_s[level, c, :, :, lanes(slot)] = product.astype(BF16)
            for k in range(CORE):
                @pl.when(c == k)
                def _(k=k):
                    for d in (2, 1, 3):
                        links.start(
                            rx_s.at[level, k, x_of[d], :, lanes(slot)],
                            rx.at[level, k, d - 1, :, lanes(slot)],
                            x_peer[d], x_sem.at[slot, k, d - 1],
                            lambda: zs.at[level, k, :, lanes(slot)],
                        )

    def add_x(slot, c):
        level, here = min(slot, 1), lanes(slot)
        for d in range(X - 1):
            links.landed(rx.at[level, c, d, :, here], x_sem.at[slot, c, d], mate)
        total = part_in[level, c, x, :, here]
        for d in range(X - 1):
            total = total + rx[level, c, d, :, here].astype(F32)
        part_in[level, c, x, :, here] = total
        zs[level, c, :, here] = total.astype(BF16)
        links.start(
            zs.at[level, c, :, here], zr.at[level, c, :, here], hi_peer, hi_sem.at[slot, c],
            lambda: zs.at[level, c, :, lanes(slot)],
        )

    def add_hi(slot, c):
        level, here = min(slot, 1), lanes(slot)
        links.landed(zr.at[level, c, :, here], hi_sem.at[slot, c], mate)
        total = part_in[level, c, x, :, here] + zr[level, c, :, here].astype(F32)
        give[level, c, :, here] = total.astype(BF16)

        @pl.when(core == c)
        def _():
            rin[level, core, x, :, lanes(slot)] = give[level, c, :, lanes(slot)]

        @pl.when(core != c)
        def _():
            pltpu.make_async_remote_copy(
                src_ref=give.at[level, c, :, lanes(slot)],
                dst_ref=rin.at[level, core, x, :, lanes(slot)],
                send_sem=give_sem.at[slot],
                recv_sem=piece_sem.at[slot, 0, core],
                device_id=mate,
                device_id_type=MESH,
            ).start()

        for d in (1, 2, 3):
            links.start(
                give.at[level, c, :, here], rin.at[level, core, x, :, here],
                device(hi, x_of[d], z, y, c), piece_sem.at[slot, d, core],
                lambda: give.at[level, c, :, lanes(slot)],
            )

    along_z(0, 1)
    along_y(0, 0)
    along_z(0, 2)
    for load in loads[2:6]:
        load.wait()
    theirs = grads.at[:, hi, x, :, bo_span]
    grads_in = [
        links.start(grads_s.at[core], theirs, hi_peer),
        links.start(grads_s.at[other], theirs, hi_other),
        links.start(grads_s.at[other], theirs, mate),
    ]
    along_y(1, 0)
    bo_swap = links.start(bo.at[:, bo_span, :], bo.at[:, bo_span, :], mate)
    for c in range(CORE):
        @pl.when(core == c)
        def _(c=c):
            grads[:, hi, x, :, pl.ds(c * ROWS_OUT, ROWS_OUT)] = grads_s[c]

    segment = sort_segments()

    along_z(0, 3)
    spread(0, 1)
    spread(0, 2)
    along_z(1, 1)
    along_z(1, 2)
    pass_on(0, 0)
    received(grads_in)
    block = grads.at[:, :, x]
    grads_x = [links.start(block, block, x_peer[d]) for d in (2, 1, 3)]
    spread(0, 3)
    along_z(1, 3)
    bi_0 = links.start(bi_hbm.at[0], bi.at[0, core], mate)
    prepare(0)
    pass_on(0, 1)
    received([bo_swap])
    received(grads_x)
    out = [rotate_out(0), None]
    spread(1, 1)
    spread(1, 2)
    pass_on(0, 2)
    pass_on(1, 0)
    pass_on(0, 3)
    spread(1, 3)
    bi_1 = links.start(bi_hbm.at[1], bi.at[1, core], mate)
    out[0] = add_y(0, out[0])
    pass_on(1, 1)
    gathered(0)
    loads[6].wait()
    received([bi_0])
    rotate(0)

    pass_on(1, 2)
    pass_on(1, 3)
    loads[7].wait()
    received([bi_1])
    rotate(1)
    out[0] = add_z(0, out[0])
    out[1] = rotate_out(1)
    add_x(0, 0)
    prepare(1)
    gathered(1)
    rotate(2)
    add_x(0, 1)
    add_x(1, 0)
    add_x(1, 1)
    gather_y(0, out[0])
    out[1] = add_y(1, out[1])
    add_x(2, 0)
    hand_over(0)
    add_hi(0, 0)
    add_hi(0, 1)
    add_x(2, 1)
    out[1] = add_z(1, out[1])
    handed(0)

    scores[...] = jnp.zeros_like(scores)

    @pl.loop(0, LAYERS * X)
    def _(step):
        level, d = step // X, step % X
        at = lax.rem(x + X - d, X)

        @pl.when(step == 1)
        def _():
            gather_y(1, out[1])

        @pl.when(step == 3)
        def _():
            add_hi(1, 0)
            add_hi(1, 1)

        @pl.when(step == 4)
        def _():
            add_hi(2, 0)
            hand_over(1)
            add_hi(2, 1)
            handed(1)

        def arrived(stream):
            @pl.when(level == 0)
            def _():
                links.landed(rin.at[0, stream, at], piece_sem.at[0, d, stream], mate)

            @pl.when(level == 1)
            def _():
                for slot in (1, 2):
                    links.landed(
                        rin.at[1, stream, at, :, lanes(slot)], piece_sem.at[slot, d, stream], mate
                    )

        arrived(other)

        @pl.when(d != 0)
        def _():
            arrived(core)

        low = lax.broadcasted_iota(jnp.int32, (PIECE, wide), 1) < wide // 2
        train_in, query_in = [], []
        for c in range(CORE):
            both = rin[level, c, at].astype(F32)
            one, two = both[:, :wide], both[:, wide:]
            train_in.append(jnp.where(low, one, pltpu.roll(two, wide // 2, axis=1)))
            query_in.append(jnp.where(low, pltpu.roll(one, wide // 2, axis=1), two))
        train_in = jnp.concatenate(train_in, axis=1)
        query_in = jnp.concatenate(query_in, axis=1).astype(BF16)
        scale = eig[level, pl.ds(pl.multiple_of(at * PIECE, PIECE), PIECE), :]
        query_out = out_t[1, level].reshape(TOK, COLS_OUT)
        train_out = out_t[0, level].reshape(TOK, COLS_OUT)

        @pl.loop(0, QUERIES // GROUP)
        def _(g):
            masked = []
            for k in range(GROUP):
                member = (segment == (g * GROUP + k).astype(F32)).astype(F32).astype(BF16)
                masked.append(query_in * member)
            masked = jnp.concatenate(masked, axis=0)
            cross = jnp.dot(masked, query_out, preferred_element_type=F32)
            cross = cross.reshape(GROUP, PIECE, COLS_OUT) * scale[None]
            precond = cross.astype(BF16).reshape(GROUP * PIECE, COLS_OUT)
            right = lax.dot_general(precond, train_out, NT, preferred_element_type=F32)
            right = right.reshape(GROUP, PIECE, TOK) * train_in[None]
            right = jnp.sum(right.reshape(GROUP, PIECE // 8, 8, TOK), axis=1)
            here = pl.ds(g * GROUP, GROUP)
            scores[here] = scores[here] + right

    summed = jnp.sum(scores[...], axis=1)
    half = TOK // 2
    es1[0] = summed[:, :half]
    es1[1] = summed[:, half:]
    ends = []
    for d in (2, 1, 3):
        ends.append(links.start(es1.at[other], er1.at[X - 1 + d], x_other[d]))
        ends.append(links.start(es1.at[core], er1.at[d], x_peer[d]))
    ends.append(links.start(es1.at[other], er1.at[0], mate))
    links.finish()
    for slot in range(LAYERS + 1):
        block = give.at[min(slot, 1), 0, :, lanes(slot)]
        pltpu.make_async_remote_copy(
            src_ref=block,
            dst_ref=block,
            send_sem=give_sem.at[slot],
            recv_sem=recv_sem.at[0],
            device_id=mate,
            device_id_type=MESH,
        ).wait_send()
    received(ends)
    total = es1[core]
    for d in range(X * CORE - 1):
        total = total + er1[d]
    es2[...] = total
    ends = []
    for d in (4, 3, 5, 2, 6, 1, 7):
        ends.append(links.start(es2, er2.at[d - 1], ring_peer[d]))
    received(ends)
    for d in range(HI * Z - 1):
        total = total + er2[d]
    es3[...] = total
    ends = [links.start(es3, er3.at[d - 1], y_peer[d]) for d in (2, 1, 3)]
    received(ends)
    for d in range(Y - 1):
        total = total + er3[d]
    own = half // (Z * Y)
    total = pltpu.roll(total, lax.rem(half - (y // 2 * Z * 2 + z * 2 + y % 2) * own, half), axis=1)
    out_ref[...] = total.T[:own]
    links.finish()


def fused(ta, qa, tg, qg, basis_in, basis_out, eigen, segment):
    y_rows = TOK // Y
    z_rows = y_rows // Z
    half = TOK // 2
    scratch = [
        pltpu.VMEM((16, ROWS_IN), BF16),
        pltpu.VMEM((16, ROWS_IN), BF16),
        pltpu.VMEM((1, TOK), jnp.int32),
        pltpu.VMEM((LAYERS, CORE, COLS_IN, ROWS_IN), BF16),
        pltpu.VMEM((LAYERS, COLS_IN, COLS_OUT), F32),
        pltpu.VMEM((TOK, ROWS_IN), BF16),
        pltpu.VMEM((LAYERS, Z, Y, 16, ROWS_IN), BF16),
        pltpu.VMEM((2, LAYERS, 32, ROWS_OUT), BF16),
        pltpu.VMEM((LAYERS, HI, X, 32, CORE * ROWS_OUT), BF16),
        pltpu.VMEM((LAYERS, CORE * ROWS_OUT, COLS_OUT), BF16),
        pltpu.VMEM((LAYERS, TOK, COLS_OUT), F32),
        pltpu.VMEM((LAYERS, Y, y_rows, COLS_OUT), BF16),
        pltpu.VMEM((LAYERS, Y - 1, y_rows, COLS_OUT), BF16),
        pltpu.VMEM((LAYERS, Z, z_rows, COLS_OUT), F32),
        pltpu.VMEM((LAYERS, Z - 1, z_rows, COLS_OUT), F32),
        pltpu.VMEM((2, LAYERS, Y, Z, z_rows, COLS_OUT), BF16),
        pltpu.VMEM((LAYERS, 2, X, PIECE, TOK), F32),
        pltpu.VMEM((LAYERS, 2, X, PIECE, TOK), BF16),
        pltpu.VMEM((LAYERS, 2, X - 1, PIECE, TOK), BF16),
        pltpu.VMEM((LAYERS, 2, PIECE, TOK), BF16),
        pltpu.VMEM((LAYERS, 2, PIECE, TOK), BF16),
        pltpu.VMEM((LAYERS, CORE, PIECE, TOK), BF16),
        pltpu.VMEM((LAYERS, 2, X, PIECE, TOK), BF16),
        pltpu.VMEM((QUERIES, 8, TOK), F32),
        pltpu.VMEM((2, QUERIES, half), F32),
        pltpu.VMEM((HI * Z - 1, QUERIES, half), F32),
        pltpu.VMEM((QUERIES, half), F32),
        pltpu.VMEM((Y * CORE - 1, QUERIES, half), F32),
        pltpu.VMEM((QUERIES, half), F32),
        pltpu.VMEM((X - 1, QUERIES, half), F32),
        pltpu.SemaphoreType.DMA((6 + 2 * LAYERS,)),
        pltpu.SemaphoreType.DMA((COPIES,)),
        pltpu.SemaphoreType.DMA((COPIES,)),
        pltpu.SemaphoreType.DMA((LAYERS, Z)),
        pltpu.SemaphoreType.DMA((LAYERS, 2, Z)),
        pltpu.SemaphoreType.DMA((LAYERS, Z)),
        pltpu.SemaphoreType.DMA((LAYERS + 1, X, 2)),
        pltpu.SemaphoreType.DMA((LAYERS + 1, CORE, X - 1)),
        pltpu.SemaphoreType.DMA((LAYERS + 1, CORE)),
        pltpu.SemaphoreType.DMA((LAYERS,)),
        pltpu.SemaphoreType.DMA((LAYERS + 1,)),
        pltpu.SemaphoreType.DMA((LAYERS, Y)),
    ]
    return pl.pallas_call(
        kernel,
        out_shape=jax.ShapeDtypeStruct((half // (Z * Y), QUERIES), F32),
        in_specs=[pl.BlockSpec(memory_space=pl.ANY)] * 8,
        out_specs=pl.BlockSpec(memory_space=pltpu.VMEM),
        scratch_shapes=scratch,
        compiler_params=pltpu.CompilerParams(
            collective_id=0, has_side_effects=True, vmem_limit_bytes=VMEM_LIMIT
        ),
        cost_estimate=pl.CostEstimate(flops=9_400_000_000, bytes_accessed=6_000_000, transcendentals=0),
    )(ta, qa, tg, qg, basis_out, segment, basis_in, eigen)


def on_device(
    train_acts, query_acts, train_grads, query_grads, basis_in, basis_out, eigen, query_segment
):
    own = fused(
        train_acts.reshape(-1, ROWS_IN),
        query_acts.reshape(-1, ROWS_IN),
        train_grads,
        query_grads,
        jnp.swapaxes(basis_in, 1, 2),
        basis_out,
        jnp.swapaxes(eigen, 1, 2),
        query_segment.reshape(1, TOK),
    )
    return jnp.swapaxes(own, 0, 1)


def solution(mesh):
    placed = (
        P(None, "seq", "layer"),
        P(None, "seq", "layer"),
        P(None, "layer", "seq"),
        P(None, "layer", "seq"),
        P(None, "layer", "seq"),
        P(None, "seq", "layer"),
        P(None, "layer", "seq"),
        P(),
    )
    return jax.shard_map(
        on_device, mesh=mesh, in_specs=placed, out_specs=P(None, "seq"), check_vma=False
    )
```

```python
import functools
import math

import jax
import jax.numpy as jnp
from jax import lax
from jax.experimental import pallas as pl
from jax.experimental.pallas import tpu as pltpu
from jax.sharding import PartitionSpec as P

D = 4096
FF = 14336
QUERIES = 16
LAYERS = 2
QMOST = 128
DAMPING = 0.1

MESH = pl.DeviceIdType.MESH
BF16 = jnp.bfloat16
F32 = jnp.float32

HI, X, Z, Y, CORE = 2, 4, 4, 4, 2
TOK = 256
ROWS_IN = FF // (HI * X)
COLS_IN = FF // (Z * Y * CORE)
ROWS_OUT = D // (Z * Y * CORE)
COLS_OUT = D // (HI * X)
COPIES = 128
PIECE = COLS_IN // X
GROUP = 16
VMEM_LIMIT = 62 * 1024 * 1024
NT = (((1,), (1,)), ((), ()))


class Links:
    def __init__(self, send_sem, recv_sem, peer):
        self.send_sem, self.recv_sem, self.peer = send_sem, recv_sem, peer
        self.sent = []
        self.pooled = 0
        self.finished = 0

    def start(self, src, dst, peer, recv=None, again=None):
        if recv is None:
            recv = self.recv_sem.at[self.pooled]
            self.pooled += 1
        copy = pltpu.make_async_remote_copy(
            src_ref=src,
            dst_ref=dst,
            send_sem=self.send_sem.at[len(self.sent)],
            recv_sem=recv,
            device_id=peer,
            device_id_type=MESH,
        )
        copy.start()
        self.sent.append(again or (lambda: src))
        return copy

    def landed(self, block, recv, peer):
        pltpu.make_async_remote_copy(
            src_ref=block,
            dst_ref=block,
            send_sem=self.send_sem.at[0],
            recv_sem=recv,
            device_id=peer,
            device_id_type=MESH,
        ).wait_recv()

    def finish(self):
        for at in range(self.finished, len(self.sent)):
            block = self.sent[at]()
            pltpu.make_async_remote_copy(
                src_ref=block,
                dst_ref=block,
                send_sem=self.send_sem.at[at],
                recv_sem=self.recv_sem.at[0],
                device_id=self.peer,
                device_id_type=MESH,
            ).wait_send()
        self.finished = len(self.sent)


def received(copies):
    for copy in copies:
        copy.wait_recv()


def kernel(
    ta_hbm, qa_hbm, tg_hbm, qg_hbm, bo_hbm, seg_hbm, bi_hbm, eig_hbm,
    out_ref,
    ta, qa, seg, bi, eig, tokens, acts, grads_s, grads, bo,
    part_out, own_out, ry, rz_s, rz, out_t,
    part_in, rx_s, rx, zs, zr, give, rin,
    scores, es1, er1, es2, er2, es3, er3,
    local_sem, send_sem, recv_sem, z_sem, y_sem, on_sem, piece_sem, x_sem, hi_sem, hand_sem, give_sem, out_sem, pass_sem,
):
    li = lax.axis_index("layer")
    si = lax.axis_index("seq")
    hi, x = li // X, li % X
    z, y, core = si // (Y * CORE), (si // CORE) % Y, si % CORE
    other = 1 - core
    factor = 1.0 / math.sqrt(D * FF * QMOST)

    def device(hh, xx, zz, yy, cc):
        return {"layer": hh * X + xx, "seq": (zz * Y + yy) * CORE + cc}

    z_of = [lax.rem(z + d, Z) for d in range(Z)]
    y_of = [lax.rem(y + d, Y) for d in range(Y)]
    x_of = [lax.rem(x + d, X) for d in range(X)]
    ring_of = [lax.rem(hi * Z + z + d, HI * Z) for d in range(HI * Z)]
    mate = device(hi, x, z, y, other)
    z_peer = [device(hi, x, z_of[d], y, core) for d in range(Z)]
    y_peer = [device(hi, x, z, y_of[d], core) for d in range(Y)]
    x_peer = [device(hi, x_of[d], z, y, core) for d in range(X)]
    x_other = [device(hi, x_of[d], z, y, other) for d in range(X)]
    hi_peer = device(1 - hi, x, z, y, core)
    hi_other = device(1 - hi, x, z, y, other)
    ring_peer = [device(at // Z, x, at % Z, y, core) for at in ring_of]
    links = Links(send_sem, recv_sem, mate)

    barrier = pltpu.get_barrier_semaphore()
    peers = [mate, hi_other] + ring_peer[1:] + y_peer[1:] + x_peer[1:] + x_other[1:]
    for peer in peers:
        pl.semaphore_signal(barrier, inc=1, device_id=peer, device_id_type=MESH)

    bo_span = pl.ds(pl.multiple_of(core * ROWS_OUT, ROWS_OUT), ROWS_OUT)
    moves = [(ta_hbm, ta), (qa_hbm, qa), (tg_hbm, grads_s.at[0]), (qg_hbm, grads_s.at[1])]
    moves += [(bo_hbm, bo.at[:, bo_span, :]), (seg_hbm, seg)]
    moves += [(bi_hbm.at[level], bi.at[level, core]) for level in range(LAYERS)]
    moves += [(eig_hbm.at[level], eig.at[level]) for level in range(LAYERS)]
    loads = []
    for at, (src, dst) in enumerate(moves):
        loads.append(pltpu.make_async_copy(src, dst, local_sem.at[at]))
        loads[-1].start()

    for load in loads[:2]:
        load.wait()
    rows = ta.shape[0] // LAYERS
    for level in range(LAYERS):
        span = slice(level * rows, (level + 1) * rows)
        block = jnp.concatenate([ta[...].astype(F32)[span], qa[...].astype(F32)[span]], axis=0)
        acts[level, z, y] = block.astype(BF16)

    def sort_segments():
        wide = jnp.broadcast_to(seg[...].astype(F32), (8, TOK)).astype(BF16)
        old = lax.broadcasted_iota(jnp.int32, (TOK, TOK), 0)
        new = lax.broadcasted_iota(jnp.int32, (TOK, TOK), 1)
        half = TOK // CORE
        source = (new % half) // rows * (rows * CORE) + new // half * rows + new % rows
        pick = (old == source).astype(F32).astype(BF16)
        return jnp.dot(wide, pick, preferred_element_type=F32)[:1]

    pl.semaphore_wait(barrier, len(peers))

    nearest = z - 1 + 2 * (1 - (z + Z - 1) // Z)
    farthest = 3 * (1 - z // 2)
    order = [z, nearest, 6 - z - nearest - farthest, farthest]

    inner = z * (Z - 1 - z) > 0

    def to_z(level, at, zz, slot):
        block = acts.at[level, at, y]
        return pltpu.make_async_remote_copy(
            src_ref=block,
            dst_ref=block,
            send_sem=pass_sem.at[level, slot],
            recv_sem=z_sem.at[level, at],
            device_id=device(hi, x, zz, y, core),
            device_id_type=MESH,
        )

    def along_z(level):
        @pl.when(z > 0)
        def _():
            to_z(level, z, z - 1, 0).start()

        @pl.when(z < Z - 1)
        def _():
            to_z(level, z, z + 1, 1).start()

    def sent_z(level):
        @pl.when(z > 0)
        def _():
            to_z(level, z, z - 1, 0).wait_send()

        @pl.when(z < Z - 1)
        def _():
            to_z(level, z, z + 1, 1).wait_send()

        @pl.when(inner)
        def _():
            for k in range(1, Z):
                to_z(level, order[k], z - 1, 1 + k).wait_send()

    def along_y(level, k):
        block = acts.at[level, order[k], y]
        links.start(block, block, y_peer[1], y_sem.at[level, 0, order[k]])
        links.start(block, block, y_peer[3], y_sem.at[level, 1, order[k]])

    def spread(level, k):
        links.landed(acts.at[level, order[k], y], z_sem.at[level, order[k]], mate)

        @pl.when(inner)
        def _():
            onward = z + 1 - 2 * ((order[k] + Z - z) // Z)
            to_z(level, order[k], onward, 1 + k).start()

        along_y(level, k)

    def pass_on(level, k):
        left = acts.at[level, order[k], y_of[3]]
        right = acts.at[level, order[k], y_of[1]]
        links.landed(left, y_sem.at[level, 0, order[k]], mate)
        if k % 2 == 0:
            links.start(left, left, y_peer[1], on_sem.at[level, order[k]])
        links.landed(right, y_sem.at[level, 1, order[k]], mate)
        if k % 2 == 1:
            links.start(right, right, y_peer[3], on_sem.at[level, order[k]])

    def gathered(level):
        for k in range(Z):
            links.landed(acts.at[level, order[k], y_of[2]], on_sem.at[level, order[k]], mate)

    y_rows = TOK // Y
    z_rows = y_rows // Z

    def rotate_out(level):
        own = grads[level].reshape(TOK, CORE * ROWS_OUT)
        product = jnp.dot(own, bo[level], preferred_element_type=F32)
        product = product.reshape(TOK // (CORE * rows), CORE, rows, COLS_OUT)
        product = jnp.swapaxes(product, 0, 1).reshape(TOK, COLS_OUT)
        part_out[level] = product
        own_out[level] = product.astype(BF16).reshape(Y, y_rows, COLS_OUT)
        return [
            links.start(own_out.at[level, y_of[d]], ry.at[level, d - 1], y_peer[d])
            for d in (2, 1, 3)
        ]

    def add_y(level, starts):
        received(starts)
        total = part_out[level, pl.ds(pl.multiple_of(y * y_rows, y_rows), y_rows), :]
        for d in range(Y - 1):
            total = total + ry[level, d].astype(F32)
        rz_s[level] = total.reshape(Z, z_rows, COLS_OUT)
        return [
            links.start(rz_s.at[level, z_of[d]], rz.at[level, d - 1], z_peer[d])
            for d in (2, 1, 3)
        ]

    def add_z(level, starts):
        received(starts)
        total = rz_s[level, z]
        for d in range(Z - 1):
            total = total + rz[level, d]
        out_t[core, level, y, z] = total.astype(BF16)
        block = out_t.at[core, level, y, z]
        return [links.start(block, block, z_peer[d]) for d in (2, 1, 3)]

    def gather_y(level, starts):
        received(starts)
        for d in (2, 1, 3):
            block = out_t.at[core, level, y]
            links.start(
                block, block, y_peer[d], out_sem.at[level, d], lambda: out_t.at[core, level, 0]
            )

    def hand_over(level):
        for d in (2, 1, 3):
            links.landed(out_t.at[core, level, y_of[d]], out_sem.at[level, d], mate)
        block = out_t.at[core, level]
        links.start(block, block, mate, hand_sem.at[level], lambda: out_t.at[core, level])

    def handed(level):
        links.landed(out_t.at[other, level], hand_sem.at[level], mate)

    def prepare(level):
        loads[8 + level].wait()
        eig[level] = factor / (eig[level] + DAMPING)

    def rotate(level):
        @pl.loop(0, TOK // 32)
        def _(p):
            pair = acts[level, p // (Y // 2), pl.ds(p % (Y // 2) * 2, 2)].astype(F32)
            for at in range(2):
                piece = pair[:, at * rows:(at + 1) * rows].reshape(2 * rows, ROWS_IN)
                here = pl.ds(pl.multiple_of(at * (TOK // 2) + p * 2 * rows, 2 * rows), 2 * rows)
                tokens[here, :] = piece.astype(BF16)

        @pl.loop(0, CORE)
        def _(c):
            product = lax.dot_general(bi[level, c], tokens[...], NT, preferred_element_type=F32)
            part_in[level, c] = product.reshape(X, PIECE, TOK)
            rx_s[level, c] = product.astype(BF16).reshape(X, PIECE, TOK)
            for k in range(CORE):
                @pl.when(c == k)
                def _(k=k):
                    for d in (2, 1, 3):
                        links.start(
                            rx_s.at[level, k, x_of[d]], rx.at[level, k, d - 1], x_peer[d],
                            x_sem.at[level, k, d - 1], lambda: zs.at[level, k],
                        )

    def add_x(level, c):
        for d in range(X - 1):
            links.landed(rx.at[level, c, d], x_sem.at[level, c, d], mate)
        total = part_in[level, c, x]
        for d in range(X - 1):
            total = total + rx[level, c, d].astype(F32)
        part_in[level, c, x] = total
        zs[level, c] = total.astype(BF16)
        links.start(
            zs.at[level, c], zr.at[level, c], hi_peer, hi_sem.at[level, c],
            lambda: zs.at[level, c],
        )

    def add_hi(level, c):
        links.landed(zr.at[level, c], hi_sem.at[level, c], mate)
        total = part_in[level, c, x] + zr[level, c].astype(F32)
        give[level, c] = total.astype(BF16)

        @pl.when(core == c)
        def _():
            rin[level, core, x] = give[level, c]

        @pl.when(core != c)
        def _():
            pltpu.make_async_remote_copy(
                src_ref=give.at[level, c],
                dst_ref=rin.at[level, core, x],
                send_sem=give_sem.at[level],
                recv_sem=piece_sem.at[level, 0, core],
                device_id=mate,
                device_id_type=MESH,
            ).start()

        for d in (1, 2, 3):
            links.start(
                give.at[level, c], rin.at[level, core, x], device(hi, x_of[d], z, y, c),
                piece_sem.at[level, d, core], lambda: give.at[level, c],
            )

    along_z(0)
    along_y(0, 0)
    for load in loads[2:6]:
        load.wait()
    theirs = grads.at[:, hi, x, :, bo_span]
    grads_in = [
        links.start(grads_s.at[core], theirs, hi_peer),
        links.start(grads_s.at[other], theirs, hi_other),
        links.start(grads_s.at[other], theirs, mate),
    ]
    along_y(1, 0)
    bo_swap = links.start(bo.at[:, bo_span, :], bo.at[:, bo_span, :], mate)
    for c in range(CORE):
        @pl.when(core == c)
        def _(c=c):
            grads[:, hi, x, :, pl.ds(c * ROWS_OUT, ROWS_OUT)] = grads_s[c]

    segment = sort_segments()

    spread(0, 1)
    spread(0, 2)
    along_z(1)
    pass_on(0, 0)
    received(grads_in)
    block = grads.at[:, :, x]
    grads_x = [links.start(block, block, x_peer[d]) for d in (2, 1, 3)]
    pass_on(0, 1)
    spread(0, 3)
    bi_0 = links.start(bi_hbm.at[0], bi.at[0, core], mate)
    prepare(0)
    received([bo_swap])
    received(grads_x)
    out = [rotate_out(0), None]
    spread(1, 1)
    spread(1, 2)
    pass_on(0, 2)
    pass_on(1, 0)
    pass_on(0, 3)
    spread(1, 3)
    bi_1 = links.start(bi_hbm.at[1], bi.at[1, core], mate)
    out[0] = add_y(0, out[0])
    pass_on(1, 1)
    gathered(0)
    loads[6].wait()
    received([bi_0])
    rotate(0)

    out[0] = add_z(0, out[0])
    out[1] = rotate_out(1)
    pass_on(1, 2)
    add_x(0, 0)
    pass_on(1, 3)
    gather_y(0, out[0])
    add_x(0, 1)
    prepare(1)
    out[1] = add_y(1, out[1])
    gathered(1)
    loads[7].wait()
    received([bi_1])
    rotate(1)
    hand_over(0)
    add_hi(0, 0)
    out[1] = add_z(1, out[1])
    add_hi(0, 1)
    add_x(1, 0)
    handed(0)

    scores[...] = jnp.zeros_like(scores)

    @pl.loop(0, LAYERS * X)
    def _(step):
        level, d = step // X, step % X
        at = lax.rem(x + X - d, X)

        @pl.when(step == 1)
        def _():
            add_x(1, 1)
            gather_y(1, out[1])

        @pl.when(step == 3)
        def _():
            hand_over(1)

        @pl.when(step == 4)
        def _():
            add_hi(1, 0)
            add_hi(1, 1)
            handed(1)

        links.landed(rin.at[level, other, at], piece_sem.at[level, d, other], mate)

        @pl.when(d != 0)
        def _():
            links.landed(rin.at[level, core, at], piece_sem.at[level, d, core], mate)

        both = [rin[level, c, at] for c in range(CORE)]
        train_in = jnp.concatenate([b[:, :TOK // 2] for b in both], axis=1).astype(F32)
        query_in = jnp.concatenate([b[:, TOK // 2:] for b in both], axis=1)
        scale = eig[level, pl.ds(pl.multiple_of(at * PIECE, PIECE), PIECE), :]
        query_out = out_t[1, level].reshape(TOK, COLS_OUT)
        train_out = out_t[0, level].reshape(TOK, COLS_OUT)

        @pl.loop(0, QUERIES // GROUP)
        def _(g):
            masked = []
            for k in range(GROUP):
                member = (segment == (g * GROUP + k).astype(F32)).astype(F32).astype(BF16)
                masked.append(query_in * member)
            masked = jnp.concatenate(masked, axis=0)
            cross = jnp.dot(masked, query_out, preferred_element_type=F32)
            cross = cross.reshape(GROUP, PIECE, COLS_OUT) * scale[None]
            precond = cross.astype(BF16).reshape(GROUP * PIECE, COLS_OUT)
            right = lax.dot_general(precond, train_out, NT, preferred_element_type=F32)
            right = right.reshape(GROUP, PIECE, TOK) * train_in[None]
            right = jnp.sum(right.reshape(GROUP, PIECE // 8, 8, TOK), axis=1)
            here = pl.ds(g * GROUP, GROUP)
            scores[here] = scores[here] + right

    summed = jnp.sum(scores[...], axis=1)
    half = TOK // 2
    es1[0] = summed[:, :half]
    es1[1] = summed[:, half:]
    ends = []
    for d in (2, 1, 3):
        ends.append(links.start(es1.at[other], er1.at[X - 1 + d], x_other[d]))
        ends.append(links.start(es1.at[core], er1.at[d], x_peer[d]))
    ends.append(links.start(es1.at[other], er1.at[0], mate))
    links.finish()
    for level in range(LAYERS):
        sent_z(level)
        pltpu.make_async_remote_copy(
            src_ref=give.at[level, 0],
            dst_ref=give.at[level, 0],
            send_sem=give_sem.at[level],
            recv_sem=recv_sem.at[0],
            device_id=mate,
            device_id_type=MESH,
        ).wait_send()
    received(ends)
    total = es1[core]
    for d in range(X * CORE - 1):
        total = total + er1[d]
    es2[...] = total
    ends = []
    for d in (4, 3, 5, 2, 6, 1, 7):
        ends.append(links.start(es2, er2.at[d - 1], ring_peer[d]))
    received(ends)
    for d in range(HI * Z - 1):
        total = total + er2[d]
    es3[...] = total
    ends = [links.start(es3, er3.at[d - 1], y_peer[d]) for d in (2, 1, 3)]
    received(ends)
    for d in range(Y - 1):
        total = total + er3[d]
    own = half // (Z * Y)
    total = pltpu.roll(total, lax.rem(half - (z * Y + y) * own, half), axis=1)
    out_ref[...] = total.T[:own]
    links.finish()


def fused(ta, qa, tg, qg, basis_in, basis_out, eigen, segment):
    y_rows = TOK // Y
    z_rows = y_rows // Z
    half = TOK // 2
    scratch = [
        pltpu.VMEM((16, ROWS_IN), BF16),
        pltpu.VMEM((16, ROWS_IN), BF16),
        pltpu.VMEM((1, TOK), jnp.int32),
        pltpu.VMEM((LAYERS, CORE, COLS_IN, ROWS_IN), BF16),
        pltpu.VMEM((LAYERS, COLS_IN, COLS_OUT), F32),
        pltpu.VMEM((TOK, ROWS_IN), BF16),
        pltpu.VMEM((LAYERS, Z, Y, 16, ROWS_IN), BF16),
        pltpu.VMEM((2, LAYERS, 32, ROWS_OUT), BF16),
        pltpu.VMEM((LAYERS, HI, X, 32, CORE * ROWS_OUT), BF16),
        pltpu.VMEM((LAYERS, CORE * ROWS_OUT, COLS_OUT), BF16),
        pltpu.VMEM((LAYERS, TOK, COLS_OUT), F32),
        pltpu.VMEM((LAYERS, Y, y_rows, COLS_OUT), BF16),
        pltpu.VMEM((LAYERS, Y - 1, y_rows, COLS_OUT), BF16),
        pltpu.VMEM((LAYERS, Z, z_rows, COLS_OUT), F32),
        pltpu.VMEM((LAYERS, Z - 1, z_rows, COLS_OUT), F32),
        pltpu.VMEM((2, LAYERS, Y, Z, z_rows, COLS_OUT), BF16),
        pltpu.VMEM((LAYERS, 2, X, PIECE, TOK), F32),
        pltpu.VMEM((LAYERS, 2, X, PIECE, TOK), BF16),
        pltpu.VMEM((LAYERS, 2, X - 1, PIECE, TOK), BF16),
        pltpu.VMEM((LAYERS, 2, PIECE, TOK), BF16),
        pltpu.VMEM((LAYERS, 2, PIECE, TOK), BF16),
        pltpu.VMEM((LAYERS, CORE, PIECE, TOK), BF16),
        pltpu.VMEM((LAYERS, 2, X, PIECE, TOK), BF16),
        pltpu.VMEM((QUERIES, 8, TOK), F32),
        pltpu.VMEM((2, QUERIES, half), F32),
        pltpu.VMEM((HI * Z - 1, QUERIES, half), F32),
        pltpu.VMEM((QUERIES, half), F32),
        pltpu.VMEM((Y * CORE - 1, QUERIES, half), F32),
        pltpu.VMEM((QUERIES, half), F32),
        pltpu.VMEM((X - 1, QUERIES, half), F32),
        pltpu.SemaphoreType.DMA((6 + 2 * LAYERS,)),
        pltpu.SemaphoreType.DMA((COPIES,)),
        pltpu.SemaphoreType.DMA((COPIES,)),
        pltpu.SemaphoreType.DMA((LAYERS, Z)),
        pltpu.SemaphoreType.DMA((LAYERS, 2, Z)),
        pltpu.SemaphoreType.DMA((LAYERS, Z)),
        pltpu.SemaphoreType.DMA((LAYERS, X, 2)),
        pltpu.SemaphoreType.DMA((LAYERS, CORE, X - 1)),
        pltpu.SemaphoreType.DMA((LAYERS, CORE)),
        pltpu.SemaphoreType.DMA((LAYERS,)),
        pltpu.SemaphoreType.DMA((LAYERS,)),
        pltpu.SemaphoreType.DMA((LAYERS, Y)),
        pltpu.SemaphoreType.DMA((LAYERS, 1 + Z)),
    ]
    return pl.pallas_call(
        kernel,
        out_shape=jax.ShapeDtypeStruct((half // (Z * Y), QUERIES), F32),
        in_specs=[pl.BlockSpec(memory_space=pl.ANY)] * 8,
        out_specs=pl.BlockSpec(memory_space=pltpu.VMEM),
        scratch_shapes=scratch,
        compiler_params=pltpu.CompilerParams(
            collective_id=0, has_side_effects=True, vmem_limit_bytes=VMEM_LIMIT
        ),
        cost_estimate=pl.CostEstimate(flops=9_400_000_000, bytes_accessed=6_000_000, transcendentals=0),
    )(ta, qa, tg, qg, basis_out, segment, basis_in, eigen)


def on_device(
    train_acts, query_acts, train_grads, query_grads, basis_in, basis_out, eigen, query_segment
):
    own = fused(
        train_acts.reshape(-1, ROWS_IN),
        query_acts.reshape(-1, ROWS_IN),
        train_grads,
        query_grads,
        jnp.swapaxes(basis_in, 1, 2),
        basis_out,
        jnp.swapaxes(eigen, 1, 2),
        query_segment.reshape(1, TOK),
    )
    return jnp.swapaxes(own, 0, 1)


def solution(mesh):
    placed = (
        P(None, "seq", "layer"),
        P(None, "seq", "layer"),
        P(None, "layer", "seq"),
        P(None, "layer", "seq"),
        P(None, "layer", "seq"),
        P(None, "seq", "layer"),
        P(None, "layer", "seq"),
        P(),
    )
    return jax.shard_map(
        on_device, mesh=mesh, in_specs=placed, out_specs=P(None, "seq"), check_vma=False
    )
```

```python
import functools
import math

import jax
import jax.numpy as jnp
from jax import lax
from jax.experimental import pallas as pl
from jax.experimental.pallas import tpu as pltpu
from jax.sharding import PartitionSpec as P

D = 4096
FF = 14336
QUERIES = 16
LAYERS = 2
QMOST = 128
DAMPING = 0.1

MESH = pl.DeviceIdType.MESH
BF16 = jnp.bfloat16
F32 = jnp.float32

HI, X, Z, Y, CORE = 2, 4, 4, 4, 2
TOK = 256
ROWS_IN = FF // (HI * X)
COLS_IN = FF // (Z * Y * CORE)
ROWS_OUT = D // (Z * Y * CORE)
COLS_OUT = D // (HI * X)
COPIES = 128
PIECE = COLS_IN // X
GROUP = 16
VMEM_LIMIT = 62 * 1024 * 1024
NT = (((1,), (1,)), ((), ()))


class Links:
    def __init__(self, send_sem, recv_sem, peer):
        self.send_sem, self.recv_sem, self.peer = send_sem, recv_sem, peer
        self.sent = []
        self.pooled = 0
        self.finished = 0

    def start(self, src, dst, peer, recv=None, again=None):
        if recv is None:
            recv = self.recv_sem.at[self.pooled]
            self.pooled += 1
        copy = pltpu.make_async_remote_copy(
            src_ref=src,
            dst_ref=dst,
            send_sem=self.send_sem.at[len(self.sent)],
            recv_sem=recv,
            device_id=peer,
            device_id_type=MESH,
        )
        copy.start()
        self.sent.append(again or (lambda: src))
        return copy

    def landed(self, block, recv, peer):
        pltpu.make_async_remote_copy(
            src_ref=block,
            dst_ref=block,
            send_sem=self.send_sem.at[0],
            recv_sem=recv,
            device_id=peer,
            device_id_type=MESH,
        ).wait_recv()

    def finish(self):
        for at in range(self.finished, len(self.sent)):
            block = self.sent[at]()
            pltpu.make_async_remote_copy(
                src_ref=block,
                dst_ref=block,
                send_sem=self.send_sem.at[at],
                recv_sem=self.recv_sem.at[0],
                device_id=self.peer,
                device_id_type=MESH,
            ).wait_send()
        self.finished = len(self.sent)


def received(copies):
    for copy in copies:
        copy.wait_recv()


def kernel(
    ta_hbm, qa_hbm, tg_hbm, qg_hbm, bo_hbm, seg_hbm, bi_hbm, eig_hbm,
    out_ref,
    ta, qa, seg, bi, eig, tokens, acts, grads_s, grads, bo,
    part_out, own_out, ry, rz_s, rz, out_t,
    part_in, rx_s, rx, zs, zr, give, rin,
    scores, es1, er1, es2, er2, es3, er3,
    local_sem, send_sem, recv_sem, z_sem, y_sem, on_sem, piece_sem, x_sem, hi_sem, hand_sem, give_sem, out_sem, pass_sem,
):
    li = lax.axis_index("layer")
    si = lax.axis_index("seq")
    hi, x = li // X, li % X
    z, y, core = si // (Y * CORE), (si // CORE) % Y, si % CORE
    other = 1 - core
    factor = 1.0 / math.sqrt(D * FF * QMOST)

    def device(hh, xx, zz, yy, cc):
        return {"layer": hh * X + xx, "seq": (zz * Y + yy) * CORE + cc}

    z_of = [lax.rem(z + d, Z) for d in range(Z)]
    y_of = [lax.rem(y + d, Y) for d in range(Y)]
    x_of = [lax.rem(x + d, X) for d in range(X)]
    ring_of = [lax.rem(hi * Z + z + d, HI * Z) for d in range(HI * Z)]
    mate = device(hi, x, z, y, other)
    z_peer = [device(hi, x, z_of[d], y, core) for d in range(Z)]
    y_peer = [device(hi, x, z, y_of[d], core) for d in range(Y)]
    x_peer = [device(hi, x_of[d], z, y, core) for d in range(X)]
    x_other = [device(hi, x_of[d], z, y, other) for d in range(X)]
    hi_peer = device(1 - hi, x, z, y, core)
    hi_other = device(1 - hi, x, z, y, other)
    ring_peer = [device(at // Z, x, at % Z, y, core) for at in ring_of]
    links = Links(send_sem, recv_sem, mate)

    barrier = pltpu.get_barrier_semaphore()
    peers = [mate, hi_other] + ring_peer[1:] + y_peer[1:] + x_peer[1:] + x_other[1:]
    for peer in peers:
        pl.semaphore_signal(barrier, inc=1, device_id=peer, device_id_type=MESH)

    bo_span = pl.ds(pl.multiple_of(core * ROWS_OUT, ROWS_OUT), ROWS_OUT)
    moves = [(ta_hbm, ta), (qa_hbm, qa), (tg_hbm, grads_s.at[0]), (qg_hbm, grads_s.at[1])]
    moves += [(bo_hbm, bo.at[:, bo_span, :]), (seg_hbm, seg)]
    moves += [(bi_hbm.at[level], bi.at[level, core]) for level in range(LAYERS)]
    moves += [(eig_hbm.at[level], eig.at[level]) for level in range(LAYERS)]
    loads = []
    for at, (src, dst) in enumerate(moves):
        loads.append(pltpu.make_async_copy(src, dst, local_sem.at[at]))
        loads[-1].start()

    for load in loads[:2]:
        load.wait()
    rows = ta.shape[0] // LAYERS
    for level in range(LAYERS):
        span = slice(level * rows, (level + 1) * rows)
        block = jnp.concatenate([ta[...].astype(F32)[span], qa[...].astype(F32)[span]], axis=0)
        acts[level, z, y] = block.astype(BF16)

    def sort_segments():
        wide = jnp.broadcast_to(seg[...].astype(F32), (8, TOK)).astype(BF16)
        old = lax.broadcasted_iota(jnp.int32, (TOK, TOK), 0)
        new = lax.broadcasted_iota(jnp.int32, (TOK, TOK), 1)
        half = TOK // CORE
        source = (new % half) // rows * (rows * CORE) + new // half * rows + new % rows
        pick = (old == source).astype(F32).astype(BF16)
        return jnp.dot(wide, pick, preferred_element_type=F32)[:1]

    pl.semaphore_wait(barrier, len(peers))

    nearest = z - 1 + 2 * (1 - (z + Z - 1) // Z)
    farthest = 3 * (1 - z // 2)
    order = [z, nearest, 6 - z - nearest - farthest, farthest]

    inner = z * (Z - 1 - z) > 0

    def to_z(level, at, zz, slot):
        block = acts.at[level, at, y]
        return pltpu.make_async_remote_copy(
            src_ref=block,
            dst_ref=block,
            send_sem=pass_sem.at[level, slot],
            recv_sem=z_sem.at[level, at],
            device_id=device(hi, x, zz, y, core),
            device_id_type=MESH,
        )

    def along_z(level):
        @pl.when(z > 0)
        def _():
            to_z(level, z, z - 1, 0).start()

        @pl.when(z < Z - 1)
        def _():
            to_z(level, z, z + 1, 1).start()

    def sent_z(level):
        @pl.when(z > 0)
        def _():
            to_z(level, z, z - 1, 0).wait_send()

        @pl.when(z < Z - 1)
        def _():
            to_z(level, z, z + 1, 1).wait_send()

        @pl.when(inner)
        def _():
            for k in range(1, Z):
                to_z(level, order[k], z - 1, 1 + k).wait_send()

    def along_y(level, k):
        block = acts.at[level, order[k], y]
        links.start(block, block, y_peer[1], y_sem.at[level, 0, order[k]])
        links.start(block, block, y_peer[3], y_sem.at[level, 1, order[k]])

    def spread(level, k):
        links.landed(acts.at[level, order[k], y], z_sem.at[level, order[k]], mate)

        @pl.when(inner)
        def _():
            onward = z + 1 - 2 * ((order[k] + Z - z) // Z)
            to_z(level, order[k], onward, 1 + k).start()

        along_y(level, k)

    def pass_on(level, k):
        left = acts.at[level, order[k], y_of[3]]
        right = acts.at[level, order[k], y_of[1]]
        links.landed(left, y_sem.at[level, 0, order[k]], mate)
        if k % 2 == 0:
            links.start(left, left, y_peer[1], on_sem.at[level, order[k]])
        links.landed(right, y_sem.at[level, 1, order[k]], mate)
        if k % 2 == 1:
            links.start(right, right, y_peer[3], on_sem.at[level, order[k]])

    def gathered(level):
        for k in range(Z):
            links.landed(acts.at[level, order[k], y_of[2]], on_sem.at[level, order[k]], mate)

    y_rows = TOK // Y
    z_rows = y_rows // Z

    def rotate_out(level):
        own = grads[level].reshape(TOK, CORE * ROWS_OUT)
        product = jnp.dot(own, bo[level], preferred_element_type=F32)
        product = product.reshape(TOK // (CORE * rows), CORE, rows, COLS_OUT)
        product = jnp.swapaxes(product, 0, 1).reshape(TOK, COLS_OUT)
        part_out[level] = product
        own_out[level] = product.astype(BF16).reshape(Y, y_rows, COLS_OUT)
        return [
            links.start(own_out.at[level, y_of[d]], ry.at[level, d - 1], y_peer[d])
            for d in (2, 1, 3)
        ]

    def add_y(level, starts):
        received(starts)
        total = part_out[level, pl.ds(pl.multiple_of(y * y_rows, y_rows), y_rows), :]
        for d in range(Y - 1):
            total = total + ry[level, d].astype(F32)
        rz_s[level] = total.reshape(Z, z_rows, COLS_OUT)
        return [
            links.start(rz_s.at[level, z_of[d]], rz.at[level, d - 1], z_peer[d])
            for d in (2, 1, 3)
        ]

    def add_z(level, starts):
        received(starts)
        total = rz_s[level, z]
        for d in range(Z - 1):
            total = total + rz[level, d]
        out_t[core, level, y, z] = total.astype(BF16)
        block = out_t.at[core, level, y, z]
        return [links.start(block, block, z_peer[d]) for d in (2, 1, 3)]

    def gather_y(level, starts):
        received(starts)
        for d in (2, 1, 3):
            block = out_t.at[core, level, y]
            links.start(
                block, block, y_peer[d], out_sem.at[level, d], lambda: out_t.at[core, level, 0]
            )

    def hand_over(level):
        for d in (2, 1, 3):
            links.landed(out_t.at[core, level, y_of[d]], out_sem.at[level, d], mate)
        block = out_t.at[core, level]
        links.start(block, block, mate, hand_sem.at[level], lambda: out_t.at[core, level])

    def handed(level):
        links.landed(out_t.at[other, level], hand_sem.at[level], mate)

    def prepare(level):
        loads[8 + level].wait()
        eig[level] = factor / (eig[level] + DAMPING)

    def rotate(level):
        @pl.loop(0, TOK // 32)
        def _(p):
            pair = acts[level, p // (Y // 2), pl.ds(p % (Y // 2) * 2, 2)].astype(F32)
            for at in range(2):
                piece = pair[:, at * rows:(at + 1) * rows].reshape(2 * rows, ROWS_IN)
                here = pl.ds(pl.multiple_of(at * (TOK // 2) + p * 2 * rows, 2 * rows), 2 * rows)
                tokens[here, :] = piece.astype(BF16)

        @pl.loop(0, CORE)
        def _(c):
            product = lax.dot_general(bi[level, c], tokens[...], NT, preferred_element_type=F32)
            part_in[level, c] = product.reshape(X, PIECE, TOK)
            rx_s[level, c] = product.astype(BF16).reshape(X, PIECE, TOK)
            for k in range(CORE):
                @pl.when(c == k)
                def _(k=k):
                    for d in (2, 1, 3):
                        links.start(
                            rx_s.at[level, k, x_of[d]], rx.at[level, k, d - 1], x_peer[d],
                            x_sem.at[level, k, d - 1], lambda: zs.at[level, k],
                        )

    def add_x(level, c):
        for d in range(X - 1):
            links.landed(rx.at[level, c, d], x_sem.at[level, c, d], mate)
        total = part_in[level, c, x]
        for d in range(X - 1):
            total = total + rx[level, c, d].astype(F32)
        part_in[level, c, x] = total
        zs[level, c] = total.astype(BF16)
        links.start(
            zs.at[level, c], zr.at[level, c], hi_peer, hi_sem.at[level, c],
            lambda: zs.at[level, c],
        )

    def add_hi(level, c):
        links.landed(zr.at[level, c], hi_sem.at[level, c], mate)
        total = part_in[level, c, x] + zr[level, c].astype(F32)
        give[level, c] = total.astype(BF16)

        @pl.when(core == c)
        def _():
            rin[level, core, x] = give[level, c]

        @pl.when(core != c)
        def _():
            pltpu.make_async_remote_copy(
                src_ref=give.at[level, c],
                dst_ref=rin.at[level, core, x],
                send_sem=give_sem.at[level],
                recv_sem=piece_sem.at[level, 0, core],
                device_id=mate,
                device_id_type=MESH,
            ).start()

        for d in (1, 2, 3):
            links.start(
                give.at[level, c], rin.at[level, core, x], device(hi, x_of[d], z, y, c),
                piece_sem.at[level, d, core], lambda: give.at[level, c],
            )

    along_z(0)
    along_y(0, 0)
    for load in loads[2:6]:
        load.wait()
    theirs = grads.at[:, hi, x, :, bo_span]
    grads_in = [
        links.start(grads_s.at[core], theirs, hi_peer),
        links.start(grads_s.at[other], theirs, hi_other),
        links.start(grads_s.at[other], theirs, mate),
    ]
    along_y(1, 0)
    bo_swap = links.start(bo.at[:, bo_span, :], bo.at[:, bo_span, :], mate)
    for c in range(CORE):
        @pl.when(core == c)
        def _(c=c):
            grads[:, hi, x, :, pl.ds(c * ROWS_OUT, ROWS_OUT)] = grads_s[c]

    segment = sort_segments()

    spread(0, 1)
    spread(0, 2)
    along_z(1)
    pass_on(0, 0)
    received(grads_in)
    block = grads.at[:, :, x]
    grads_x = [links.start(block, block, x_peer[d]) for d in (2, 1, 3)]
    pass_on(0, 1)
    spread(0, 3)
    bi_0 = links.start(bi_hbm.at[0], bi.at[0, core], mate)
    prepare(0)
    received([bo_swap])
    received(grads_x)
    out = [rotate_out(0), None]
    spread(1, 1)
    spread(1, 2)
    pass_on(0, 2)
    pass_on(1, 0)
    pass_on(0, 3)
    spread(1, 3)
    bi_1 = links.start(bi_hbm.at[1], bi.at[1, core], mate)
    out[0] = add_y(0, out[0])
    pass_on(1, 1)
    gathered(0)
    loads[6].wait()
    received([bi_0])
    rotate(0)

    out[0] = add_z(0, out[0])
    out[1] = rotate_out(1)
    pass_on(1, 2)
    add_x(0, 0)
    pass_on(1, 3)
    gather_y(0, out[0])
    add_x(0, 1)
    prepare(1)
    out[1] = add_y(1, out[1])
    gathered(1)
    loads[7].wait()
    received([bi_1])
    rotate(1)
    hand_over(0)
    add_hi(0, 0)
    out[1] = add_z(1, out[1])
    add_hi(0, 1)
    add_x(1, 0)
    handed(0)

    def given(level):
        pltpu.make_async_remote_copy(
            src_ref=give.at[level, 0],
            dst_ref=give.at[level, 0],
            send_sem=give_sem.at[level],
            recv_sem=recv_sem.at[0],
            device_id=mate,
            device_id_type=MESH,
        ).wait_send()

    scores[...] = jnp.zeros_like(scores)

    @pl.loop(0, LAYERS * X)
    def _(step):
        level, d = step // X, step % X
        at = lax.rem(x + X - d, X)

        @pl.when(step == 1)
        def _():
            add_x(1, 1)
            gather_y(1, out[1])

        @pl.when(step == 3)
        def _():
            hand_over(1)

        @pl.when(step == 4)
        def _():
            links.finish()
            for side in range(LAYERS):
                sent_z(side)
            given(0)
            add_hi(1, 0)
            add_hi(1, 1)
            handed(1)

        links.landed(rin.at[level, other, at], piece_sem.at[level, d, other], mate)

        @pl.when(d != 0)
        def _():
            links.landed(rin.at[level, core, at], piece_sem.at[level, d, core], mate)

        both = [rin[level, c, at] for c in range(CORE)]
        train_in = jnp.concatenate([b[:, :TOK // 2] for b in both], axis=1).astype(F32)
        query_in = jnp.concatenate([b[:, TOK // 2:] for b in both], axis=1)
        scale = eig[level, pl.ds(pl.multiple_of(at * PIECE, PIECE), PIECE), :]
        query_out = out_t[1, level].reshape(TOK, COLS_OUT)
        train_out = out_t[0, level].reshape(TOK, COLS_OUT)

        @pl.loop(0, QUERIES // GROUP)
        def _(g):
            masked = []
            for k in range(GROUP):
                member = (segment == (g * GROUP + k).astype(F32)).astype(F32).astype(BF16)
                masked.append(query_in * member)
            masked = jnp.concatenate(masked, axis=0)
            cross = jnp.dot(masked, query_out, preferred_element_type=F32)
            cross = cross.reshape(GROUP, PIECE, COLS_OUT) * scale[None]
            precond = cross.astype(BF16).reshape(GROUP * PIECE, COLS_OUT)
            right = lax.dot_general(precond, train_out, NT, preferred_element_type=F32)
            right = right.reshape(GROUP, PIECE, TOK) * train_in[None]
            right = jnp.sum(right.reshape(GROUP, PIECE // 8, 8, TOK), axis=1)
            here = pl.ds(g * GROUP, GROUP)
            scores[here] = scores[here] + right

    summed = jnp.sum(scores[...], axis=1)
    half = TOK // 2
    es1[0] = summed[:, :half]
    es1[1] = summed[:, half:]
    ends = []
    for d in (2, 1, 3):
        ends.append(links.start(es1.at[other], er1.at[X - 1 + d], x_other[d]))
        ends.append(links.start(es1.at[core], er1.at[d], x_peer[d]))
    ends.append(links.start(es1.at[other], er1.at[0], mate))
    links.finish()
    given(1)
    received(ends)
    total = es1[core]
    for d in range(X * CORE - 1):
        total = total + er1[d]
    es2[...] = total
    ends = []
    for d in (4, 3, 5, 2, 6, 1, 7):
        ends.append(links.start(es2, er2.at[d - 1], ring_peer[d]))
    received(ends)
    for d in range(HI * Z - 1):
        total = total + er2[d]
    es3[...] = total
    ends = [links.start(es3, er3.at[d - 1], y_peer[d]) for d in (2, 1, 3)]
    received(ends)
    for d in range(Y - 1):
        total = total + er3[d]
    own = half // (Z * Y)
    total = pltpu.roll(total, lax.rem(half - (z * Y + y) * own, half), axis=1)
    out_ref[...] = total.T[:own]
    links.finish()


def fused(ta, qa, tg, qg, basis_in, basis_out, eigen, segment):
    y_rows = TOK // Y
    z_rows = y_rows // Z
    half = TOK // 2
    scratch = [
        pltpu.VMEM((16, ROWS_IN), BF16),
        pltpu.VMEM((16, ROWS_IN), BF16),
        pltpu.VMEM((1, TOK), jnp.int32),
        pltpu.VMEM((LAYERS, CORE, COLS_IN, ROWS_IN), BF16),
        pltpu.VMEM((LAYERS, COLS_IN, COLS_OUT), F32),
        pltpu.VMEM((TOK, ROWS_IN), BF16),
        pltpu.VMEM((LAYERS, Z, Y, 16, ROWS_IN), BF16),
        pltpu.VMEM((2, LAYERS, 32, ROWS_OUT), BF16),
        pltpu.VMEM((LAYERS, HI, X, 32, CORE * ROWS_OUT), BF16),
        pltpu.VMEM((LAYERS, CORE * ROWS_OUT, COLS_OUT), BF16),
        pltpu.VMEM((LAYERS, TOK, COLS_OUT), F32),
        pltpu.VMEM((LAYERS, Y, y_rows, COLS_OUT), BF16),
        pltpu.VMEM((LAYERS, Y - 1, y_rows, COLS_OUT), BF16),
        pltpu.VMEM((LAYERS, Z, z_rows, COLS_OUT), F32),
        pltpu.VMEM((LAYERS, Z - 1, z_rows, COLS_OUT), F32),
        pltpu.VMEM((2, LAYERS, Y, Z, z_rows, COLS_OUT), BF16),
        pltpu.VMEM((LAYERS, 2, X, PIECE, TOK), F32),
        pltpu.VMEM((LAYERS, 2, X, PIECE, TOK), BF16),
        pltpu.VMEM((LAYERS, 2, X - 1, PIECE, TOK), BF16),
        pltpu.VMEM((LAYERS, 2, PIECE, TOK), BF16),
        pltpu.VMEM((LAYERS, 2, PIECE, TOK), BF16),
        pltpu.VMEM((LAYERS, CORE, PIECE, TOK), BF16),
        pltpu.VMEM((LAYERS, 2, X, PIECE, TOK), BF16),
        pltpu.VMEM((QUERIES, 8, TOK), F32),
        pltpu.VMEM((2, QUERIES, half), F32),
        pltpu.VMEM((HI * Z - 1, QUERIES, half), F32),
        pltpu.VMEM((QUERIES, half), F32),
        pltpu.VMEM((Y * CORE - 1, QUERIES, half), F32),
        pltpu.VMEM((QUERIES, half), F32),
        pltpu.VMEM((X - 1, QUERIES, half), F32),
        pltpu.SemaphoreType.DMA((6 + 2 * LAYERS,)),
        pltpu.SemaphoreType.DMA((COPIES,)),
        pltpu.SemaphoreType.DMA((COPIES,)),
        pltpu.SemaphoreType.DMA((LAYERS, Z)),
        pltpu.SemaphoreType.DMA((LAYERS, 2, Z)),
        pltpu.SemaphoreType.DMA((LAYERS, Z)),
        pltpu.SemaphoreType.DMA((LAYERS, X, 2)),
        pltpu.SemaphoreType.DMA((LAYERS, CORE, X - 1)),
        pltpu.SemaphoreType.DMA((LAYERS, CORE)),
        pltpu.SemaphoreType.DMA((LAYERS,)),
        pltpu.SemaphoreType.DMA((LAYERS,)),
        pltpu.SemaphoreType.DMA((LAYERS, Y)),
        pltpu.SemaphoreType.DMA((LAYERS, 1 + Z)),
    ]
    return pl.pallas_call(
        kernel,
        out_shape=jax.ShapeDtypeStruct((half // (Z * Y), QUERIES), F32),
        in_specs=[pl.BlockSpec(memory_space=pl.ANY)] * 8,
        out_specs=pl.BlockSpec(memory_space=pltpu.VMEM),
        scratch_shapes=scratch,
        compiler_params=pltpu.CompilerParams(
            collective_id=0, has_side_effects=True, vmem_limit_bytes=VMEM_LIMIT
        ),
        cost_estimate=pl.CostEstimate(flops=9_400_000_000, bytes_accessed=6_000_000, transcendentals=0),
    )(ta, qa, tg, qg, basis_out, segment, basis_in, eigen)


def on_device(
    train_acts, query_acts, train_grads, query_grads, basis_in, basis_out, eigen, query_segment
):
    own = fused(
        train_acts.reshape(-1, ROWS_IN),
        query_acts.reshape(-1, ROWS_IN),
        train_grads,
        query_grads,
        jnp.swapaxes(basis_in, 1, 2),
        basis_out,
        jnp.swapaxes(eigen, 1, 2),
        query_segment.reshape(1, TOK),
    )
    return jnp.swapaxes(own, 0, 1)


def solution(mesh):
    placed = (
        P(None, "seq", "layer"),
        P(None, "seq", "layer"),
        P(None, "layer", "seq"),
        P(None, "layer", "seq"),
        P(None, "layer", "seq"),
        P(None, "seq", "layer"),
        P(None, "layer", "seq"),
        P(),
    )
    return jax.shard_map(
        on_device, mesh=mesh, in_specs=placed, out_specs=P(None, "seq"), check_vma=False
    )
```

```python
import functools
import math

import jax
import jax.numpy as jnp
from jax import lax
from jax.experimental import pallas as pl
from jax.experimental.pallas import tpu as pltpu
from jax.sharding import PartitionSpec as P

D = 4096
FF = 14336
QUERIES = 16
LAYERS = 2
QMOST = 128
DAMPING = 0.1

MESH = pl.DeviceIdType.MESH
BF16 = jnp.bfloat16
F32 = jnp.float32

HI, X, Z, Y, CORE = 2, 4, 4, 4, 2
TOK = 256
ROWS_IN = FF // (HI * X)
COLS_IN = FF // (Z * Y * CORE)
ROWS_OUT = D // (Z * Y * CORE)
COLS_OUT = D // (HI * X)
COPIES = 128
PIECE = COLS_IN // X
GROUP = 16
VMEM_LIMIT = 62 * 1024 * 1024
NT = (((1,), (1,)), ((), ()))


class Links:
    def __init__(self, send_sem, recv_sem, peer):
        self.send_sem, self.recv_sem, self.peer = send_sem, recv_sem, peer
        self.sent = []
        self.pooled = 0
        self.finished = 0

    def start(self, src, dst, peer, recv=None, again=None):
        if recv is None:
            recv = self.recv_sem.at[self.pooled]
            self.pooled += 1
        copy = pltpu.make_async_remote_copy(
            src_ref=src,
            dst_ref=dst,
            send_sem=self.send_sem.at[len(self.sent)],
            recv_sem=recv,
            device_id=peer,
            device_id_type=MESH,
        )
        copy.start()
        self.sent.append(again or (lambda: src))
        return copy

    def landed(self, block, recv, peer):
        pltpu.make_async_remote_copy(
            src_ref=block,
            dst_ref=block,
            send_sem=self.send_sem.at[0],
            recv_sem=recv,
            device_id=peer,
            device_id_type=MESH,
        ).wait_recv()

    def finish(self):
        for at in range(self.finished, len(self.sent)):
            block = self.sent[at]()
            pltpu.make_async_remote_copy(
                src_ref=block,
                dst_ref=block,
                send_sem=self.send_sem.at[at],
                recv_sem=self.recv_sem.at[0],
                device_id=self.peer,
                device_id_type=MESH,
            ).wait_send()
        self.finished = len(self.sent)


def received(copies):
    for copy in copies:
        copy.wait_recv()


def kernel(
    ta_hbm, qa_hbm, tg_hbm, qg_hbm, bo_hbm, seg_hbm, bi_hbm, eig_hbm,
    out_ref,
    ta, qa, seg, bi, eig, tokens, acts, grads_s, grads, bo,
    part_out, own_out, ry, rz_s, rz, out_t,
    part_in, rx_s, rx, zs, zr, give, rin,
    scores, es1, er1, es2, er2, es3, er3,
    local_sem, send_sem, recv_sem, z_sem, y_sem, on_sem, piece_sem, x_sem, hi_sem, hand_sem, give_sem, out_sem, pass_sem,
):
    li = lax.axis_index("layer")
    si = lax.axis_index("seq")
    hi, x = li // X, li % X
    z, y, core = si // (Y * CORE), (si // CORE) % Y, si % CORE
    other = 1 - core
    factor = 1.0 / math.sqrt(D * FF * QMOST)

    def device(hh, xx, zz, yy, cc):
        return {"layer": hh * X + xx, "seq": (zz * Y + yy) * CORE + cc}

    z_of = [lax.rem(z + d, Z) for d in range(Z)]
    y_of = [lax.rem(y + d, Y) for d in range(Y)]
    x_of = [lax.rem(x + d, X) for d in range(X)]
    ring_of = [lax.rem(hi * Z + z + d, HI * Z) for d in range(HI * Z)]
    mate = device(hi, x, z, y, other)
    z_peer = [device(hi, x, z_of[d], y, core) for d in range(Z)]
    y_peer = [device(hi, x, z, y_of[d], core) for d in range(Y)]
    x_peer = [device(hi, x_of[d], z, y, core) for d in range(X)]
    x_other = [device(hi, x_of[d], z, y, other) for d in range(X)]
    hi_peer = device(1 - hi, x, z, y, core)
    hi_other = device(1 - hi, x, z, y, other)
    ring_peer = [device(at // Z, x, at % Z, y, core) for at in ring_of]
    links = Links(send_sem, recv_sem, mate)

    barrier = pltpu.get_barrier_semaphore()
    peers = [mate, hi_other] + ring_peer[1:] + y_peer[1:] + x_peer[1:] + x_other[1:]
    for peer in peers:
        pl.semaphore_signal(barrier, inc=1, device_id=peer, device_id_type=MESH)

    bo_span = pl.ds(pl.multiple_of(core * ROWS_OUT, ROWS_OUT), ROWS_OUT)
    moves = [(ta_hbm, ta), (qa_hbm, qa), (tg_hbm, grads_s.at[0]), (qg_hbm, grads_s.at[1])]
    moves += [(bo_hbm, bo.at[:, bo_span, :]), (seg_hbm, seg)]
    moves += [(bi_hbm.at[level], bi.at[level, core]) for level in range(LAYERS)]
    moves += [(eig_hbm.at[level], eig.at[level]) for level in range(LAYERS)]
    loads = []
    for at, (src, dst) in enumerate(moves):
        loads.append(pltpu.make_async_copy(src, dst, local_sem.at[at]))
        loads[-1].start()

    for load in loads[:2]:
        load.wait()
    rows = ta.shape[0] // LAYERS
    for level in range(LAYERS):
        span = slice(level * rows, (level + 1) * rows)
        block = jnp.concatenate([ta[...].astype(F32)[span], qa[...].astype(F32)[span]], axis=0)
        acts[level, z, y] = block.astype(BF16)

    def sort_segments():
        wide = jnp.broadcast_to(seg[...].astype(F32), (8, TOK)).astype(BF16)
        old = lax.broadcasted_iota(jnp.int32, (TOK, TOK), 0)
        new = lax.broadcasted_iota(jnp.int32, (TOK, TOK), 1)
        half = TOK // CORE
        source = (new % half) // rows * (rows * CORE) + new // half * rows + new % rows
        pick = (old == source).astype(F32).astype(BF16)
        return jnp.dot(wide, pick, preferred_element_type=F32)[:1]

    pl.semaphore_wait(barrier, len(peers))

    nearest = z - 1 + 2 * (1 - (z + Z - 1) // Z)
    farthest = 3 * (1 - z // 2)
    order = [z, nearest, 6 - z - nearest - farthest, farthest]

    inner = z * (Z - 1 - z) > 0

    def to_z(level, at, zz, slot):
        block = acts.at[level, at, y]
        return pltpu.make_async_remote_copy(
            src_ref=block,
            dst_ref=block,
            send_sem=pass_sem.at[level, slot],
            recv_sem=z_sem.at[level, at],
            device_id=device(hi, x, zz, y, core),
            device_id_type=MESH,
        )

    def along_z(level):
        @pl.when(z > 0)
        def _():
            to_z(level, z, z - 1, 0).start()

        @pl.when(z < Z - 1)
        def _():
            to_z(level, z, z + 1, 1).start()

    def sent_z(level):
        @pl.when(z > 0)
        def _():
            to_z(level, z, z - 1, 0).wait_send()

        @pl.when(z < Z - 1)
        def _():
            to_z(level, z, z + 1, 1).wait_send()

        @pl.when(inner)
        def _():
            for k in range(1, Z):
                to_z(level, order[k], z - 1, 1 + k).wait_send()

    def along_y(level, k):
        block = acts.at[level, order[k], y]
        links.start(block, block, y_peer[1], y_sem.at[level, 0, order[k]])
        links.start(block, block, y_peer[3], y_sem.at[level, 1, order[k]])

    def spread(level, k):
        links.landed(acts.at[level, order[k], y], z_sem.at[level, order[k]], mate)

        @pl.when(inner)
        def _():
            onward = z + 1 - 2 * ((order[k] + Z - z) // Z)
            to_z(level, order[k], onward, 1 + k).start()

        along_y(level, k)

    def pass_on(level, k):
        left = acts.at[level, order[k], y_of[3]]
        right = acts.at[level, order[k], y_of[1]]
        links.landed(left, y_sem.at[level, 0, order[k]], mate)
        if k % 2 == 0:
            links.start(left, left, y_peer[1], on_sem.at[level, order[k]])
        links.landed(right, y_sem.at[level, 1, order[k]], mate)
        if k % 2 == 1:
            links.start(right, right, y_peer[3], on_sem.at[level, order[k]])

    def gathered(level):
        for k in range(Z):
            links.landed(acts.at[level, order[k], y_of[2]], on_sem.at[level, order[k]], mate)

    y_rows = TOK // Y
    z_rows = y_rows // Z

    def rotate_out(level):
        own = grads[level].reshape(TOK, CORE * ROWS_OUT)
        product = jnp.dot(own, bo[level], preferred_element_type=F32)
        product = product.reshape(TOK // (CORE * rows), CORE, rows, COLS_OUT)
        product = jnp.swapaxes(product, 0, 1).reshape(TOK, COLS_OUT)
        part_out[level] = product
        own_out[level] = product.astype(BF16).reshape(Y, y_rows, COLS_OUT)
        return [
            links.start(own_out.at[level, y_of[d]], ry.at[level, d - 1], y_peer[d])
            for d in (2, 1, 3)
        ]

    def add_y(level, starts):
        received(starts)
        total = part_out[level, pl.ds(pl.multiple_of(y * y_rows, y_rows), y_rows), :]
        for d in range(Y - 1):
            total = total + ry[level, d].astype(F32)
        rz_s[level] = total.reshape(Z, z_rows, COLS_OUT)
        return [
            links.start(rz_s.at[level, z_of[d]], rz.at[level, d - 1], z_peer[d])
            for d in (2, 1, 3)
        ]

    def add_z(level, starts):
        received(starts)
        total = rz_s[level, z]
        for d in range(Z - 1):
            total = total + rz[level, d]
        out_t[core, level, y, z] = total.astype(BF16)
        block = out_t.at[core, level, y, z]
        return [links.start(block, block, z_peer[d]) for d in (2, 1, 3)]

    def gather_y(level, starts):
        received(starts)
        for d in (2, 1, 3):
            block = out_t.at[core, level, y]
            links.start(
                block, block, y_peer[d], out_sem.at[level, d], lambda: out_t.at[core, level, 0]
            )

    def hand_over(level):
        for d in (2, 1, 3):
            links.landed(out_t.at[core, level, y_of[d]], out_sem.at[level, d], mate)
        block = out_t.at[core, level]
        links.start(block, block, mate, hand_sem.at[level], lambda: out_t.at[core, level])

    def handed(level):
        links.landed(out_t.at[other, level], hand_sem.at[level], mate)

    def prepare(level):
        loads[8 + level].wait()
        eig[level] = factor / (eig[level] + DAMPING)

    def rotate(level):
        @pl.loop(0, TOK // 32)
        def _(p):
            pair = acts[level, p // (Y // 2), pl.ds(p % (Y // 2) * 2, 2)].astype(F32)
            for at in range(2):
                piece = pair[:, at * rows:(at + 1) * rows].reshape(2 * rows, ROWS_IN)
                here = pl.ds(pl.multiple_of(at * (TOK // 2) + p * 2 * rows, 2 * rows), 2 * rows)
                tokens[here, :] = piece.astype(BF16)

        @pl.loop(0, CORE)
        def _(c):
            product = lax.dot_general(bi[level, c], tokens[...], NT, preferred_element_type=F32)
            part_in[level, c] = product.reshape(X, PIECE, TOK)
            rx_s[level, c] = product.astype(BF16).reshape(X, PIECE, TOK)
            for k in range(CORE):
                @pl.when(c == k)
                def _(k=k):
                    for d in (2, 1, 3):
                        links.start(
                            rx_s.at[level, k, x_of[d]], rx.at[level, k, d - 1], x_peer[d],
                            x_sem.at[level, k, d - 1], lambda: zs.at[level, k],
                        )

    def add_x(level, c):
        for d in range(X - 1):
            links.landed(rx.at[level, c, d], x_sem.at[level, c, d], mate)
        total = part_in[level, c, x]
        for d in range(X - 1):
            total = total + rx[level, c, d].astype(F32)
        part_in[level, c, x] = total
        zs[level, c] = total.astype(BF16)
        links.start(
            zs.at[level, c], zr.at[level, c], hi_peer, hi_sem.at[level, c],
            lambda: zs.at[level, c],
        )

    def add_hi(level, c):
        links.landed(zr.at[level, c], hi_sem.at[level, c], mate)
        total = part_in[level, c, x] + zr[level, c].astype(F32)
        give[level, c] = total.astype(BF16)

        @pl.when(core == c)
        def _():
            rin[level, core, x] = give[level, c]

        @pl.when(core != c)
        def _():
            pltpu.make_async_remote_copy(
                src_ref=give.at[level, c],
                dst_ref=rin.at[level, core, x],
                send_sem=give_sem.at[level],
                recv_sem=piece_sem.at[level, 0, core],
                device_id=mate,
                device_id_type=MESH,
            ).start()

        for d in (1, 2, 3):
            links.start(
                give.at[level, c], rin.at[level, core, x], device(hi, x_of[d], z, y, c),
                piece_sem.at[level, d, core], lambda: give.at[level, c],
            )

    along_z(0)
    along_y(0, 0)
    for load in loads[2:6]:
        load.wait()
    theirs = grads.at[:, hi, x, :, bo_span]
    grads_in = [
        links.start(grads_s.at[core], theirs, hi_peer),
        links.start(grads_s.at[other], theirs, hi_other),
        links.start(grads_s.at[other], theirs, mate),
    ]
    along_y(1, 0)
    bo_swap = links.start(bo.at[:, bo_span, :], bo.at[:, bo_span, :], mate)
    for c in range(CORE):
        @pl.when(core == c)
        def _(c=c):
            grads[:, hi, x, :, pl.ds(c * ROWS_OUT, ROWS_OUT)] = grads_s[c]

    segment = sort_segments()

    spread(0, 1)
    spread(0, 2)
    along_z(1)
    pass_on(0, 0)
    received(grads_in)
    block = grads.at[:, :, x]
    grads_x = [links.start(block, block, x_peer[d]) for d in (2, 1, 3)]
    pass_on(0, 1)
    spread(0, 3)
    bi_0 = links.start(bi_hbm.at[0], bi.at[0, core], mate)
    prepare(0)
    received([bo_swap])
    received(grads_x)
    out = [rotate_out(0), None]
    spread(1, 1)
    spread(1, 2)
    pass_on(0, 2)
    pass_on(1, 0)
    pass_on(0, 3)
    spread(1, 3)
    bi_1 = links.start(bi_hbm.at[1], bi.at[1, core], mate)
    out[0] = add_y(0, out[0])
    pass_on(1, 1)
    gathered(0)
    loads[6].wait()
    received([bi_0])
    rotate(0)

    out[0] = add_z(0, out[0])
    out[1] = rotate_out(1)
    pass_on(1, 2)
    add_x(0, 0)
    pass_on(1, 3)
    gather_y(0, out[0])
    add_x(0, 1)
    prepare(1)
    out[1] = add_y(1, out[1])
    gathered(1)
    loads[7].wait()
    received([bi_1])
    rotate(1)
    hand_over(0)
    add_hi(0, 0)
    out[1] = add_z(1, out[1])
    add_hi(0, 1)
    add_x(1, 0)
    add_x(1, 1)
    handed(0)

    def given(level):
        pltpu.make_async_remote_copy(
            src_ref=give.at[level, 0],
            dst_ref=give.at[level, 0],
            send_sem=give_sem.at[level],
            recv_sem=recv_sem.at[0],
            device_id=mate,
            device_id_type=MESH,
        ).wait_send()

    scores[...] = jnp.zeros_like(scores)

    @pl.loop(0, LAYERS * X)
    def _(step):
        level, d = step // X, step % X
        at = lax.rem(x + X - d, X)

        @pl.when(step == 1)
        def _():
            gather_y(1, out[1])

        @pl.when(step == 3)
        def _():
            hand_over(1)

        @pl.when(step == 4)
        def _():
            links.finish()
            for side in range(LAYERS):
                sent_z(side)
            given(0)
            add_hi(1, 0)
            add_hi(1, 1)
            handed(1)

        links.landed(rin.at[level, other, at], piece_sem.at[level, d, other], mate)

        @pl.when(d != 0)
        def _():
            links.landed(rin.at[level, core, at], piece_sem.at[level, d, core], mate)

        both = [rin[level, c, at] for c in range(CORE)]
        train_in = jnp.concatenate([b[:, :TOK // 2] for b in both], axis=1).astype(F32)
        query_in = jnp.concatenate([b[:, TOK // 2:] for b in both], axis=1)
        scale = eig[level, pl.ds(pl.multiple_of(at * PIECE, PIECE), PIECE), :]
        query_out = out_t[1, level].reshape(TOK, COLS_OUT)
        train_out = out_t[0, level].reshape(TOK, COLS_OUT)

        @pl.loop(0, QUERIES // GROUP)
        def _(g):
            masked = []
            for k in range(GROUP):
                member = (segment == (g * GROUP + k).astype(F32)).astype(F32).astype(BF16)
                masked.append(query_in * member)
            masked = jnp.concatenate(masked, axis=0)
            cross = jnp.dot(masked, query_out, preferred_element_type=F32)
            cross = cross.reshape(GROUP, PIECE, COLS_OUT) * scale[None]
            precond = cross.astype(BF16).reshape(GROUP * PIECE, COLS_OUT)
            right = lax.dot_general(precond, train_out, NT, preferred_element_type=F32)
            right = right.reshape(GROUP, PIECE, TOK) * train_in[None]
            right = jnp.sum(right.reshape(GROUP, PIECE // 8, 8, TOK), axis=1)
            here = pl.ds(g * GROUP, GROUP)
            scores[here] = scores[here] + right

    summed = jnp.sum(scores[...], axis=1)
    half = TOK // 2
    es1[0] = summed[:, :half]
    es1[1] = summed[:, half:]
    ends = []
    for d in (2, 1, 3):
        ends.append(links.start(es1.at[other], er1.at[X - 1 + d], x_other[d]))
        ends.append(links.start(es1.at[core], er1.at[d], x_peer[d]))
    ends.append(links.start(es1.at[other], er1.at[0], mate))
    links.finish()
    given(1)
    received(ends)
    total = es1[core]
    for d in range(X * CORE - 1):
        total = total + er1[d]
    es2[...] = total
    ends = []
    for d in (4, 3, 5, 2, 6, 1, 7):
        ends.append(links.start(es2, er2.at[d - 1], ring_peer[d]))
    received(ends)
    for d in range(HI * Z - 1):
        total = total + er2[d]
    es3[...] = total
    ends = [links.start(es3, er3.at[d - 1], y_peer[d]) for d in (2, 1, 3)]
    received(ends)
    for d in range(Y - 1):
        total = total + er3[d]
    own = half // (Z * Y)
    total = pltpu.roll(total, lax.rem(half - (z * Y + y) * own, half), axis=1)
    out_ref[...] = total.T[:own]
    links.finish()


def fused(ta, qa, tg, qg, basis_in, basis_out, eigen, segment):
    y_rows = TOK // Y
    z_rows = y_rows // Z
    half = TOK // 2
    scratch = [
        pltpu.VMEM((16, ROWS_IN), BF16),
        pltpu.VMEM((16, ROWS_IN), BF16),
        pltpu.VMEM((1, TOK), jnp.int32),
        pltpu.VMEM((LAYERS, CORE, COLS_IN, ROWS_IN), BF16),
        pltpu.VMEM((LAYERS, COLS_IN, COLS_OUT), F32),
        pltpu.VMEM((TOK, ROWS_IN), BF16),
        pltpu.VMEM((LAYERS, Z, Y, 16, ROWS_IN), BF16),
        pltpu.VMEM((2, LAYERS, 32, ROWS_OUT), BF16),
        pltpu.VMEM((LAYERS, HI, X, 32, CORE * ROWS_OUT), BF16),
        pltpu.VMEM((LAYERS, CORE * ROWS_OUT, COLS_OUT), BF16),
        pltpu.VMEM((LAYERS, TOK, COLS_OUT), F32),
        pltpu.VMEM((LAYERS, Y, y_rows, COLS_OUT), BF16),
        pltpu.VMEM((LAYERS, Y - 1, y_rows, COLS_OUT), BF16),
        pltpu.VMEM((LAYERS, Z, z_rows, COLS_OUT), F32),
        pltpu.VMEM((LAYERS, Z - 1, z_rows, COLS_OUT), F32),
        pltpu.VMEM((2, LAYERS, Y, Z, z_rows, COLS_OUT), BF16),
        pltpu.VMEM((LAYERS, 2, X, PIECE, TOK), F32),
        pltpu.VMEM((LAYERS, 2, X, PIECE, TOK), BF16),
        pltpu.VMEM((LAYERS, 2, X - 1, PIECE, TOK), BF16),
        pltpu.VMEM((LAYERS, 2, PIECE, TOK), BF16),
        pltpu.VMEM((LAYERS, 2, PIECE, TOK), BF16),
        pltpu.VMEM((LAYERS, CORE, PIECE, TOK), BF16),
        pltpu.VMEM((LAYERS, 2, X, PIECE, TOK), BF16),
        pltpu.VMEM((QUERIES, 8, TOK), F32),
        pltpu.VMEM((2, QUERIES, half), F32),
        pltpu.VMEM((HI * Z - 1, QUERIES, half), F32),
        pltpu.VMEM((QUERIES, half), F32),
        pltpu.VMEM((Y * CORE - 1, QUERIES, half), F32),
        pltpu.VMEM((QUERIES, half), F32),
        pltpu.VMEM((X - 1, QUERIES, half), F32),
        pltpu.SemaphoreType.DMA((6 + 2 * LAYERS,)),
        pltpu.SemaphoreType.DMA((COPIES,)),
        pltpu.SemaphoreType.DMA((COPIES,)),
        pltpu.SemaphoreType.DMA((LAYERS, Z)),
        pltpu.SemaphoreType.DMA((LAYERS, 2, Z)),
        pltpu.SemaphoreType.DMA((LAYERS, Z)),
        pltpu.SemaphoreType.DMA((LAYERS, X, 2)),
        pltpu.SemaphoreType.DMA((LAYERS, CORE, X - 1)),
        pltpu.SemaphoreType.DMA((LAYERS, CORE)),
        pltpu.SemaphoreType.DMA((LAYERS,)),
        pltpu.SemaphoreType.DMA((LAYERS,)),
        pltpu.SemaphoreType.DMA((LAYERS, Y)),
        pltpu.SemaphoreType.DMA((LAYERS, 1 + Z)),
    ]
    return pl.pallas_call(
        kernel,
        out_shape=jax.ShapeDtypeStruct((half // (Z * Y), QUERIES), F32),
        in_specs=[pl.BlockSpec(memory_space=pl.ANY)] * 8,
        out_specs=pl.BlockSpec(memory_space=pltpu.VMEM),
        scratch_shapes=scratch,
        compiler_params=pltpu.CompilerParams(
            collective_id=0, has_side_effects=True, vmem_limit_bytes=VMEM_LIMIT
        ),
        cost_estimate=pl.CostEstimate(flops=9_400_000_000, bytes_accessed=6_000_000, transcendentals=0),
    )(ta, qa, tg, qg, basis_out, segment, basis_in, eigen)


def on_device(
    train_acts, query_acts, train_grads, query_grads, basis_in, basis_out, eigen, query_segment
):
    own = fused(
        train_acts.reshape(-1, ROWS_IN),
        query_acts.reshape(-1, ROWS_IN),
        train_grads,
        query_grads,
        jnp.swapaxes(basis_in, 1, 2),
        basis_out,
        jnp.swapaxes(eigen, 1, 2),
        query_segment.reshape(1, TOK),
    )
    return jnp.swapaxes(own, 0, 1)


def solution(mesh):
    placed = (
        P(None, "seq", "layer"),
        P(None, "seq", "layer"),
        P(None, "layer", "seq"),
        P(None, "layer", "seq"),
        P(None, "layer", "seq"),
        P(None, "seq", "layer"),
        P(None, "layer", "seq"),
        P(),
    )
    return jax.shard_map(
        on_device, mesh=mesh, in_specs=placed, out_specs=P(None, "seq"), check_vma=False
    )
```
